32 devices in a mesh: dp: 4 (over y, x), seq: 8 (over z, core).
Axes of the slice: x: 2, y: 2, z: 4, core: 2. Of those that a mesh axis runs over, the one named last changes fastest.
Arguments:
- tokens: bfloat16 [4, 2048, 4096], P('dp', 'seq'), may hold values from -6 to 6
- w_qkv: bfloat16 [4096, 768], P('dp'), may hold values from -0.09375 to 0.09375
- norm_gain: float32 [256], replicated, may hold values from 0.1 to 1.9
- w_out: bfloat16 [256, 4096], P(None, 'dp'), may hold values from -0.375 to 0.375
Outputs:
- mixed: bfloat16 [4, 2048, 4096], P('dp', 'seq')
The draws below stay inside these ranges and needn't reach their ends.
All inputs are finite; a program needn't handle non-finite values.
Results may differ from the reference program's by a relative error of at most 0.015.
Values may be sent and summed in bfloat16 or wider, within the bound.
No kernel may reach another device: no remote copies, remote signals or barrier semaphores. Data moves between devices by JAX's collectives and lax.ppermute only.
A program may use at most 64 MiB of HBM per device.

```python
import jax
import jax.numpy as jnp
from jax import lax

D = 4096
HEAD = 128
HEADS = 2
TOK_DEV = 256
HD = 256
LEN = 2048
BATCH = 4
N_SEQ = 8


def steps_of(stream_key, shape, shards, low, largest):
    loudness = 1.0
    for axis_at, shards_of in shards:
        draws = jax.random.uniform(jax.random.fold_in(jax.random.fold_in(stream_key, 6), axis_at), (shards_of,), jnp.float32, low / len(shards), largest / len(shards))
        loudness = loudness * jnp.repeat(jnp.exp(draws), shape[axis_at] // shards_of).reshape((-1,) + (1,) * (len(shape) - 1 - axis_at))
    return loudness


def bell_draw(key, extent, scale, bound, split=(), kind=jnp.bfloat16):
    gain = steps_of(key, extent, split, -0.22, 0.18) if split else 1.0
    result = jax.random.normal(key, extent, jnp.float32) * scale * gain
    return jnp.minimum(jnp.maximum(result, -bound), bound).astype(kind)


def setup_inputs(seed: int = 0) -> dict:
    key_of = jax.random.split(jax.random.key(seed), 5)
    return {
        "tokens": bell_draw(key_of[0], (BATCH, LEN, D), 1.0, 6.0, ((0, 4), (1, 8))),
        "w_qkv": bell_draw(key_of[1], (D, 3 * HD), D ** -0.5, 0.09375, ((0, 4),)),
        "norm_gain": jnp.clip(1.0 + 0.18 * jax.random.normal(key_of[2], (HD,), jnp.float32), 0.1, 1.9),
        "w_out": bell_draw(key_of[3], (HD, D), HD ** -0.5, 0.375, ((1, 4),)),
    }


def one_sequence(x, w_qkv, norm_gain, w_out):
    proj = jnp.dot(x, w_qkv, preferred_element_type=jnp.float32)
    query = jax.nn.silu(proj[:, :HD]).astype(jnp.bfloat16)
    keys = jax.nn.silu(proj[:, HD:2 * HD]).astype(jnp.bfloat16)
    values = proj[:, 2 * HD:].astype(jnp.bfloat16)
    shape4 = (N_SEQ, TOK_DEV, HEADS, HEAD)
    qf = query.reshape(shape4).astype(jnp.float32)
    kf = keys.reshape(shape4).astype(jnp.float32)
    vf = values.reshape(shape4).astype(jnp.float32)
    state = jnp.einsum('cthA,cthB->chAB', kf, vf)
    running = jnp.cumsum(state, axis=0)
    prefix = jnp.concatenate([jnp.zeros_like(state[:1]), running[:-1]], axis=0)
    prefix = prefix.astype(jnp.bfloat16).astype(jnp.float32)
    inter = jnp.einsum('cthA,chAB->cthB', qf, prefix)
    scores = jnp.einsum('cthA,cshA->chts', qf, kf)
    rows = jnp.arange(TOK_DEV)
    causal = rows[:, None] >= rows[None, :]
    scores = jnp.where(causal[None, None], scores, 0.0).astype(jnp.bfloat16).astype(jnp.float32)
    intra = jnp.einsum('chts,cshB->cthB', scores, vf)
    attended = inter + intra
    meansq = lax.optimization_barrier(jnp.mean(attended * attended, axis=-1, keepdims=True))
    normed = attended * lax.rsqrt(meansq + 1e-06) * norm_gain.reshape(HEADS, HEAD)
    normed = normed.astype(jnp.bfloat16).reshape(LEN, HD)
    return jnp.dot(normed, w_out, preferred_element_type=jnp.float32).astype(jnp.bfloat16)

def reference(tokens, w_qkv, norm_gain, w_out):
    return lax.map(lambda x: one_sequence(x, w_qkv, norm_gain, w_out), tokens)
```

```python
import functools

import jax
import jax.numpy as jnp
from jax import lax
from jax.experimental import pallas as pl
from jax.experimental.pallas import tpu as pltpu
from jax.sharding import PartitionSpec as P

HEAD = 128
CORES = 2
VMEM_LIMIT = 40 * 1024 * 1024


def in_vmem(count):
    return [pl.BlockSpec(memory_space=pltpu.VMEM)] * count


def flip(x, axis, size, mask):
    return lax.ppermute(x, axis, [(i, i ^ mask) for i in range(size)])


def spread(own, n):
    bits = [1 << b for b in range(n.bit_length() - 1)]
    half = own.shape[0] // 2
    held = [{0: own[:half]}, {0: own[half:]}]
    orders = [bits, bits[::-1]]
    for step in range(len(bits)):
        for which in range(2):
            bit = orders[which][step]
            got = {m ^ bit: flip(piece, "dp", n, bit) for m, piece in held[which].items()}
            held[which].update(got)
    return {m: [held[0][m], held[1][m]] for m in range(n)}


def dot(a, b, contract=((1,), (0,))):
    return lax.dot_general(a, b, (contract, ((), ())), preferred_element_type=jnp.float32)


def project(count, first, places, tok_a, tok_b, *refs):
    pieces, rest = refs[:count], refs[count:]
    out = rest[-1]
    rows = tok_a.shape[0]
    total = None if first else rest[0][...]
    for i, piece in enumerate(pieces):
        width = piece.shape[0]
        cols = pl.ds(pl.multiple_of(places[i], 128), width)
        tok = jnp.concatenate([tok_a[:, cols], tok_b[:, cols]], axis=0)
        term = dot(tok, piece[...])
        total = term if total is None else total + term
    out[...] = total


def attend(proj, query_out, state_out, chip_out, intra_out):
    rows = intra_out.shape[1]
    row = lax.broadcasted_iota(jnp.int32, (rows, rows), 0)
    col = lax.broadcasted_iota(jnp.int32, (rows, rows), 1)
    chip = None
    for b in range(CORES):
        part = proj[b * rows : (b + 1) * rows, :]
        act = part[:, : 2 * HEAD]
        act = (act / (1.0 + jnp.exp(-act))).astype(jnp.bfloat16)
        query, keys = act[:, :HEAD], act[:, HEAD:]
        values = part[:, 2 * HEAD :].astype(jnp.bfloat16)
        state = dot(keys, values, ((0,), (0,)))
        chip = state if chip is None else chip + state
        query_out[b] = query
        state_out[b] = state
        scores = dot(query, keys, ((1,), (1,)))
        scores = jnp.where(row >= col, scores, 0.0).astype(jnp.bfloat16)
        intra_out[b] = dot(scores, values)
    chip_out[...] = chip.astype(jnp.bfloat16)


def normalise(count, core, query, state, intra, gain, *refs):
    earlier, (own_out, other_out) = refs[:count], refs[count:]
    base = jnp.zeros((HEAD, HEAD), jnp.float32)
    for ref in earlier:
        base = base + ref[...].astype(jnp.float32)
    odd = core[0] == 1
    own_prefix = jnp.where(odd, base + state[1], base)
    other_prefix = jnp.where(odd, base, base + state[0])
    for b, (prefix, out) in enumerate(((own_prefix, own_out), (other_prefix, other_out))):
        attended = dot(query[b], prefix.astype(jnp.bfloat16)) + intra[b]
        meansq = jnp.mean(attended * attended, axis=-1, keepdims=True)
        out[...] = (attended * lax.rsqrt(meansq + 1e-06) * gain[...]).astype(jnp.bfloat16)


def mix(n, parts, place, own, other, *refs):
    mine, theirs, out = refs[: n * parts], refs[n * parts : 2 * n * parts], refs[-1]
    step = pl.program_id(0)
    normed = jnp.concatenate([own[...], other[...]], axis=1)
    for m in range(n):

        @pl.when(step == m)
        def _():
            for p in range(parts):
                i = m * parts + p
                width = mine[i].shape[1]
                weights = jnp.concatenate([mine[i][...], theirs[i][...]], axis=0)
                out[:, p * width : (p + 1) * width] = dot(normed, weights).astype(jnp.bfloat16)


def shards(n, blocks, tokens, w_qkv, norm_gain, w_out):
    tok_own = tokens[0]
    rows, depth = tok_own.shape
    shard = w_qkv.shape[0]
    heads = norm_gain.shape[0] // HEAD
    at = lax.axis_index("dp")
    core = lax.rem(lax.axis_index("seq"), CORES)
    params = pltpu.CompilerParams(vmem_limit_bytes=VMEM_LIMIT)

    tok_other = flip(tok_own, "seq", blocks, 1)
    w_head = lax.dynamic_index_in_dim(
        w_qkv.reshape(shard, 3, heads, HEAD), core, axis=2, keepdims=False
    ).reshape(shard, 3 * HEAD)
    out_head = lax.dynamic_slice_in_dim(w_out, core * HEAD, HEAD, axis=0)

    pieces = spread(w_head, n)
    half = shard // 2

    def run(offsets, total):
        parts = [pieces[m][h] for m in offsets for h in range(2)]
        places = jnp.stack([(at ^ m) * shard + h * half for m in offsets for h in range(2)])
        count = len(parts)
        extra = [] if total is None else [total]
        flops = 2 * CORES * rows * half * count * 3 * HEAD
        return pl.pallas_call(
            functools.partial(project, count, total is None),
            out_shape=jax.ShapeDtypeStruct((CORES * rows, 3 * HEAD), jnp.float32),
            in_specs=[pl.BlockSpec(memory_space=pltpu.SMEM)] + in_vmem(2 + count + len(extra)),
            out_specs=pl.BlockSpec(memory_space=pltpu.VMEM),
            compiler_params=params,
            cost_estimate=pl.CostEstimate(
                flops=flops, bytes_accessed=8 * 1024 * 1024, transcendentals=0
            ),
        )(places.astype(jnp.int32), tok_own, tok_other, *parts, *extra)

    total = run([0], None)
    total = run(list(range(1, n)), total)

    query, state, chip, intra = pl.pallas_call(
        attend,
        out_shape=(
            jax.ShapeDtypeStruct((CORES, rows, HEAD), jnp.bfloat16),
            jax.ShapeDtypeStruct((CORES, HEAD, HEAD), jnp.float32),
            jax.ShapeDtypeStruct((HEAD, HEAD), jnp.bfloat16),
            jax.ShapeDtypeStruct((CORES, rows, HEAD), jnp.float32),
        ),
        in_specs=in_vmem(1),
        out_specs=tuple(in_vmem(4)),
        compiler_params=params,
    )(total)

    earlier = [
        lax.ppermute(chip, "seq", [(i, i + CORES * k) for i in range(blocks - CORES * k)])
        for k in range(1, blocks // CORES)
    ]
    gain = lax.dynamic_slice_in_dim(norm_gain, core * HEAD, HEAD).reshape(1, HEAD)
    normed_own, normed_other = pl.pallas_call(
        functools.partial(normalise, len(earlier)),
        out_shape=(jax.ShapeDtypeStruct((rows, HEAD), jnp.bfloat16),) * 2,
        in_specs=[pl.BlockSpec(memory_space=pltpu.SMEM)] + in_vmem(4 + len(earlier)),
        out_specs=tuple(in_vmem(2)),
        compiler_params=params,
    )(core.reshape(1).astype(jnp.int32), query, state, intra, gain, *earlier)
    normed_got = flip(normed_other, "seq", blocks, 1)

    width = w_out.shape[1]
    out_pieces = spread_columns(out_head, n)
    out_other = [[flip(p, "seq", blocks, 1) for p in out_pieces[m]] for m in range(n)]
    mine = [p for m in range(n) for p in out_pieces[m]]
    theirs = [p for m in range(n) for p in out_other[m]]
    parts = len(mine) // n
    mixed = pl.pallas_call(
        functools.partial(mix, n, parts),
        out_shape=jax.ShapeDtypeStruct((rows, n * width), jnp.bfloat16),
        grid_spec=pltpu.PrefetchScalarGridSpec(
            num_scalar_prefetch=1,
            grid=(n,),
            in_specs=in_vmem(2 + 2 * len(mine)),
            out_specs=pl.BlockSpec((rows, width), lambda i, place: (0, place[0] ^ i)),
        ),
        compiler_params=params,
    )(at.reshape(1).astype(jnp.int32), normed_own, normed_got, *mine, *theirs)
    return mixed[None]


def spread_columns(own, n):
    bits = [1 << b for b in range(n.bit_length() - 1)]
    half = own.shape[1] // 2
    held = [{0: own[:, :half]}, {0: own[:, half:]}]
    orders = [bits, bits[::-1]]
    for step in range(len(bits)):
        for which in range(2):
            bit = orders[which][step]
            got = {m ^ bit: flip(piece, "dp", n, bit) for m, piece in held[which].items()}
            held[which].update(got)
    return {m: [held[0][m], held[1][m]] for m in range(n)}


def solution(mesh):
    n, blocks = mesh.shape["dp"], mesh.shape["seq"]
    return jax.shard_map(
        functools.partial(shards, n, blocks),
        mesh=mesh,
        in_specs=(P("dp", "seq", None), P("dp", None), P(), P(None, "dp")),
        out_specs=P("dp", "seq", None),
        check_vma=False,
    )
```

```python
import functools

import jax
import jax.numpy as jnp
from jax import lax
from jax.experimental import pallas as pl
from jax.experimental.pallas import tpu as pltpu
from jax.sharding import PartitionSpec as P

HEAD = 128
CORES = 2
VMEM_LIMIT = 24 * 1024 * 1024
VMEM = pl.BlockSpec(memory_space=pltpu.VMEM)
HBM = pl.BlockSpec(memory_space=pltpu.HBM)


def flip(x, axis, size, mask):
    return lax.ppermute(x, axis, [(i, i ^ mask) for i in range(size)])


def dot(a, b, contract=((1,), (0,))):
    return lax.dot_general(a, b, (contract, ((), ())), preferred_element_type=jnp.float32)


def position():
    at = lax.axis_index("dp")
    seq = lax.axis_index("seq")
    return at, lax.rem(seq, CORES), lax.rem(seq // CORES, 2)


def cut_qkv(layout, w_qkv, *outs):
    _, core, parity = position()
    quarter = w_qkv.shape[0] // 4
    feat = w_qkv.shape[1] // 3
    for out, quarters in zip(outs, layout(parity)):
        for i, q in enumerate(quarters):
            rows = pl.ds(pl.multiple_of(q * quarter, quarter), quarter)
            for j in range(3):
                cols = pl.ds(pl.multiple_of(j * feat + core * HEAD, HEAD), HEAD)
                out[i * quarter : (i + 1) * quarter, j * HEAD : (j + 1) * HEAD] = w_qkv[rows, cols]


def cut_out(w_out, mine, theirs):
    _, core, _ = position()
    for out, head in ((mine, core), (theirs, 1 - core)):
        out[...] = w_out[pl.ds(pl.multiple_of(head * HEAD, HEAD), HEAD), :]


def quarters_x(parity):
    return [[parity], [1 - parity, 2, 3]]


def quarters_y(parity):
    return [[2 + parity], [3 - parity, 0, 1]]


def product(tok_a, tok_b, pieces, places):
    width = pieces[0].shape[0] // len(places[0])
    cols = [pl.ds(place, width) for piece in places for place in piece]
    tok = jnp.concatenate(
        [jnp.concatenate([ref[:, c] for c in cols], axis=1) for ref in (tok_a, tok_b)], axis=0
    )
    weights = jnp.concatenate([piece[...] for piece in pieces], axis=0)
    return dot(tok, weights)


def places_of(shard, offset, groups):
    at, _, parity = position()
    start = (at ^ offset) * shard
    quarter = shard // 4
    return [[pl.multiple_of(start + q * quarter, quarter) for q in group] for group in groups(parity)]


def places_own(shard):
    return places_of(shard, 0, quarters_x)


def places_near(shard, which):
    return [places_of(shard, 1, quarters_x)[which], places_of(shard, 2, quarters_y)[which]]


def places_far(shard):
    return places_of(shard, 3, lambda parity: [[parity], [2 + parity], [1 - parity], [3 - parity]])


def project(count, places, tok_a, tok_b, *refs):
    pieces, before, total = refs[:count], refs[count:-1], refs[-1]
    term = product(tok_a, tok_b, pieces, places())
    total[...] = before[0][...] + term if before else term


def project_attend(count, places, tok_a, tok_b, *refs):
    pieces, before = refs[:count], refs[count:-4]
    query_out, state_out, chip_out, intra_out = refs[-4:]
    proj = product(tok_a, tok_b, pieces, places())
    if before:
        proj = before[0][...] + proj
    rows = intra_out.shape[1]
    row = lax.broadcasted_iota(jnp.int32, (rows, rows), 0)
    col = lax.broadcasted_iota(jnp.int32, (rows, rows), 1)
    chip = None
    for b in range(CORES):
        part = proj[b * rows : (b + 1) * rows, :]
        act = part[:, : 2 * HEAD]
        act = (act / (1.0 + jnp.exp(-act))).astype(jnp.bfloat16)
        query, keys = act[:, :HEAD], act[:, HEAD:]
        values = part[:, 2 * HEAD :].astype(jnp.bfloat16)
        state = dot(keys, values, ((0,), (0,)))
        chip = state if chip is None else chip + state
        query_out[b] = query
        state_out[b] = state
        scores = dot(query, keys, ((1,), (1,)))
        scores = jnp.where(row >= col, scores, 0.0).astype(jnp.bfloat16)
        intra_out[b] = dot(scores, values)
    chip_out[...] = chip.astype(jnp.bfloat16)


def normalise(count, query, state, intra, gain, *refs):
    earlier, (own_out, other_out) = refs[:count], refs[count:]
    _, core, _ = position()
    base = jnp.zeros((HEAD, HEAD), jnp.float32)
    for ref in earlier:
        base = base + ref[...].astype(jnp.float32)
    odd = core == 1
    own_prefix = jnp.where(odd, base + state[1], base)
    other_prefix = jnp.where(odd, base, base + state[0])
    scale = gain[pl.ds(core, 1), :]
    for b, (prefix, out) in enumerate(((own_prefix, own_out), (other_prefix, other_out))):
        attended = dot(query[b], prefix.astype(jnp.bfloat16)) + intra[b]
        meansq = jnp.mean(attended * attended, axis=-1, keepdims=True)
        out[...] = (attended * lax.rsqrt(meansq + 1e-06) * scale).astype(jnp.bfloat16)


def mix(count, places, own, other, *refs):
    mine, theirs, (out, stage, sem) = refs[:count], refs[count : 2 * count], refs[2 * count :]
    normed = jnp.concatenate([own[...], other[...]], axis=1)
    copies = []
    slot = 0
    for my_rows, their_rows, place in zip(mine, theirs, places()):
        width = my_rows.shape[1]
        step = min(width, 512)
        for at_col in range(0, width, step):
            part = slice(at_col, at_col + step)
            weights = jnp.concatenate([my_rows[:, part], their_rows[:, part]], axis=0)
            here = stage.at[:, slot : slot + step]
            here[...] = dot(normed, weights).astype(jnp.bfloat16)
            cols = pl.ds(pl.multiple_of(place + at_col, 128), step)
            copies.append(pltpu.make_async_copy(here, out.at[:, cols], sem.at[len(copies)]))
            copies[-1].start()
            slot += step
    for copy in copies:
        copy.wait()


def places_out(width):
    at = lax.axis_index("dp")
    offsets = [(0, 0), (1, 0), (2, 0), (3, 0), (3, width // 2)]
    return [(at ^ offset) * width + start for offset, start in offsets]


def shards(n, blocks, tokens, w_qkv, norm_gain, w_out):
    tok_own = tokens[0]
    rows, depth = tok_own.shape
    shard = w_qkv.shape[0]
    heads = norm_gain.shape[0] // HEAD
    params = pltpu.CompilerParams(vmem_limit_bytes=VMEM_LIMIT)
    bf16, f32 = jnp.bfloat16, jnp.float32

    def call(kernel, outs, ins, out_specs, in_specs, scratch=(), flops=0, moved=0):
        return pl.pallas_call(
            kernel,
            out_shape=outs,
            in_specs=in_specs,
            out_specs=out_specs,
            scratch_shapes=scratch,
            compiler_params=params,
            cost_estimate=pl.CostEstimate(flops=flops, bytes_accessed=moved, transcendentals=0),
        )(*ins)

    def array(shape, kind):
        return jax.ShapeDtypeStruct(shape, kind)

    def add_product(pieces, places, total=None):
        extra = [] if total is None else [total]
        return call(
            functools.partial(project, len(pieces), places),
            array((CORES * rows, 3 * HEAD), f32),
            [tok_own, tok_other, *pieces, *extra],
            VMEM, [VMEM] * (2 + len(pieces) + len(extra)),
            flops=2 * CORES * rows * sum(piece.shape[0] for piece in pieces) * 3 * HEAD,
        )

    tok_other = flip(tok_own, "seq", blocks, 1)
    width = w_out.shape[1]
    half = width // 2
    grid = n == 4 and blocks % (2 * CORES) == 0 and shard % 512 == 0 and width % 256 == 0

    quarter = shard // 4
    layout = lambda parity: quarters_x(parity) + quarters_y(parity)
    if not grid:
        layout = lambda parity: [[0, 1, 2, 3]]
    cut = call(
        functools.partial(cut_qkv, layout),
        [array((len(group) * quarter, 3 * HEAD), bf16) for group in layout(0)],
        [w_qkv], [VMEM] * len(layout(0)), [VMEM],
    )
    out_cut = functools.partial(
        call, cut_out, [array((HEAD, width), bf16)] * 2, [w_out], [VMEM] * 2, [VMEM]
    )
    if grid:
        first_x, rest_x, first_y, rest_y = cut
        x_first = flip(first_x, "dp", n, 1)
        y_first = flip(first_y, "dp", n, 2)
        rest_x, rest_y, x_first, y_first = lax.optimization_barrier(
            (rest_x, rest_y, x_first, y_first)
        )
        x_rest = flip(rest_x, "dp", n, 1)
        y_rest = flip(rest_y, "dp", n, 2)
        here_x = flip(x_first, "dp", n, 2)
        here_y = flip(y_first, "dp", n, 1)
        total = add_product([first_x, rest_x], functools.partial(places_own, shard))
        total = add_product([x_first, y_first], functools.partial(places_near, shard, 0), total)
        swap_x, swap_y, total = lax.optimization_barrier((here_x, here_y, total))
        there_x = flip(swap_x, "seq", blocks, CORES)
        there_y = flip(swap_y, "seq", blocks, CORES)
        far = [here_x, here_y, there_x, there_y]
        total = add_product(far, functools.partial(places_far, shard), total)
        own_mine, own_theirs = out_cut()
        sent, x_rest, y_rest = lax.optimization_barrier((own_mine, x_rest, y_rest))
        out_x = flip(sent, "dp", n, 1)
        out_y = flip(sent, "dp", n, 2)
        pieces, places = [x_rest, y_rest], functools.partial(places_near, shard, 1)
    else:
        pieces, places = [lax.all_gather(cut[0], "dp", axis=0, tiled=True)], lambda: [[0]]
        total = None
    extra = [] if total is None else [total]

    query, state, chip, intra = call(
        functools.partial(project_attend, len(pieces), places),
        [
            array((CORES, rows, HEAD), bf16),
            array((CORES, HEAD, HEAD), f32),
            array((HEAD, HEAD), bf16),
            array((CORES, rows, HEAD), f32),
        ],
        [tok_own, tok_other, *pieces, *extra],
        [VMEM] * 4, [VMEM] * (2 + len(pieces) + len(extra)),
        flops=2 * CORES * rows * sum(piece.shape[0] for piece in pieces) * 3 * HEAD,
    )

    earlier = [
        lax.ppermute(chip, "seq", [(i, i + CORES * k) for i in range(blocks - CORES * k)])
        for k in range(1, blocks // CORES)
    ]
    normed_own, normed_other = call(
        functools.partial(normalise, len(earlier)),
        [array((rows, HEAD), bf16)] * 2,
        [query, state, intra, norm_gain.reshape(heads, HEAD), *earlier],
        [VMEM] * 2, [VMEM] * (4 + len(earlier)),
    )
    normed_got = flip(normed_other, "seq", blocks, 1)

    if grid:
        out_x, out_y, normed_other = lax.optimization_barrier((out_x, out_y, normed_other))
        out_low = flip(out_x[:, :half], "dp", n, 2)
        out_high = flip(out_y[:, half:], "dp", n, 1)
        their_x = flip(out_x, "seq", blocks, 1)
        their_y = flip(out_y, "seq", blocks, 1)
        send_low, send_high, normed_got = lax.optimization_barrier((out_low, out_high, normed_got))
        their_low = flip(send_low, "seq", blocks, 1)
        their_high = flip(send_high, "seq", blocks, 1)
        mine = [own_mine, out_x, out_y, out_low, out_high]
        theirs = [own_theirs, their_x, their_y, their_low, their_high]
        places = functools.partial(places_out, width)
    else:
        mine = [lax.all_gather(out_cut()[0], "dp", axis=1, tiled=True)]
        theirs = [flip(mine[0], "seq", blocks, 1)]
        places = lambda: [0]
    mixed = call(
        functools.partial(mix, len(mine), places),
        array((rows, n * width), bf16),
        [normed_own, normed_got, *mine, *theirs],
        HBM, [VMEM] * (2 + 2 * len(mine)),
        scratch=[pltpu.VMEM((rows, n * width), bf16), pltpu.SemaphoreType.DMA((16,))],
        flops=2 * rows * 2 * HEAD * n * width, moved=2 * rows * n * width,
    )
    return mixed[None]


def solution(mesh):
    n, blocks = mesh.shape["dp"], mesh.shape["seq"]
    return jax.shard_map(
        functools.partial(shards, n, blocks),
        mesh=mesh,
        in_specs=(P("dp", "seq", None), P("dp", None), P(), P(None, "dp")),
        out_specs=P("dp", "seq", None),
        check_vma=False,
    )
```

```python
import functools

import jax
import jax.numpy as jnp
from jax import lax
from jax.experimental import pallas as pl
from jax.experimental.pallas import tpu as pltpu
from jax.sharding import PartitionSpec as P

HEAD = 128
CORES = 2
VMEM_LIMIT = 24 * 1024 * 1024
CUT_LIMIT = 52 * 1024 * 1024
VMEM = pl.BlockSpec(memory_space=pltpu.VMEM)
HBM = pl.BlockSpec(memory_space=pltpu.HBM)


def flip(x, axis, size, mask):
    return lax.ppermute(x, axis, [(i, i ^ mask) for i in range(size)])


def dot(a, b, contract=((1,), (0,))):
    return lax.dot_general(a, b, (contract, ((), ())), preferred_element_type=jnp.float32)


def position():
    at = lax.axis_index("dp")
    seq = lax.axis_index("seq")
    return at, lax.rem(seq, CORES), lax.rem(seq // CORES, 2)


def cut_qkv(count, layout, w_qkv, *refs):
    outs, sem = refs[:count], refs[count]
    _, core, parity = position()
    quarter = w_qkv.shape[0] // 4
    feat = w_qkv.shape[1] // 3
    copies = []
    for out, quarters in zip(outs, layout(parity)):
        for i, q in enumerate(quarters):
            rows = pl.ds(pl.multiple_of(q * quarter, quarter), quarter)
            for j in range(3):
                cols = pl.ds(pl.multiple_of(j * feat + core * HEAD, HEAD), HEAD)
                target = out.at[i * quarter : (i + 1) * quarter, j * HEAD : (j + 1) * HEAD]
                copies.append(pltpu.make_async_copy(w_qkv.at[rows, cols], target, sem.at[len(copies)]))
                copies[-1].start()
    for copy in copies:
        copy.wait()


def cut_out(w_out, mine, theirs):
    _, core, _ = position()
    for out, head in ((mine, core), (theirs, 1 - core)):
        out[...] = w_out[pl.ds(pl.multiple_of(head * HEAD, HEAD), HEAD), :]


def layout_of(parity):
    return [[parity], [1 - parity], [2, 3], [2 + parity], [3 - parity], [0, 1]]


def product(tok_a, tok_b, pieces, places):
    width = pieces[0].shape[0] // len(places[0])
    cols = [pl.ds(place, width) for piece in places for place in piece]
    tok = jnp.concatenate(
        [jnp.concatenate([ref[:, c] for c in cols], axis=1) for ref in (tok_a, tok_b)], axis=0
    )
    weights = jnp.concatenate([piece[...] for piece in pieces], axis=0)
    return dot(tok, weights)


def places_of(shard, offset, groups):
    at, _, parity = position()
    start = (at ^ offset) * shard
    quarter = shard // 4
    return [[pl.multiple_of(start + q * quarter, quarter) for q in group] for group in groups(parity)]


def places_own(shard):
    return places_of(shard, 0, lambda parity: [[0, 1], [2, 3]])


def places_near(shard, which):
    from_x = places_of(shard, 1, lambda parity: layout_of(parity)[:3])
    from_y = places_of(shard, 2, lambda parity: layout_of(parity)[3:])
    return [from_[i] for from_ in (from_x, from_y) for i in which]


def places_far(shard):
    return places_of(shard, 3, lambda parity: [[parity], [2 + parity], [1 - parity], [3 - parity]])


def project(count, places, tok_a, tok_b, *refs):
    pieces, before, total = refs[:count], refs[count:-1], refs[-1]
    term = product(tok_a, tok_b, pieces, places())
    total[...] = before[0][...] + term if before else term


def project_attend(count, places, tok_a, tok_b, *refs):
    pieces, before = refs[:count], refs[count:-4]
    query_out, state_out, chip_out, intra_out = refs[-4:]
    proj = product(tok_a, tok_b, pieces, places())
    if before:
        proj = before[0][...] + proj
    rows = intra_out.shape[1]
    row = lax.broadcasted_iota(jnp.int32, (rows, rows), 0)
    col = lax.broadcasted_iota(jnp.int32, (rows, rows), 1)
    chip = None
    for b in range(CORES):
        part = proj[b * rows : (b + 1) * rows, :]
        act = part[:, : 2 * HEAD]
        act = (act / (1.0 + jnp.exp(-act))).astype(jnp.bfloat16)
        query, keys = act[:, :HEAD], act[:, HEAD:]
        values = part[:, 2 * HEAD :].astype(jnp.bfloat16)
        state = dot(keys, values, ((0,), (0,)))
        chip = state if chip is None else chip + state
        query_out[b] = query
        state_out[b] = state
        scores = dot(query, keys, ((1,), (1,)))
        scores = jnp.where(row >= col, scores, 0.0).astype(jnp.bfloat16)
        intra_out[b] = dot(scores, values)
    chip_out[...] = chip.astype(jnp.bfloat16)


def normalise(count, query, state, intra, gain, *refs):
    earlier, (own_out, other_out) = refs[:count], refs[count:]
    _, core, _ = position()
    base = jnp.zeros((HEAD, HEAD), jnp.float32)
    for ref in earlier:
        base = base + ref[...].astype(jnp.float32)
    odd = core == 1
    own_prefix = jnp.where(odd, base + state[1], base)
    other_prefix = jnp.where(odd, base, base + state[0])
    scale = gain[pl.ds(core, 1), :]
    for b, (prefix, out) in enumerate(((own_prefix, own_out), (other_prefix, other_out))):
        attended = dot(query[b], prefix.astype(jnp.bfloat16)) + intra[b]
        meansq = jnp.mean(attended * attended, axis=-1, keepdims=True)
        out[...] = (attended * lax.rsqrt(meansq + 1e-06) * scale).astype(jnp.bfloat16)


def mix(count, places, own, other, *refs):
    mine, theirs, (out, stage, sem) = refs[:count], refs[count : 2 * count], refs[2 * count :]
    normed = jnp.concatenate([own[...], other[...]], axis=1)
    copies = []
    slot = 0
    for my_rows, their_rows, place in zip(mine, theirs, places()):
        width = my_rows.shape[1]
        step = min(width, 512)
        for at_col in range(0, width, step):
            part = slice(at_col, at_col + step)
            weights = jnp.concatenate([my_rows[:, part], their_rows[:, part]], axis=0)
            here = stage.at[:, slot : slot + step]
            here[...] = dot(normed, weights).astype(jnp.bfloat16)
            cols = pl.ds(pl.multiple_of(place + at_col, 128), step)
            copies.append(pltpu.make_async_copy(here, out.at[:, cols], sem.at[len(copies)]))
            copies[-1].start()
            slot += step
    for copy in copies:
        copy.wait()


def places_out(width):
    at = lax.axis_index("dp")
    offsets = [(0, 0), (1, 0), (2, 0), (3, 0), (3, width // 2)]
    return [(at ^ offset) * width + start for offset, start in offsets]


def shards(n, blocks, tokens, w_qkv, norm_gain, w_out):
    tok_own = tokens[0]
    rows, depth = tok_own.shape
    shard = w_qkv.shape[0]
    heads = norm_gain.shape[0] // HEAD
    bf16, f32 = jnp.bfloat16, jnp.float32

    def call(kernel, outs, ins, out_specs, in_specs, scratch=(), flops=0, moved=0, limit=VMEM_LIMIT):
        return pl.pallas_call(
            kernel,
            out_shape=outs,
            in_specs=in_specs,
            out_specs=out_specs,
            scratch_shapes=scratch,
            compiler_params=pltpu.CompilerParams(vmem_limit_bytes=limit),
            cost_estimate=pl.CostEstimate(flops=flops, bytes_accessed=moved, transcendentals=0),
        )(*ins)

    def array(shape, kind):
        return jax.ShapeDtypeStruct(shape, kind)

    def add_product(pieces, places, total=None):
        extra = [] if total is None else [total]
        return call(
            functools.partial(project, len(pieces), places),
            array((CORES * rows, 3 * HEAD), f32),
            [tok_own, tok_other, *pieces, *extra],
            VMEM, [VMEM] * (2 + len(pieces) + len(extra)),
            flops=rows * HEAD,
        )

    tok_other = flip(tok_own, "seq", blocks, 1)
    width = w_out.shape[1]
    half = width // 2
    grid = n == 4 and blocks % (2 * CORES) == 0 and shard % 512 == 0 and width % 256 == 0

    quarter = shard // 4
    layout = layout_of if grid else lambda parity: [[0, 1, 2, 3]]
    groups = layout(0)
    cut = call(
        functools.partial(cut_qkv, len(groups), layout),
        [array((len(group) * quarter, 3 * HEAD), bf16) for group in groups],
        [w_qkv], [VMEM] * len(groups), [HBM],
        scratch=[pltpu.SemaphoreType.DMA((24,))], moved=4 * shard * 3 * HEAD, limit=CUT_LIMIT,
    )
    out_cut = functools.partial(
        call, cut_out, [array((HEAD, width), bf16)] * 2, [w_out], [VMEM] * 2, [VMEM]
    )
    if grid:
        one_x, two_x, high, one_y, two_y, low = cut
        x_one = flip(one_x, "dp", n, 1)
        y_one = flip(one_y, "dp", n, 2)
        x_two = flip(two_x, "dp", n, 1)
        y_two = flip(two_y, "dp", n, 2)
        here_x = flip(x_one, "dp", n, 2)
        here_y = flip(y_one, "dp", n, 1)
        send_high, send_low, x_two, y_two = lax.optimization_barrier((high, low, x_two, y_two))
        x_last = flip(send_high, "dp", n, 1)
        y_last = flip(send_low, "dp", n, 2)
        total = add_product([low, high], functools.partial(places_own, shard))
        near = [x_one, x_two, y_one, y_two]
        total = add_product(near, functools.partial(places_near, shard, (0, 1)), total)
        swap_x, swap_y, total = lax.optimization_barrier((here_x, here_y, total))
        there_x = flip(swap_x, "seq", blocks, CORES)
        there_y = flip(swap_y, "seq", blocks, CORES)
        far = [here_x, here_y, there_x, there_y]
        total = add_product(far, functools.partial(places_far, shard), total)
        own_mine, own_theirs = out_cut()
        sent, total = lax.optimization_barrier((own_mine, total))
        out_x = flip(sent, "dp", n, 1)
        out_y = flip(sent, "dp", n, 2)
        pieces, places = [x_last, y_last], functools.partial(places_near, shard, (2,))
    else:
        pieces, places = [lax.all_gather(cut[0], "dp", axis=0, tiled=True)], lambda: [[0]]
        total = None
    extra = [] if total is None else [total]

    query, state, chip, intra = call(
        functools.partial(project_attend, len(pieces), places),
        [
            array((CORES, rows, HEAD), bf16),
            array((CORES, HEAD, HEAD), f32),
            array((HEAD, HEAD), bf16),
            array((CORES, rows, HEAD), f32),
        ],
        [tok_own, tok_other, *pieces, *extra],
        [VMEM] * 4, [VMEM] * (2 + len(pieces) + len(extra)),
        flops=2 * CORES * rows * sum(piece.shape[0] for piece in pieces) * 3 * HEAD,
    )

    earlier = [
        lax.ppermute(chip, "seq", [(i, i + CORES * k) for i in range(blocks - CORES * k)])
        for k in range(1, blocks // CORES)
    ]
    normed_own, normed_other = call(
        functools.partial(normalise, len(earlier)),
        [array((rows, HEAD), bf16)] * 2,
        [query, state, intra, norm_gain.reshape(heads, HEAD), *earlier],
        [VMEM] * 2, [VMEM] * (4 + len(earlier)),
    )
    normed_got = flip(normed_other, "seq", blocks, 1)

    if grid:
        out_x, out_y, normed_other = lax.optimization_barrier((out_x, out_y, normed_other))
        out_low = flip(out_x[:, :half], "dp", n, 2)
        out_high = flip(out_y[:, half:], "dp", n, 1)
        their_x = flip(out_x, "seq", blocks, 1)
        their_y = flip(out_y, "seq", blocks, 1)
        send_low, send_high, normed_got = lax.optimization_barrier((out_low, out_high, normed_got))
        their_low = flip(send_low, "seq", blocks, 1)
        their_high = flip(send_high, "seq", blocks, 1)
        mine = [own_mine, out_x, out_y, out_low, out_high]
        theirs = [own_theirs, their_x, their_y, their_low, their_high]
        places = functools.partial(places_out, width)
    else:
        mine = [lax.all_gather(out_cut()[0], "dp", axis=1, tiled=True)]
        theirs = [flip(mine[0], "seq", blocks, 1)]
        places = lambda: [0]
    mixed = call(
        functools.partial(mix, len(mine), places),
        array((rows, n * width), bf16),
        [normed_own, normed_got, *mine, *theirs],
        HBM, [VMEM] * (2 + 2 * len(mine)),
        scratch=[pltpu.VMEM((rows, n * width), bf16), pltpu.SemaphoreType.DMA((16,))],
        flops=2 * rows * 2 * HEAD * n * width, moved=2 * rows * n * width,
    )
    return mixed[None]


def solution(mesh):
    n, blocks = mesh.shape["dp"], mesh.shape["seq"]
    return jax.shard_map(
        functools.partial(shards, n, blocks),
        mesh=mesh,
        in_specs=(P("dp", "seq", None), P("dp", None), P(), P(None, "dp")),
        out_specs=P("dp", "seq", None),
        check_vma=False,
    )
```

```python
import functools

import jax
import jax.numpy as jnp
from jax import lax
from jax.experimental import pallas as pl
from jax.experimental.pallas import tpu as pltpu
from jax.sharding import PartitionSpec as P

HEAD = 128
CORES = 2
VMEM_LIMIT = 24 * 1024 * 1024
CUT_LIMIT = 52 * 1024 * 1024
VMEM = pl.BlockSpec(memory_space=pltpu.VMEM)
HBM = pl.BlockSpec(memory_space=pltpu.HBM)


def flip(x, axis, size, mask):
    return lax.ppermute(x, axis, [(i, i ^ mask) for i in range(size)])


def dot(a, b, contract=((1,), (0,))):
    return lax.dot_general(a, b, (contract, ((), ())), preferred_element_type=jnp.float32)


def position():
    at = lax.axis_index("dp")
    seq = lax.axis_index("seq")
    return at, lax.rem(seq, CORES), lax.rem(seq // CORES, 2)


def cut_qkv(count, layout, w_qkv, *refs):
    outs, sem = refs[:count], refs[count]
    _, core, parity = position()
    quarter = w_qkv.shape[0] // 4
    feat = w_qkv.shape[1] // 3
    copies = []
    for out, quarters in zip(outs, layout(parity)):
        for i, q in enumerate(quarters):
            rows = pl.ds(pl.multiple_of(q * quarter, quarter), quarter)
            for j in range(3):
                cols = pl.ds(pl.multiple_of(j * feat + core * HEAD, HEAD), HEAD)
                target = out.at[i * quarter : (i + 1) * quarter, j * HEAD : (j + 1) * HEAD]
                copies.append(pltpu.make_async_copy(w_qkv.at[rows, cols], target, sem.at[len(copies)]))
                copies[-1].start()
    for copy in copies:
        copy.wait()


def cut_out(w_out, mine, theirs):
    _, core, _ = position()
    for out, head in ((mine, core), (theirs, 1 - core)):
        out[...] = w_out[pl.ds(pl.multiple_of(head * HEAD, HEAD), HEAD), :]


def layout_of(parity):
    return [[parity], [2 + parity], [1 - parity], [3 - parity], [2, 3], [0, 1]]


def product(tok_a, tok_b, pieces, places):
    cols = [
        pl.ds(place, piece.shape[0] // len(group))
        for piece, group in zip(pieces, places)
        for place in group
    ]
    tok = jnp.concatenate(
        [jnp.concatenate([ref[:, c] for c in cols], axis=1) for ref in (tok_a, tok_b)], axis=0
    )
    weights = jnp.concatenate([piece[...] for piece in pieces], axis=0)
    return dot(tok, weights)


def places_of(shard, offset, groups):
    at, _, parity = position()
    start = (at ^ offset) * shard
    quarter = shard // 4
    return [[pl.multiple_of(start + q * quarter, quarter) for q in group] for group in groups(parity)]


def places_own(shard):
    return places_of(shard, 0, lambda parity: [[0, 1], [2, 3]])


def places_near(shard, which):
    from_x = places_of(shard, 1, lambda parity: layout_of(parity)[0::2])
    from_y = places_of(shard, 2, lambda parity: layout_of(parity)[1::2])
    return [from_[i] for from_ in (from_x, from_y) for i in which]


def places_far(shard):
    return places_of(shard, 3, lambda parity: [[parity], [2 + parity], [1 - parity], [3 - parity]])


def places_rest(shard):
    return places_far(shard) + places_near(shard, (2,))


def project(count, places, tok_a, tok_b, *refs):
    pieces, before, total = refs[:count], refs[count:-1], refs[-1]
    term = product(tok_a, tok_b, pieces, places())
    total[...] = before[0][...] + term if before else term


def project_attend(count, places, tok_a, tok_b, *refs):
    pieces, before = refs[:count], refs[count:-4]
    query_out, state_out, chip_out, intra_out = refs[-4:]
    proj = product(tok_a, tok_b, pieces, places())
    if before:
        proj = before[0][...] + proj
    rows = intra_out.shape[1]
    row = lax.broadcasted_iota(jnp.int32, (rows, rows), 0)
    col = lax.broadcasted_iota(jnp.int32, (rows, rows), 1)
    chip = None
    for b in range(CORES):
        part = proj[b * rows : (b + 1) * rows, :]
        act = part[:, : 2 * HEAD]
        act = (act / (1.0 + jnp.exp(-act))).astype(jnp.bfloat16)
        query, keys = act[:, :HEAD], act[:, HEAD:]
        values = part[:, 2 * HEAD :].astype(jnp.bfloat16)
        state = dot(keys, values, ((0,), (0,)))
        chip = state if chip is None else chip + state
        query_out[b] = query
        state_out[b] = state
        scores = dot(query, keys, ((1,), (1,)))
        scores = jnp.where(row >= col, scores, 0.0).astype(jnp.bfloat16)
        intra_out[b] = dot(scores, values)
    chip_out[...] = chip.astype(jnp.bfloat16)


def normalise(masks, query, state, intra, gain, *refs):
    others, (own_out, other_out) = refs[: len(masks)], refs[len(masks) :]
    _, core, _ = position()
    chip_at = lax.axis_index("seq") // CORES
    base = jnp.zeros((HEAD, HEAD), jnp.float32)
    for mask, ref in zip(masks, others):
        base = base + jnp.where((chip_at ^ mask) < chip_at, ref[...].astype(jnp.float32), 0.0)
    odd = core == 1
    own_prefix = jnp.where(odd, base + state[1], base)
    other_prefix = jnp.where(odd, base, base + state[0])
    scale = gain[pl.ds(core, 1), :]
    for b, (prefix, out) in enumerate(((own_prefix, own_out), (other_prefix, other_out))):
        attended = dot(query[b], prefix.astype(jnp.bfloat16)) + intra[b]
        meansq = jnp.mean(attended * attended, axis=-1, keepdims=True)
        out[...] = (attended * lax.rsqrt(meansq + 1e-06) * scale).astype(jnp.bfloat16)


def mix(count, places, own, other, *refs):
    mine, theirs, (out, stage, sem) = refs[:count], refs[count : 2 * count], refs[2 * count :]
    normed = jnp.concatenate([own[...], other[...]], axis=1)
    copies = []
    slot = 0
    for my_rows, their_rows, place in zip(mine, theirs, places()):
        width = my_rows.shape[1]
        step = min(width, 512)
        for at_col in range(0, width, step):
            part = slice(at_col, at_col + step)
            weights = jnp.concatenate([my_rows[:, part], their_rows[:, part]], axis=0)
            here = stage.at[:, slot : slot + step]
            here[...] = dot(normed, weights).astype(jnp.bfloat16)
            cols = pl.ds(pl.multiple_of(place + at_col, 128), step)
            copies.append(pltpu.make_async_copy(here, out.at[:, cols], sem.at[len(copies)]))
            copies[-1].start()
            slot += step
    for copy in copies:
        copy.wait()


def places_out(width):
    at = lax.axis_index("dp")
    return [(at ^ offset) * width for offset in range(4)]


def shards(n, blocks, tokens, w_qkv, norm_gain, w_out):
    tok_own = tokens[0]
    rows, depth = tok_own.shape
    shard = w_qkv.shape[0]
    heads = norm_gain.shape[0] // HEAD
    bf16, f32 = jnp.bfloat16, jnp.float32

    def call(kernel, outs, ins, out_specs, in_specs, scratch=(), flops=0, moved=0, limit=VMEM_LIMIT):
        return pl.pallas_call(
            kernel,
            out_shape=outs,
            in_specs=in_specs,
            out_specs=out_specs,
            scratch_shapes=scratch,
            compiler_params=pltpu.CompilerParams(vmem_limit_bytes=limit),
            cost_estimate=pl.CostEstimate(flops=flops, bytes_accessed=moved, transcendentals=0),
        )(*ins)

    def array(shape, kind):
        return jax.ShapeDtypeStruct(shape, kind)

    def add_product(pieces, places, total=None):
        extra = [] if total is None else [total]
        return call(
            functools.partial(project, len(pieces), places),
            array((CORES * rows, 3 * HEAD), f32),
            [tok_own, tok_other, *pieces, *extra],
            VMEM, [VMEM] * (2 + len(pieces) + len(extra)),
            flops=rows * HEAD,
        )

    tok_other = flip(tok_own, "seq", blocks, 1)
    width = w_out.shape[1]
    grid = n == 4 and blocks % (2 * CORES) == 0 and shard % 512 == 0 and width % 256 == 0

    quarter = shard // 4
    layout = layout_of if grid else lambda parity: [[0, 1, 2, 3]]

    def cut(which):
        groups = layout(0)[which]
        return call(
            functools.partial(cut_qkv, len(groups), lambda parity: layout(parity)[which]),
            [array((len(group) * quarter, 3 * HEAD), bf16) for group in groups],
            [w_qkv], [VMEM] * len(groups), [HBM],
            scratch=[pltpu.SemaphoreType.DMA((24,))], limit=CUT_LIMIT,
        )

    out_cut = functools.partial(
        call, cut_out, [array((HEAD, width), bf16)] * 2, [w_out], [VMEM] * 2, [VMEM]
    )
    if grid:
        one_x, one_y, two_x, two_y, high, low = cut(slice(0, 6))
        x_one = flip(one_x, "dp", n, 1)
        y_one = flip(one_y, "dp", n, 2)
        x_two = flip(two_x, "dp", n, 1)
        y_two = flip(two_y, "dp", n, 2)
        x_one, y_one = lax.optimization_barrier((x_one, y_one))
        here_x = flip(x_one, "dp", n, 2)
        here_y = flip(y_one, "dp", n, 1)
        there_x = flip(here_x, "seq", blocks, CORES)
        there_y = flip(here_y, "seq", blocks, CORES)
        send_high, send_low, x_two, y_two = lax.optimization_barrier((high, low, x_two, y_two))
        x_last = flip(send_high, "dp", n, 1)
        y_last = flip(send_low, "dp", n, 2)
        low, high, here_x, here_y = lax.optimization_barrier((low, high, here_x, here_y))
        total = add_product([low, high], functools.partial(places_own, shard))
        near = [x_one, x_two, y_one, y_two]
        total = add_product(near, functools.partial(places_near, shard, (0, 1)), total)
        own_mine, own_theirs = out_cut()
        sent, there_x, total = lax.optimization_barrier((own_mine, there_x, total))
        out_x = flip(sent, "dp", n, 1)
        out_y = flip(sent, "dp", n, 2)
        pieces = [here_x, here_y, there_x, there_y, x_last, y_last]
        places = functools.partial(places_rest, shard)
    else:
        pieces, places = [lax.all_gather(cut(slice(0, 1))[0], "dp", axis=0, tiled=True)], lambda: [[0]]
        total = None
    extra = [] if total is None else [total]

    query, state, chip, intra = call(
        functools.partial(project_attend, len(pieces), places),
        [
            array((CORES, rows, HEAD), bf16),
            array((CORES, HEAD, HEAD), f32),
            array((HEAD, HEAD), bf16),
            array((CORES, rows, HEAD), f32),
        ],
        [tok_own, tok_other, *pieces, *extra],
        [VMEM] * 4, [VMEM] * (2 + len(pieces) + len(extra)),
        flops=2 * CORES * rows * sum(piece.shape[0] for piece in pieces) * 3 * HEAD,
    )

    masks = range(1, blocks // CORES)
    others = [flip(chip, "seq", blocks, CORES * mask) for mask in masks]
    if grid:
        sent, out_x, others[-1] = lax.optimization_barrier((sent, out_x, others[-1]))
        out_d = flip(sent, "dp", n, 3)
    normed_own, normed_other = call(
        functools.partial(normalise, masks),
        [array((rows, HEAD), bf16)] * 2,
        [query, state, intra, norm_gain.reshape(heads, HEAD), *others],
        [VMEM] * 2, [VMEM] * (4 + len(masks)),
    )
    normed_got = flip(normed_other, "seq", blocks, 1)

    if grid:
        out_x, out_y, normed_other = lax.optimization_barrier((out_x, out_y, normed_other))
        their_x = flip(out_x, "seq", blocks, 1)
        their_y = flip(out_y, "seq", blocks, 1)
        send_d, normed_got = lax.optimization_barrier((out_d, normed_got))
        their_d = flip(send_d, "seq", blocks, 1)
        mine = [own_mine, out_x, out_y, out_d]
        theirs = [own_theirs, their_x, their_y, their_d]
        places = functools.partial(places_out, width)
    else:
        mine = [lax.all_gather(out_cut()[0], "dp", axis=1, tiled=True)]
        theirs = [flip(mine[0], "seq", blocks, 1)]
        places = lambda: [0]
    mixed = call(
        functools.partial(mix, len(mine), places),
        array((rows, n * width), bf16),
        [normed_own, normed_got, *mine, *theirs],
        HBM, [VMEM] * (2 + 2 * len(mine)),
        scratch=[pltpu.VMEM((rows, n * width), bf16), pltpu.SemaphoreType.DMA((16,))],
        flops=2 * rows * 2 * HEAD * n * width, moved=2 * rows * n * width,
    )
    return mixed[None]


def solution(mesh):
    n, blocks = mesh.shape["dp"], mesh.shape["seq"]
    return jax.shard_map(
        functools.partial(shards, n, blocks),
        mesh=mesh,
        in_specs=(P("dp", "seq", None), P("dp", None), P(), P(None, "dp")),
        out_specs=P("dp", "seq", None),
        check_vma=False,
    )
```

```python
import functools

import jax
import jax.numpy as jnp
from jax import lax
from jax.experimental import pallas as pl
from jax.experimental.pallas import tpu as pltpu
from jax.sharding import PartitionSpec as P

HEAD = 128
CORES = 2
VMEM_LIMIT = 24 * 1024 * 1024
CUT_LIMIT = 52 * 1024 * 1024
VMEM = pl.BlockSpec(memory_space=pltpu.VMEM)
HBM = pl.BlockSpec(memory_space=pltpu.HBM)


def flip(x, axis, size, mask):
    return lax.ppermute(x, axis, [(i, i ^ mask) for i in range(size)])


def dot(a, b, contract=((1,), (0,))):
    return lax.dot_general(a, b, (contract, ((), ())), preferred_element_type=jnp.float32)


def position():
    at = lax.axis_index("dp")
    seq = lax.axis_index("seq")
    return at, lax.rem(seq, CORES), lax.rem(seq // CORES, 2)


def cut_qkv(layout, w_qkv, *refs):
    outs, sem = refs[:-1], refs[-1]
    _, core, parity = position()
    shard = w_qkv.shape[0]
    feat = w_qkv.shape[1] // 3
    copies = []
    for out, start in zip(outs, layout(shard, parity)):
        rows = pl.ds(pl.multiple_of(start, 16), out.shape[0])
        for j in range(3):
            cols = pl.ds(pl.multiple_of(j * feat + core * HEAD, HEAD), HEAD)
            target = out.at[:, j * HEAD : (j + 1) * HEAD]
            copies.append(pltpu.make_async_copy(w_qkv.at[rows, cols], target, sem.at[len(copies)]))
            copies[-1].start()
    for copy in copies:
        copy.wait()


def cut_out(w_out, mine, theirs):
    _, core, _ = position()
    for out, head in ((mine, core), (theirs, 1 - core)):
        out[...] = w_out[pl.ds(pl.multiple_of(head * HEAD, HEAD), HEAD), :]


def split_rows(shard, parity):
    eighth = shard // 8
    return [parity * 2 * eighth, (1 - parity) * 2 * eighth, 4 * eighth, parity * 4 * eighth, (parity * 4 + 2) * eighth]


def product(tok_a, tok_b, pieces, places):
    cols = [
        pl.ds(pl.multiple_of(place, 128), piece.shape[0]) for piece, place in zip(pieces, places)
    ]
    tok = jnp.concatenate(
        [jnp.concatenate([ref[:, c] for c in cols], axis=1) for ref in (tok_a, tok_b)], axis=0
    )
    weights = jnp.concatenate([piece[...] for piece in pieces], axis=0)
    return dot(tok, weights)


def places_of(shard, wanted):
    at, _, parity = position()
    kinds = dict(zip(("mine", "theirs", "rest", "half", "half2"), split_rows(shard, parity)))
    kinds["other half"] = (1 - parity) * (shard // 2)
    kinds["other half2"] = kinds["other half"] + shard // 4
    return [(at ^ offset) * shard + kinds[kind] for offset, kind in wanted]


def project(count, places, tok_a, tok_b, *refs):
    pieces, before, total = refs[:count], refs[count:-1], refs[-1]
    term = product(tok_a, tok_b, pieces, places())
    total[...] = before[0][...] + term if before else term


def project_attend(count, places, tok_a, tok_b, *refs):
    pieces, before = refs[:count], refs[count:-4]
    query_out, state_out, chip_out, intra_out = refs[-4:]
    proj = product(tok_a, tok_b, pieces, places())
    if before:
        proj = before[0][...] + proj
    rows = intra_out.shape[1]
    row = lax.broadcasted_iota(jnp.int32, (rows, rows), 0)
    col = lax.broadcasted_iota(jnp.int32, (rows, rows), 1)
    chip = None
    for b in range(CORES):
        part = proj[b * rows : (b + 1) * rows, :]
        act = part[:, : 2 * HEAD]
        act = (act / (1.0 + jnp.exp(-act))).astype(jnp.bfloat16)
        query, keys = act[:, :HEAD], act[:, HEAD:]
        values = part[:, 2 * HEAD :].astype(jnp.bfloat16)
        state = dot(keys, values, ((0,), (0,)))
        chip = state if chip is None else chip + state
        query_out[b] = query
        state_out[b] = state
        scores = dot(query, keys, ((1,), (1,)))
        scores = jnp.where(row >= col, scores, 0.0).astype(jnp.bfloat16)
        intra_out[b] = dot(scores, values)
    chip_out[...] = chip.astype(jnp.bfloat16)


def normalise(masks, query, state, intra, gain, *refs):
    others, (own_out, other_out) = refs[: len(masks)], refs[len(masks) :]
    _, core, _ = position()
    chip_at = lax.axis_index("seq") // CORES
    base = jnp.zeros((HEAD, HEAD), jnp.float32)
    for mask, ref in zip(masks, others):
        base = base + jnp.where((chip_at ^ mask) < chip_at, ref[...].astype(jnp.float32), 0.0)
    odd = core == 1
    own_prefix = jnp.where(odd, base + state[1], base)
    other_prefix = jnp.where(odd, base, base + state[0])
    scale = gain[pl.ds(core, 1), :]
    for b, (prefix, out) in enumerate(((own_prefix, own_out), (other_prefix, other_out))):
        attended = dot(query[b], prefix.astype(jnp.bfloat16)) + intra[b]
        meansq = jnp.mean(attended * attended, axis=-1, keepdims=True)
        out[...] = (attended * lax.rsqrt(meansq + 1e-06) * scale).astype(jnp.bfloat16)


def mix(count, places, own, other, *refs):
    mine, theirs, (out, stage, sem) = refs[:count], refs[count : 2 * count], refs[2 * count :]
    normed = jnp.concatenate([own[...], other[...]], axis=1)
    copies = []
    slot = 0
    for my_rows, their_rows, place in zip(mine, theirs, places()):
        width = my_rows.shape[1]
        step = min(width, 512)
        for at_col in range(0, width, step):
            part = slice(at_col, at_col + step)
            weights = jnp.concatenate([my_rows[:, part], their_rows[:, part]], axis=0)
            here = stage.at[:, slot : slot + step]
            here[...] = dot(normed, weights).astype(jnp.bfloat16)
            cols = pl.ds(pl.multiple_of(place + at_col, 128), step)
            copies.append(pltpu.make_async_copy(here, out.at[:, cols], sem.at[len(copies)]))
            copies[-1].start()
            slot += step
    for copy in copies:
        copy.wait()


def places_out(width):
    at = lax.axis_index("dp")
    return [(at ^ offset) * width for offset in range(4)]


def shards(n, blocks, tokens, w_qkv, norm_gain, w_out):
    tok_own = tokens[0]
    rows, depth = tok_own.shape
    shard = w_qkv.shape[0]
    heads = norm_gain.shape[0] // HEAD
    bf16, f32 = jnp.bfloat16, jnp.float32

    def call(kernel, outs, ins, out_specs, in_specs, scratch=(), flops=0, moved=0, limit=VMEM_LIMIT):
        return pl.pallas_call(
            kernel,
            out_shape=outs,
            in_specs=in_specs,
            out_specs=out_specs,
            scratch_shapes=scratch,
            compiler_params=pltpu.CompilerParams(vmem_limit_bytes=limit),
            cost_estimate=pl.CostEstimate(flops=flops, bytes_accessed=moved, transcendentals=0),
        )(*ins)

    def array(shape, kind):
        return jax.ShapeDtypeStruct(shape, kind)

    def add_product(pieces, places, total=None):
        extra = [] if total is None else [total]
        return call(
            functools.partial(project, len(pieces), places),
            array((CORES * rows, 3 * HEAD), f32),
            [tok_own, tok_other, *pieces, *extra],
            VMEM, [VMEM] * (2 + len(pieces) + len(extra)),
            flops=rows * HEAD,
        )

    tok_other = flip(tok_own, "seq", blocks, 1)
    width = w_out.shape[1]
    grid = n == 4 and blocks % (2 * CORES) == 0 and shard % 1024 == 0 and width % 256 == 0

    def cut(layout, *sizes):
        return call(
            functools.partial(cut_qkv, layout),
            [array((size, 3 * HEAD), bf16) for size in sizes],
            [w_qkv], [VMEM] * len(sizes), [HBM],
            scratch=[pltpu.SemaphoreType.DMA((3 * len(sizes),))], limit=CUT_LIMIT,
        )

    out_cut = functools.partial(
        call, cut_out, [array((HEAD, width), bf16)] * 2, [w_out], [VMEM] * 2, [VMEM]
    )
    total = None
    if grid:
        eighth = shard // 8
        mine, theirs, rest, part, part2 = cut(split_rows, 2 * eighth, 2 * eighth, 4 * eighth, 2 * eighth, 2 * eighth)
        x_mine = flip(mine, "dp", n, 1)
        y_mine = flip(mine, "dp", n, 2)
        d_half = flip(part, "dp", n, 3)
        d_half2 = flip(part2, "dp", n, 3)
        send, x_mine, y_mine, tok_other = lax.optimization_barrier((rest, x_mine, y_mine, tok_other))
        x_rest = flip(send, "dp", n, 1)
        y_rest = flip(send, "dp", n, 2)
        x_theirs = flip(x_mine, "seq", blocks, CORES)
        y_theirs = flip(y_mine, "seq", blocks, CORES)
        d_other = flip(d_half, "seq", blocks, CORES)
        d_other2 = flip(d_half2, "seq", blocks, CORES)

        def places(*wanted):
            return functools.partial(places_of, shard, wanted)

        mine, x_mine, y_mine = lax.optimization_barrier((mine, x_mine, y_mine))
        total = add_product([mine, theirs, rest], places((0, "mine"), (0, "theirs"), (0, "rest")))
        total = add_product(
            [x_mine, y_mine, x_theirs, y_theirs, d_half, d_half2],
            places((1, "mine"), (2, "mine"), (1, "theirs"), (2, "theirs"), (3, "half"), (3, "half2")), total,
        )
        own_mine, own_theirs = out_cut()
        sent, total = lax.optimization_barrier((own_mine, total))
        out_x = flip(sent, "dp", n, 1)
        out_y = flip(sent, "dp", n, 2)
        out_d = flip(sent, "dp", n, 3)
        total = add_product([d_other, d_other2], places((3, "other half"), (3, "other half2")), total)
        pieces = [x_rest, y_rest]
        places = places((1, "rest"), (2, "rest"))
    else:
        whole = cut(lambda shard, parity: [0], shard)[0]
        pieces, places = [lax.all_gather(whole, "dp", axis=0, tiled=True)], lambda: [0]
    extra = [] if total is None else [total]

    query, state, chip, intra = call(
        functools.partial(project_attend, len(pieces), places),
        [
            array((CORES, rows, HEAD), bf16),
            array((CORES, HEAD, HEAD), f32),
            array((HEAD, HEAD), bf16),
            array((CORES, rows, HEAD), f32),
        ],
        [tok_own, tok_other, *pieces, *extra],
        [VMEM] * 4, [VMEM] * (2 + len(pieces) + len(extra)),
        flops=2 * CORES * rows * sum(piece.shape[0] for piece in pieces) * 3 * HEAD,
    )

    masks = range(1, blocks // CORES)
    others = [flip(chip, "seq", blocks, CORES * mask) for mask in masks]
    normed_own, normed_other = call(
        functools.partial(normalise, masks),
        [array((rows, HEAD), bf16)] * 2,
        [query, state, intra, norm_gain.reshape(heads, HEAD), *others],
        [VMEM] * 2, [VMEM] * (4 + len(masks)),
    )
    normed_got = flip(normed_other, "seq", blocks, 1)

    if grid:
        out_x, out_y, normed_other = lax.optimization_barrier((out_x, out_y, normed_other))
        their_x = flip(out_x, "seq", blocks, 1)
        their_y = flip(out_y, "seq", blocks, 1)
        send_d, normed_got = lax.optimization_barrier((out_d, normed_got))
        their_d = flip(send_d, "seq", blocks, 1)
        mine = [own_mine, out_x, out_y, out_d]
        theirs = [own_theirs, their_x, their_y, their_d]
        places = functools.partial(places_out, width)
    else:
        mine = [lax.all_gather(out_cut()[0], "dp", axis=1, tiled=True)]
        theirs = [flip(mine[0], "seq", blocks, 1)]
        places = lambda: [0]
    mixed = call(
        functools.partial(mix, len(mine), places),
        array((rows, n * width), bf16),
        [normed_own, normed_got, *mine, *theirs],
        HBM, [VMEM] * (2 + 2 * len(mine)),
        scratch=[pltpu.VMEM((rows, n * width), bf16), pltpu.SemaphoreType.DMA((16,))],
        flops=2 * rows * 2 * HEAD * n * width, moved=2 * rows * n * width,
    )
    return mixed[None]


def solution(mesh):
    n, blocks = mesh.shape["dp"], mesh.shape["seq"]
    return jax.shard_map(
        functools.partial(shards, n, blocks),
        mesh=mesh,
        in_specs=(P("dp", "seq", None), P("dp", None), P(), P(None, "dp")),
        out_specs=P("dp", "seq", None),
        check_vma=False,
    )
```

```python
import functools

import jax
import jax.numpy as jnp
from jax import lax
from jax.experimental import pallas as pl
from jax.experimental.pallas import tpu as pltpu
from jax.sharding import PartitionSpec as P

HEAD = 128
CORES = 2
VMEM_LIMIT = 24 * 1024 * 1024
CUT_LIMIT = 52 * 1024 * 1024
VMEM = pl.BlockSpec(memory_space=pltpu.VMEM)
HBM = pl.BlockSpec(memory_space=pltpu.HBM)


def flip(x, axis, size, mask):
    return lax.ppermute(x, axis, [(i, i ^ mask) for i in range(size)])


def dot(a, b, contract=((1,), (0,))):
    return lax.dot_general(a, b, (contract, ((), ())), preferred_element_type=jnp.float32)


def position():
    return lax.axis_index("dp"), lax.rem(lax.axis_index("seq"), CORES)


def quarter_of():
    return lax.rem(lax.axis_index("seq") // CORES, 4)


def cut_qkv(layout, w_qkv, *refs):
    outs, sem = refs[:-1], refs[-1]
    _, core = position()
    shard = w_qkv.shape[0]
    feat = w_qkv.shape[1] // 3
    copies = []
    for out, start in zip(outs, layout(shard)):
        rows = pl.ds(pl.multiple_of(start, 16), out.shape[0])
        for j in range(3):
            cols = pl.ds(pl.multiple_of(j * feat + core * HEAD, HEAD), HEAD)
            target = out.at[:, j * HEAD : (j + 1) * HEAD]
            copies.append(pltpu.make_async_copy(w_qkv.at[rows, cols], target, sem.at[len(copies)]))
            copies[-1].start()
    for copy in copies:
        copy.wait()


def cut_out(w_out, mine, theirs):
    _, core = position()
    for out, head in ((mine, core), (theirs, 1 - core)):
        out[...] = w_out[pl.ds(pl.multiple_of(head * HEAD, HEAD), HEAD), :]


def product(tok_a, tok_b, pieces, places):
    cols = [
        pl.ds(pl.multiple_of(place, 128), piece.shape[0]) for piece, place in zip(pieces, places)
    ]
    tok = jnp.concatenate(
        [jnp.concatenate([ref[:, c] for c in cols], axis=1) for ref in (tok_a, tok_b)], axis=0
    )
    weights = jnp.concatenate([piece[...] for piece in pieces], axis=0)
    return dot(tok, weights)


def places_near(shard, offsets):
    at = lax.axis_index("dp")
    return [(at ^ offset) * shard for offset in offsets]


def places_far(shard):
    start = places_near(shard, (3,))[0]
    mine = quarter_of()
    return [start + (mine ^ mask) * (shard // 4) for mask in range(4)]


def project(count, places, tok_a, tok_b, *refs):
    pieces, before, total = refs[:count], refs[count:-1], refs[-1]
    term = product(tok_a, tok_b, pieces, places())
    total[...] = before[0][...] + term if before else term


def project_attend(count, places, tok_a, tok_b, *refs):
    pieces, before = refs[:count], refs[count:-4]
    query_out, state_out, chip_out, intra_out = refs[-4:]
    proj = product(tok_a, tok_b, pieces, places())
    if before:
        proj = before[0][...] + proj
    rows = intra_out.shape[1]
    row = lax.broadcasted_iota(jnp.int32, (rows, rows), 0)
    col = lax.broadcasted_iota(jnp.int32, (rows, rows), 1)
    chip = None
    for b in range(CORES):
        part = proj[b * rows : (b + 1) * rows, :]
        act = part[:, : 2 * HEAD]
        act = (act / (1.0 + jnp.exp(-act))).astype(jnp.bfloat16)
        query, keys = act[:, :HEAD], act[:, HEAD:]
        values = part[:, 2 * HEAD :].astype(jnp.bfloat16)
        state = dot(keys, values, ((0,), (0,)))
        chip = state if chip is None else chip + state
        query_out[b] = query
        state_out[b] = state
        scores = dot(query, keys, ((1,), (1,)))
        scores = jnp.where(row >= col, scores, 0.0).astype(jnp.bfloat16)
        intra_out[b] = dot(scores, values)
    chip_out[...] = chip.astype(jnp.bfloat16)


def normalise(masks, query, state, intra, gain, *refs):
    others, (own_out, other_out) = refs[: len(masks)], refs[len(masks) :]
    _, core = position()
    chip_at = lax.axis_index("seq") // CORES
    base = jnp.zeros((HEAD, HEAD), jnp.float32)
    for mask, ref in zip(masks, others):
        base = base + jnp.where((chip_at ^ mask) < chip_at, ref[...].astype(jnp.float32), 0.0)
    odd = core == 1
    own_prefix = jnp.where(odd, base + state[1], base)
    other_prefix = jnp.where(odd, base, base + state[0])
    scale = gain[pl.ds(core, 1), :]
    for b, (prefix, out) in enumerate(((own_prefix, own_out), (other_prefix, other_out))):
        attended = dot(query[b], prefix.astype(jnp.bfloat16)) + intra[b]
        meansq = jnp.mean(attended * attended, axis=-1, keepdims=True)
        out[...] = (attended * lax.rsqrt(meansq + 1e-06) * scale).astype(jnp.bfloat16)


def mix(count, places, own, other, *refs):
    mine, theirs, (out, stage, sem) = refs[:count], refs[count : 2 * count], refs[2 * count :]
    normed = jnp.concatenate([own[...], other[...]], axis=1)
    copies = []
    slot = 0
    for my_rows, their_rows, place in zip(mine, theirs, places()):
        width = my_rows.shape[1]
        step = min(width, 512)
        for at_col in range(0, width, step):
            part = slice(at_col, at_col + step)
            weights = jnp.concatenate([my_rows[:, part], their_rows[:, part]], axis=0)
            here = stage.at[:, slot : slot + step]
            here[...] = dot(normed, weights).astype(jnp.bfloat16)
            cols = pl.ds(pl.multiple_of(place + at_col, 128), step)
            copies.append(pltpu.make_async_copy(here, out.at[:, cols], sem.at[len(copies)]))
            copies[-1].start()
            slot += step
    for copy in copies:
        copy.wait()


def places_out(width):
    at = lax.axis_index("dp")
    return [(at ^ offset) * width for offset in range(4)]


def shards(n, blocks, tokens, w_qkv, norm_gain, w_out):
    tok_own = tokens[0]
    rows, depth = tok_own.shape
    shard = w_qkv.shape[0]
    heads = norm_gain.shape[0] // HEAD
    bf16, f32 = jnp.bfloat16, jnp.float32

    def call(kernel, outs, ins, out_specs, in_specs, scratch=(), flops=0, moved=0, limit=VMEM_LIMIT):
        return pl.pallas_call(
            kernel,
            out_shape=outs,
            in_specs=in_specs,
            out_specs=out_specs,
            scratch_shapes=scratch,
            compiler_params=pltpu.CompilerParams(vmem_limit_bytes=limit),
            cost_estimate=pl.CostEstimate(flops=flops, bytes_accessed=moved, transcendentals=0),
        )(*ins)

    def array(shape, kind):
        return jax.ShapeDtypeStruct(shape, kind)

    def add_product(pieces, places, total=None):
        extra = [] if total is None else [total]
        return call(
            functools.partial(project, len(pieces), places),
            array((CORES * rows, 3 * HEAD), f32),
            [tok_own, tok_other, *pieces, *extra],
            VMEM, [VMEM] * (2 + len(pieces) + len(extra)),
            flops=rows * HEAD * (1 if total is not None else 1000000),
        )

    tok_other = flip(tok_own, "seq", blocks, 1)
    width = w_out.shape[1]
    grid = n == 4 and blocks % (4 * CORES) == 0 and shard % 512 == 0 and width % 256 == 0

    def cut(layout, *sizes):
        return call(
            functools.partial(cut_qkv, layout),
            [array((size, 3 * HEAD), bf16) for size in sizes],
            [w_qkv], [VMEM] * len(sizes), [HBM],
            scratch=[pltpu.SemaphoreType.DMA((3 * len(sizes),))], limit=CUT_LIMIT,
        )

    out_cut = functools.partial(
        call, cut_out, [array((HEAD, width), bf16)] * 2, [w_out], [VMEM] * 2, [VMEM]
    )
    total = None
    if grid:
        quarter = shard // 4
        own, part = cut(lambda shard: [0, quarter_of() * quarter], shard, quarter)
        far = [flip(part, "dp", n, 3)]
        from_x = flip(own, "dp", n, 1)
        from_y = flip(own, "dp", n, 2)
        far += [flip(far[0], "seq", blocks, CORES * mask) for mask in (1, 2, 3)]
        here, own = lax.optimization_barrier((far[0], own))
        total = add_product([own], functools.partial(places_near, shard, (0,)))
        own_mine, own_theirs = out_cut()
        sent, far[1], total = lax.optimization_barrier((own_mine, far[1], total))
        out_x = flip(sent, "dp", n, 1)
        out_y = flip(sent, "dp", n, 2)
        out_d = flip(sent, "dp", n, 3)
        total = add_product([from_x, from_y], functools.partial(places_near, shard, (1, 2)), total)
        pieces, places = far, functools.partial(places_far, shard)
    else:
        whole = cut(lambda shard: [0], shard)[0]
        pieces, places = [lax.all_gather(whole, "dp", axis=0, tiled=True)], lambda: [0]
    extra = [] if total is None else [total]

    query, state, chip, intra = call(
        functools.partial(project_attend, len(pieces), places),
        [
            array((CORES, rows, HEAD), bf16),
            array((CORES, HEAD, HEAD), f32),
            array((HEAD, HEAD), bf16),
            array((CORES, rows, HEAD), f32),
        ],
        [tok_own, tok_other, *pieces, *extra],
        [VMEM] * 4, [VMEM] * (2 + len(pieces) + len(extra)),
        flops=2 * CORES * rows * sum(piece.shape[0] for piece in pieces) * 3 * HEAD,
    )

    masks = range(1, blocks // CORES)
    others = [flip(chip, "seq", blocks, CORES * mask) for mask in masks]
    normed_own, normed_other = call(
        functools.partial(normalise, masks),
        [array((rows, HEAD), bf16)] * 2,
        [query, state, intra, norm_gain.reshape(heads, HEAD), *others],
        [VMEM] * 2, [VMEM] * (4 + len(masks)),
    )
    normed_got = flip(normed_other, "seq", blocks, 1)

    if grid:
        out_x, out_y, normed_other = lax.optimization_barrier((out_x, out_y, normed_other))
        their_x = flip(out_x, "seq", blocks, 1)
        their_y = flip(out_y, "seq", blocks, 1)
        send_d, normed_got = lax.optimization_barrier((out_d, normed_got))
        their_d = flip(send_d, "seq", blocks, 1)
        mine = [own_mine, out_x, out_y, out_d]
        theirs = [own_theirs, their_x, their_y, their_d]
        places = functools.partial(places_out, width)
    else:
        mine = [lax.all_gather(out_cut()[0], "dp", axis=1, tiled=True)]
        theirs = [flip(mine[0], "seq", blocks, 1)]
        places = lambda: [0]
    mixed = call(
        functools.partial(mix, len(mine), places),
        array((rows, n * width), bf16),
        [normed_own, normed_got, *mine, *theirs],
        HBM, [VMEM] * (2 + 2 * len(mine)),
        scratch=[pltpu.VMEM((rows, n * width), bf16), pltpu.SemaphoreType.DMA((16,))],
        flops=2 * rows * 2 * HEAD * n * width, moved=2 * rows * n * width,
    )
    return mixed[None]


def solution(mesh):
    n, blocks = mesh.shape["dp"], mesh.shape["seq"]
    return jax.shard_map(
        functools.partial(shards, n, blocks),
        mesh=mesh,
        in_specs=(P("dp", "seq", None), P("dp", None), P(), P(None, "dp")),
        out_specs=P("dp", "seq", None),
        check_vma=False,
    )
```

```python
import functools

import jax
import jax.numpy as jnp
from jax import lax
from jax.experimental import pallas as pl
from jax.experimental.pallas import tpu as pltpu
from jax.sharding import PartitionSpec as P

HEAD = 128
CORES = 2
VMEM_LIMIT = 24 * 1024 * 1024
CUT_LIMIT = 52 * 1024 * 1024
VMEM = pl.BlockSpec(memory_space=pltpu.VMEM)
HBM = pl.BlockSpec(memory_space=pltpu.HBM)


def flip(x, axis, size, mask):
    return lax.ppermute(x, axis, [(i, i ^ mask) for i in range(size)])


def dot(a, b, contract=((1,), (0,))):
    return lax.dot_general(a, b, (contract, ((), ())), preferred_element_type=jnp.float32)


def position():
    return lax.axis_index("dp"), lax.rem(lax.axis_index("seq"), CORES)


def quarter_of():
    return lax.rem(lax.axis_index("seq") // CORES, 4)


def cut_qkv(layout, w_qkv, *refs):
    outs, sem = refs[:-1], refs[-1]
    _, core = position()
    shard = w_qkv.shape[0]
    feat = w_qkv.shape[1] // 3
    copies = []
    for out, start in zip(outs, layout(shard)):
        rows = pl.ds(pl.multiple_of(start, 16), out.shape[0])
        for j in range(3):
            cols = pl.ds(pl.multiple_of(j * feat + core * HEAD, HEAD), HEAD)
            target = out.at[:, j * HEAD : (j + 1) * HEAD]
            copies.append(pltpu.make_async_copy(w_qkv.at[rows, cols], target, sem.at[len(copies)]))
            copies[-1].start()
    for copy in copies:
        copy.wait()


def cut_out(w_out, mine, theirs):
    _, core = position()
    for out, head in ((mine, core), (theirs, 1 - core)):
        out[...] = w_out[pl.ds(pl.multiple_of(head * HEAD, HEAD), HEAD), :]


def product(tok_a, tok_b, pieces, places):
    cols = [
        pl.ds(pl.multiple_of(place, 128), piece.shape[0]) for piece, place in zip(pieces, places)
    ]
    tok = jnp.concatenate(
        [jnp.concatenate([ref[:, c] for c in cols], axis=1) for ref in (tok_a, tok_b)], axis=0
    )
    weights = jnp.concatenate([piece[...] for piece in pieces], axis=0)
    return dot(tok, weights)


def places_near(shard, offsets):
    at = lax.axis_index("dp")
    return [(at ^ offset) * shard for offset in offsets]


def places_far(shard):
    start = places_near(shard, (3,))[0]
    mine = quarter_of()
    return [start + (mine ^ mask) * (shard // 4) for mask in range(4)]


def project(count, places, tok_a, tok_b, *refs):
    pieces, before, total = refs[:count], refs[count:-1], refs[-1]
    term = product(tok_a, tok_b, pieces, places())
    total[...] = before[0][...] + term if before else term


def project_attend(count, places, tok_a, tok_b, *refs):
    pieces, before = refs[:count], refs[count:-4]
    query_out, state_out, chip_out, intra_out = refs[-4:]
    proj = product(tok_a, tok_b, pieces, places())
    if before:
        proj = before[0][...] + proj
    rows = intra_out.shape[1]
    row = lax.broadcasted_iota(jnp.int32, (rows, rows), 0)
    col = lax.broadcasted_iota(jnp.int32, (rows, rows), 1)
    chip = None
    for b in range(CORES):
        part = proj[b * rows : (b + 1) * rows, :]
        act = part[:, : 2 * HEAD]
        act = (act / (1.0 + jnp.exp(-act))).astype(jnp.bfloat16)
        query, keys = act[:, :HEAD], act[:, HEAD:]
        values = part[:, 2 * HEAD :].astype(jnp.bfloat16)
        state = dot(keys, values, ((0,), (0,)))
        chip = state if chip is None else chip + state
        query_out[b] = query
        state_out[b] = state
        scores = dot(query, keys, ((1,), (1,)))
        scores = jnp.where(row >= col, scores, 0.0).astype(jnp.bfloat16)
        intra_out[b] = dot(scores, values)
    chip_out[...] = chip.astype(jnp.bfloat16)


def normalise(steps, query, state, intra, gain, *refs):
    got, (own_out, other_out) = refs[:steps], refs[steps:]
    _, core = position()
    chip_at = lax.axis_index("seq") // CORES
    base = jnp.zeros((HEAD, HEAD), jnp.float32)
    for step, ref in enumerate(got):
        base = base + jnp.where((chip_at >> step) % 2 == 1, ref[...].astype(jnp.float32), 0.0)
    odd = core == 1
    own_prefix = jnp.where(odd, base + state[1], base)
    other_prefix = jnp.where(odd, base, base + state[0])
    scale = gain[pl.ds(core, 1), :]
    for b, (prefix, out) in enumerate(((own_prefix, own_out), (other_prefix, other_out))):
        attended = dot(query[b], prefix.astype(jnp.bfloat16)) + intra[b]
        meansq = jnp.mean(attended * attended, axis=-1, keepdims=True)
        out[...] = (attended * lax.rsqrt(meansq + 1e-06) * scale).astype(jnp.bfloat16)


def mix(count, places, own, other, *refs):
    mine, theirs, (out, stage, sem) = refs[:count], refs[count : 2 * count], refs[2 * count :]
    normed = jnp.concatenate([own[...], other[...]], axis=1)
    copies = []
    slot = 0
    for my_rows, their_rows, place in zip(mine, theirs, places()):
        width = my_rows.shape[1]
        step = min(width, 512)
        for at_col in range(0, width, step):
            part = slice(at_col, at_col + step)
            weights = jnp.concatenate([my_rows[:, part], their_rows[:, part]], axis=0)
            here = stage.at[:, slot : slot + step]
            here[...] = dot(normed, weights).astype(jnp.bfloat16)
            cols = pl.ds(pl.multiple_of(place + at_col, 128), step)
            copies.append(pltpu.make_async_copy(here, out.at[:, cols], sem.at[len(copies)]))
            copies[-1].start()
            slot += step
    for copy in copies:
        copy.wait()


def places_out(width):
    at = lax.axis_index("dp")
    return [(at ^ offset) * width for offset in range(4)]


def shards(n, blocks, tokens, w_qkv, norm_gain, w_out):
    tok_own = tokens[0]
    rows, depth = tok_own.shape
    shard = w_qkv.shape[0]
    heads = norm_gain.shape[0] // HEAD
    bf16, f32 = jnp.bfloat16, jnp.float32

    def call(kernel, outs, ins, out_specs, in_specs, scratch=(), flops=0, moved=0, limit=VMEM_LIMIT):
        return pl.pallas_call(
            kernel,
            out_shape=outs,
            in_specs=in_specs,
            out_specs=out_specs,
            scratch_shapes=scratch,
            compiler_params=pltpu.CompilerParams(vmem_limit_bytes=limit),
            cost_estimate=pl.CostEstimate(flops=flops, bytes_accessed=moved, transcendentals=0),
        )(*ins)

    def array(shape, kind):
        return jax.ShapeDtypeStruct(shape, kind)

    def add_product(pieces, places, total=None):
        extra = [] if total is None else [total]
        return call(
            functools.partial(project, len(pieces), places),
            array((CORES * rows, 3 * HEAD), f32),
            [tok_own, tok_other, *pieces, *extra],
            VMEM, [VMEM] * (2 + len(pieces) + len(extra)),
            flops=rows * HEAD * (1 if total is not None else 1000000),
        )

    tok_other = flip(tok_own, "seq", blocks, 1)
    width = w_out.shape[1]
    grid = n == 4 and blocks % (4 * CORES) == 0 and shard % 512 == 0 and width % 256 == 0

    def cut(layout, *sizes):
        return call(
            functools.partial(cut_qkv, layout),
            [array((size, 3 * HEAD), bf16) for size in sizes],
            [w_qkv], [VMEM] * len(sizes), [HBM],
            scratch=[pltpu.SemaphoreType.DMA((3 * len(sizes),))], limit=CUT_LIMIT,
        )

    out_cut = functools.partial(
        call, cut_out, [array((HEAD, width), bf16)] * 2, [w_out], [VMEM] * 2, [VMEM]
    )
    total = None
    if grid:
        quarter = shard // 4
        own, part = cut(lambda shard: [0, quarter_of() * quarter], shard, quarter)
        far = [flip(part, "dp", n, 3)]
        from_x = flip(own, "dp", n, 1)
        from_y = flip(own, "dp", n, 2)
        far += [flip(far[0], "seq", blocks, CORES * mask) for mask in (1, 2, 3)]
        here, own = lax.optimization_barrier((far[0], own))
        total = add_product([own], functools.partial(places_near, shard, (0,)))
        own_mine, own_theirs = out_cut()
        sent = own_mine
        outs = []
        for i, mask in enumerate((1, 2, 3)):
            sent, far[1 + i], total = lax.optimization_barrier((sent, far[1 + i], total))
            outs.append(flip(sent, "dp", n, mask))
        out_x, out_y, out_d = outs
        total = add_product(far, functools.partial(places_far, shard), total)
        pieces, places = [from_x, from_y], functools.partial(places_near, shard, (1, 2))
    else:
        whole = cut(lambda shard: [0], shard)[0]
        pieces, places = [lax.all_gather(whole, "dp", axis=0, tiled=True)], lambda: [0]
    extra = [] if total is None else [total]

    query, state, chip, intra = call(
        functools.partial(project_attend, len(pieces), places),
        [
            array((CORES, rows, HEAD), bf16),
            array((CORES, HEAD, HEAD), f32),
            array((HEAD, HEAD), bf16),
            array((CORES, rows, HEAD), f32),
        ],
        [tok_own, tok_other, *pieces, *extra],
        [VMEM] * 4, [VMEM] * (2 + len(pieces) + len(extra)),
        flops=2 * CORES * rows * sum(piece.shape[0] for piece in pieces) * 3 * HEAD,
    )

    got, group = [], chip
    for step in range((blocks // CORES).bit_length() - 1):
        if got:
            group = (group.astype(f32) + got[-1].astype(f32)).astype(bf16)
            if grid:
                group, out_x, out_y = lax.optimization_barrier((group, out_x, out_y))
        got.append(flip(group, "seq", blocks, CORES << step))
    if grid:
        their_x = flip(out_x, "seq", blocks, 1)
        their_y = flip(out_y, "seq", blocks, 1)
    normed_own, normed_other = call(
        functools.partial(normalise, len(got)),
        [array((rows, HEAD), bf16)] * 2,
        [query, state, intra, norm_gain.reshape(heads, HEAD), *got],
        [VMEM] * 2, [VMEM] * (4 + len(got)),
    )
    normed_got = flip(normed_other, "seq", blocks, 1)

    if grid:
        out_d, normed_other = lax.optimization_barrier((out_d, normed_other))
        their_d = flip(out_d, "seq", blocks, 1)
        mine = [own_mine, out_x, out_y, out_d]
        theirs = [own_theirs, their_x, their_y, their_d]
        places = functools.partial(places_out, width)
    else:
        mine = [lax.all_gather(out_cut()[0], "dp", axis=1, tiled=True)]
        theirs = [flip(mine[0], "seq", blocks, 1)]
        places = lambda: [0]
    mixed = call(
        functools.partial(mix, len(mine), places),
        array((rows, n * width), bf16),
        [normed_own, normed_got, *mine, *theirs],
        HBM, [VMEM] * (2 + 2 * len(mine)),
        scratch=[pltpu.VMEM((rows, n * width), bf16), pltpu.SemaphoreType.DMA((16,))],
        flops=2 * rows * 2 * HEAD * n * width, moved=2 * rows * n * width,
    )
    return mixed[None]


def solution(mesh):
    n, blocks = mesh.shape["dp"], mesh.shape["seq"]
    return jax.shard_map(
        functools.partial(shards, n, blocks),
        mesh=mesh,
        in_specs=(P("dp", "seq", None), P("dp", None), P(), P(None, "dp")),
        out_specs=P("dp", "seq", None),
        check_vma=False,
    )
```

```python
import functools

import jax
import jax.numpy as jnp
from jax import lax
from jax.experimental import pallas as pl
from jax.experimental.pallas import tpu as pltpu
from jax.sharding import PartitionSpec as P

HEAD = 128
CORES = 2
VMEM_LIMIT = 24 * 1024 * 1024
CUT_LIMIT = 52 * 1024 * 1024
VMEM = pl.BlockSpec(memory_space=pltpu.VMEM)
HBM = pl.BlockSpec(memory_space=pltpu.HBM)


def flip(x, axis, size, mask):
    return lax.ppermute(x, axis, [(i, i ^ mask) for i in range(size)])


def dot(a, b, contract=((1,), (0,))):
    return lax.dot_general(a, b, (contract, ((), ())), preferred_element_type=jnp.float32)


def position():
    return lax.axis_index("dp"), lax.rem(lax.axis_index("seq"), CORES)


def quarter_of():
    return lax.rem(lax.axis_index("seq") // CORES, 4)


def cut_qkv(layout, w_qkv, *refs):
    outs, sem = refs[:-1], refs[-1]
    _, core = position()
    shard = w_qkv.shape[0]
    feat = w_qkv.shape[1] // 3
    copies = []
    for out, start in zip(outs, layout(shard)):
        rows = pl.ds(pl.multiple_of(start, 16), out.shape[0])
        for j in range(3):
            cols = pl.ds(pl.multiple_of(j * feat + core * HEAD, HEAD), HEAD)
            target = out.at[:, j * HEAD : (j + 1) * HEAD]
            copies.append(pltpu.make_async_copy(w_qkv.at[rows, cols], target, sem.at[len(copies)]))
            copies[-1].start()
    for copy in copies:
        copy.wait()


def cut_out(w_out, mine, theirs):
    _, core = position()
    for out, head in ((mine, core), (theirs, 1 - core)):
        out[...] = w_out[pl.ds(pl.multiple_of(head * HEAD, HEAD), HEAD), :]


def product(tok_a, tok_b, pieces, places):
    cols = [
        pl.ds(pl.multiple_of(place, 128), piece.shape[0]) for piece, place in zip(pieces, places)
    ]
    tok = jnp.concatenate(
        [jnp.concatenate([ref[:, c] for c in cols], axis=1) for ref in (tok_a, tok_b)], axis=0
    )
    weights = jnp.concatenate([piece[...] for piece in pieces], axis=0)
    return dot(tok, weights)


def places_near(shard, offsets):
    at = lax.axis_index("dp")
    return [(at ^ offset) * shard for offset in offsets]


def places_far(shard):
    start = places_near(shard, (3,))[0]
    mine = quarter_of()
    return [start + (mine ^ mask) * (shard // 4) for mask in (0, 2, 1, 3)]


def project(count, places, tok_a, tok_b, *refs):
    pieces, before, total = refs[:count], refs[count:-1], refs[-1]
    term = product(tok_a, tok_b, pieces, places())
    total[...] = before[0][...] + term if before else term


def project_attend(count, places, tok_a, tok_b, *refs):
    pieces, before = refs[:count], refs[count:-4]
    query_out, state_out, chip_out, intra_out = refs[-4:]
    proj = product(tok_a, tok_b, pieces, places())
    if before:
        proj = before[0][...] + proj
    rows = intra_out.shape[1]
    row = lax.broadcasted_iota(jnp.int32, (rows, rows), 0)
    col = lax.broadcasted_iota(jnp.int32, (rows, rows), 1)
    chip = None
    for b in range(CORES):
        part = proj[b * rows : (b + 1) * rows, :]
        act = part[:, : 2 * HEAD]
        act = (act / (1.0 + jnp.exp(-act))).astype(jnp.bfloat16)
        query, keys = act[:, :HEAD], act[:, HEAD:]
        values = part[:, 2 * HEAD :].astype(jnp.bfloat16)
        state = dot(keys, values, ((0,), (0,)))
        chip = state if chip is None else chip + state
        query_out[b] = query
        state_out[b] = state
        scores = dot(query, keys, ((1,), (1,)))
        scores = jnp.where(row >= col, scores, 0.0).astype(jnp.bfloat16)
        intra_out[b] = dot(scores, values)
    chip_out[...] = chip.astype(jnp.bfloat16)


def normalise(steps, query, state, intra, gain, *refs):
    got, (own_out, other_out) = refs[:steps], refs[steps:]
    _, core = position()
    chip_at = lax.axis_index("seq") // CORES
    base = jnp.zeros((HEAD, HEAD), jnp.float32)
    for step, ref in enumerate(got):
        base = base + jnp.where((chip_at >> step) % 2 == 1, ref[...].astype(jnp.float32), 0.0)
    odd = core == 1
    own_prefix = jnp.where(odd, base + state[1], base)
    other_prefix = jnp.where(odd, base, base + state[0])
    scale = gain[pl.ds(core, 1), :]
    for b, (prefix, out) in enumerate(((own_prefix, own_out), (other_prefix, other_out))):
        attended = dot(query[b], prefix.astype(jnp.bfloat16)) + intra[b]
        meansq = jnp.mean(attended * attended, axis=-1, keepdims=True)
        out[...] = (attended * lax.rsqrt(meansq + 1e-06) * scale).astype(jnp.bfloat16)


def mix(count, places, own, other, *refs):
    mine, theirs, (out, stage, sem) = refs[:count], refs[count : 2 * count], refs[2 * count :]
    normed = jnp.concatenate([own[...], other[...]], axis=1)
    copies = []
    slot = 0
    for my_rows, their_rows, place in zip(mine, theirs, places()):
        width = my_rows.shape[1]
        step = min(width, 512)
        for at_col in range(0, width, step):
            part = slice(at_col, at_col + step)
            weights = jnp.concatenate([my_rows[:, part], their_rows[:, part]], axis=0)
            here = stage.at[:, slot : slot + step]
            here[...] = dot(normed, weights).astype(jnp.bfloat16)
            cols = pl.ds(pl.multiple_of(place + at_col, 128), step)
            copies.append(pltpu.make_async_copy(here, out.at[:, cols], sem.at[len(copies)]))
            copies[-1].start()
            slot += step
    for copy in copies:
        copy.wait()


def places_out(width):
    at = lax.axis_index("dp")
    return [(at ^ offset) * width for offset in range(4)]


def shards(n, blocks, tokens, w_qkv, norm_gain, w_out):
    tok_own = tokens[0]
    rows, depth = tok_own.shape
    shard = w_qkv.shape[0]
    heads = norm_gain.shape[0] // HEAD
    bf16, f32 = jnp.bfloat16, jnp.float32

    def call(kernel, outs, ins, out_specs, in_specs, scratch=(), flops=0, moved=0, limit=VMEM_LIMIT):
        return pl.pallas_call(
            kernel,
            out_shape=outs,
            in_specs=in_specs,
            out_specs=out_specs,
            scratch_shapes=scratch,
            compiler_params=pltpu.CompilerParams(vmem_limit_bytes=limit),
            cost_estimate=pl.CostEstimate(flops=flops, bytes_accessed=moved, transcendentals=0),
        )(*ins)

    def array(shape, kind):
        return jax.ShapeDtypeStruct(shape, kind)

    def add_product(pieces, places, total=None):
        extra = [] if total is None else [total]
        return call(
            functools.partial(project, len(pieces), places),
            array((CORES * rows, 3 * HEAD), f32),
            [tok_own, tok_other, *pieces, *extra],
            VMEM, [VMEM] * (2 + len(pieces) + len(extra)),
            flops=rows * HEAD * (1 if total is not None else 1000000),
        )

    tok_other = flip(tok_own, "seq", blocks, 1)
    width = w_out.shape[1]
    grid = n == 4 and blocks % (4 * CORES) == 0 and shard % 512 == 0 and width % 256 == 0

    def cut(layout, *sizes):
        return call(
            functools.partial(cut_qkv, layout),
            [array((size, 3 * HEAD), bf16) for size in sizes],
            [w_qkv], [VMEM] * len(sizes), [HBM],
            scratch=[pltpu.SemaphoreType.DMA((3 * len(sizes),))], limit=CUT_LIMIT,
        )

    out_cut = functools.partial(
        call, cut_out, [array((HEAD, width), bf16)] * 2, [w_out], [VMEM] * 2, [VMEM]
    )
    total = None
    if grid:
        quarter = shard // 4
        own, part = cut(lambda shard: [0, quarter_of() * quarter], shard, quarter)
        far = [flip(part, "dp", n, 3)]
        from_x = flip(own, "dp", n, 1)
        from_y = flip(own, "dp", n, 2)
        far.append(flip(far[0], "seq", blocks, CORES * 2))
        far.append(flip(far[0], "seq", blocks, CORES))
        here, own = lax.optimization_barrier((far[0], own))
        total = add_product([own], functools.partial(places_near, shard, (0,)))
        passed, total = lax.optimization_barrier((far[1], total))
        far.append(flip(passed, "seq", blocks, CORES))
        own_mine, own_theirs = out_cut()
        sent = own_mine
        outs = []
        for i, mask in enumerate((3, 1, 2)):
            sent, far[1 + i], total = lax.optimization_barrier((sent, far[1 + i], total))
            outs.append(flip(sent, "dp", n, mask))
        out_d, out_x, out_y = outs
        total = add_product(far, functools.partial(places_far, shard), total)
        pieces, places = [from_x, from_y], functools.partial(places_near, shard, (1, 2))
    else:
        whole = cut(lambda shard: [0], shard)[0]
        pieces, places = [lax.all_gather(whole, "dp", axis=0, tiled=True)], lambda: [0]
    extra = [] if total is None else [total]

    query, state, chip, intra = call(
        functools.partial(project_attend, len(pieces), places),
        [
            array((CORES, rows, HEAD), bf16),
            array((CORES, HEAD, HEAD), f32),
            array((HEAD, HEAD), bf16),
            array((CORES, rows, HEAD), f32),
        ],
        [tok_own, tok_other, *pieces, *extra],
        [VMEM] * 4, [VMEM] * (2 + len(pieces) + len(extra)),
        flops=2 * CORES * rows * sum(piece.shape[0] for piece in pieces) * 3 * HEAD,
    )

    got, group = [], chip
    for step in range((blocks // CORES).bit_length() - 1):
        if got:
            group = (group.astype(f32) + got[-1].astype(f32)).astype(bf16)
            if grid:
                group, out_x, out_d = lax.optimization_barrier((group, out_x, out_d))
        got.append(flip(group, "seq", blocks, CORES << step))
    if grid:
        their_x = flip(out_x, "seq", blocks, 1)
        their_d = flip(out_d, "seq", blocks, 1)
    normed_own, normed_other = call(
        functools.partial(normalise, len(got)),
        [array((rows, HEAD), bf16)] * 2,
        [query, state, intra, norm_gain.reshape(heads, HEAD), *got],
        [VMEM] * 2, [VMEM] * (4 + len(got)),
    )
    normed_got = flip(normed_other, "seq", blocks, 1)

    if grid:
        out_y, normed_other = lax.optimization_barrier((out_y, normed_other))
        their_y = flip(out_y, "seq", blocks, 1)
        mine = [own_mine, out_x, out_y, out_d]
        theirs = [own_theirs, their_x, their_y, their_d]
        places = functools.partial(places_out, width)
    else:
        mine = [lax.all_gather(out_cut()[0], "dp", axis=1, tiled=True)]
        theirs = [flip(mine[0], "seq", blocks, 1)]
        places = lambda: [0]
    mixed = call(
        functools.partial(mix, len(mine), places),
        array((rows, n * width), bf16),
        [normed_own, normed_got, *mine, *theirs],
        HBM, [VMEM] * (2 + 2 * len(mine)),
        scratch=[pltpu.VMEM((rows, n * width), bf16), pltpu.SemaphoreType.DMA((16,))],
        flops=2 * rows * 2 * HEAD * n * width, moved=2 * rows * n * width,
    )
    return mixed[None]


def solution(mesh):
    n, blocks = mesh.shape["dp"], mesh.shape["seq"]
    return jax.shard_map(
        functools.partial(shards, n, blocks),
        mesh=mesh,
        in_specs=(P("dp", "seq", None), P("dp", None), P(), P(None, "dp")),
        out_specs=P("dp", "seq", None),
        check_vma=False,
    )
```

```python
import functools

import jax
import jax.numpy as jnp
from jax import lax
from jax.experimental import pallas as pl
from jax.experimental.pallas import tpu as pltpu
from jax.sharding import PartitionSpec as P

HEAD = 128
CORES = 2
VMEM_LIMIT = 24 * 1024 * 1024
CUT_LIMIT = 52 * 1024 * 1024
VMEM = pl.BlockSpec(memory_space=pltpu.VMEM)
HBM = pl.BlockSpec(memory_space=pltpu.HBM)


def flip(x, axis, size, mask):
    return lax.ppermute(x, axis, [(i, i ^ mask) for i in range(size)])


def dot(a, b, contract=((1,), (0,))):
    return lax.dot_general(a, b, (contract, ((), ())), preferred_element_type=jnp.float32)


def position():
    return lax.axis_index("dp"), lax.rem(lax.axis_index("seq"), CORES)


def quarter_of():
    return lax.rem(lax.axis_index("seq") // CORES, 4)


def cut_qkv(layout, w_qkv, *refs):
    outs, sem = refs[:-1], refs[-1]
    _, core = position()
    shard = w_qkv.shape[0]
    feat = w_qkv.shape[1] // 3
    copies = []
    for out, start in zip(outs, layout(shard)):
        rows = pl.ds(pl.multiple_of(start, 16), out.shape[0])
        for j in range(3):
            cols = pl.ds(pl.multiple_of(j * feat + core * HEAD, HEAD), HEAD)
            target = out.at[:, j * HEAD : (j + 1) * HEAD]
            copies.append(pltpu.make_async_copy(w_qkv.at[rows, cols], target, sem.at[len(copies)]))
            copies[-1].start()
    for copy in copies:
        copy.wait()


def cut_out(w_out, mine, theirs):
    _, core = position()
    for out, head in ((mine, core), (theirs, 1 - core)):
        out[...] = w_out[pl.ds(pl.multiple_of(head * HEAD, HEAD), HEAD), :]


def product(tok_a, tok_b, pieces, places):
    cols = [
        pl.ds(pl.multiple_of(place, 128), piece.shape[0]) for piece, place in zip(pieces, places)
    ]
    tok = jnp.concatenate(
        [jnp.concatenate([ref[:, c] for c in cols], axis=1) for ref in (tok_a, tok_b)], axis=0
    )
    weights = jnp.concatenate([piece[...] for piece in pieces], axis=0)
    return dot(tok, weights)


def places_near(shard, offsets):
    at = lax.axis_index("dp")
    return [(at ^ offset) * shard for offset in offsets]


def places_far(shard):
    start = places_near(shard, (3,))[0]
    mine = quarter_of()
    return [start + (mine ^ mask) * (shard // 4) for mask in (0, 2, 1, 3)]


def project(count, places, tok_a, tok_b, *refs):
    pieces, before, total = refs[:count], refs[count:-1], refs[-1]
    term = product(tok_a, tok_b, pieces, places())
    total[...] = before[0][...] + term if before else term


def project_attend(count, places, tok_a, tok_b, *refs):
    pieces, before = refs[:count], refs[count:-4]
    query_out, state_out, chip_out, intra_out = refs[-4:]
    proj = product(tok_a, tok_b, pieces, places())
    if before:
        proj = before[0][...] + proj
    rows = intra_out.shape[1]
    row = lax.broadcasted_iota(jnp.int32, (rows, rows), 0)
    col = lax.broadcasted_iota(jnp.int32, (rows, rows), 1)
    chip = None
    for b in range(CORES):
        part = proj[b * rows : (b + 1) * rows, :]
        act = part[:, : 2 * HEAD]
        act = (act / (1.0 + jnp.exp(-act))).astype(jnp.bfloat16)
        query, keys = act[:, :HEAD], act[:, HEAD:]
        values = part[:, 2 * HEAD :].astype(jnp.bfloat16)
        state = dot(keys, values, ((0,), (0,)))
        chip = state if chip is None else chip + state
        query_out[b] = query
        state_out[b] = state
        scores = dot(query, keys, ((1,), (1,)))
        scores = jnp.where(row >= col, scores, 0.0).astype(jnp.bfloat16)
        intra_out[b] = dot(scores, values)
    chip_out[...] = chip.astype(jnp.bfloat16)


def normalise(steps, query, state, intra, gain, *refs):
    got, (own_out, other_out) = refs[:steps], refs[steps:]
    _, core = position()
    chip_at = lax.axis_index("seq") // CORES
    base = jnp.zeros((HEAD, HEAD), jnp.float32)
    for step, ref in enumerate(got):
        base = base + jnp.where((chip_at >> step) % 2 == 1, ref[...].astype(jnp.float32), 0.0)
    odd = core == 1
    own_prefix = jnp.where(odd, base + state[1], base)
    other_prefix = jnp.where(odd, base, base + state[0])
    scale = gain[pl.ds(core, 1), :]
    for b, (prefix, out) in enumerate(((own_prefix, own_out), (other_prefix, other_out))):
        attended = dot(query[b], prefix.astype(jnp.bfloat16)) + intra[b]
        meansq = jnp.mean(attended * attended, axis=-1, keepdims=True)
        out[...] = (attended * lax.rsqrt(meansq + 1e-06) * scale).astype(jnp.bfloat16)


def mix(count, places, own, other, *refs):
    mine, theirs, (out, stage, sem) = refs[:count], refs[count : 2 * count], refs[2 * count :]
    normed = jnp.concatenate([own[...], other[...]], axis=1)
    copies = []
    slot = 0
    for my_rows, their_rows, place in zip(mine, theirs, places()):
        width = my_rows.shape[1]
        step = min(width, 512)
        for at_col in range(0, width, step):
            part = slice(at_col, at_col + step)
            weights = jnp.concatenate([my_rows[:, part], their_rows[:, part]], axis=0)
            here = stage.at[:, slot : slot + step]
            here[...] = dot(normed, weights).astype(jnp.bfloat16)
            cols = pl.ds(pl.multiple_of(place + at_col, 128), step)
            copies.append(pltpu.make_async_copy(here, out.at[:, cols], sem.at[len(copies)]))
            copies[-1].start()
            slot += step
    for copy in copies:
        copy.wait()


def places_out(width):
    at = lax.axis_index("dp")
    return [(at ^ offset) * width for offset in range(4)]


def shards(n, blocks, tokens, w_qkv, norm_gain, w_out):
    tok_own = tokens[0]
    rows, depth = tok_own.shape
    shard = w_qkv.shape[0]
    heads = norm_gain.shape[0] // HEAD
    bf16, f32 = jnp.bfloat16, jnp.float32

    def call(kernel, outs, ins, out_specs, in_specs, scratch=(), flops=0, moved=0, limit=VMEM_LIMIT):
        return pl.pallas_call(
            kernel,
            out_shape=outs,
            in_specs=in_specs,
            out_specs=out_specs,
            scratch_shapes=scratch,
            compiler_params=pltpu.CompilerParams(vmem_limit_bytes=limit),
            cost_estimate=pl.CostEstimate(flops=flops, bytes_accessed=moved, transcendentals=0),
        )(*ins)

    def array(shape, kind):
        return jax.ShapeDtypeStruct(shape, kind)

    def add_product(pieces, places, total=None):
        extra = [] if total is None else [total]
        return call(
            functools.partial(project, len(pieces), places),
            array((CORES * rows, 3 * HEAD), f32),
            [tok_own, tok_other, *pieces, *extra],
            VMEM, [VMEM] * (2 + len(pieces) + len(extra)),
            flops=rows * HEAD * (1 if total is not None else 1000000),
        )

    tok_other = flip(tok_own, "seq", blocks, 1)
    width = w_out.shape[1]
    grid = n == 4 and blocks % (4 * CORES) == 0 and shard % 512 == 0 and width % 256 == 0

    def cut(layout, *sizes):
        return call(
            functools.partial(cut_qkv, layout),
            [array((size, 3 * HEAD), bf16) for size in sizes],
            [w_qkv], [VMEM] * len(sizes), [HBM],
            scratch=[pltpu.SemaphoreType.DMA((3 * len(sizes),))], limit=CUT_LIMIT,
        )

    out_cut = functools.partial(
        call, cut_out, [array((HEAD, width), bf16)] * 2, [w_out], [VMEM] * 2, [VMEM]
    )
    total = None
    if grid:
        quarter = shard // 4
        own, part = cut(lambda shard: [0, quarter_of() * quarter], shard, quarter)
        far = [flip(part, "dp", n, 3)]
        from_x = flip(own, "dp", n, 1)
        from_y = flip(own, "dp", n, 2)
        far.append(flip(far[0], "seq", blocks, CORES * 2))
        far.append(flip(far[0], "seq", blocks, CORES))
        here, own = lax.optimization_barrier((far[0], own))
        total = add_product([own], functools.partial(places_near, shard, (0,)))
        passed, total = lax.optimization_barrier((far[1], total))
        far.append(flip(passed, "seq", blocks, CORES))
        own_mine, own_theirs = out_cut()
        sent = own_mine
        outs = []
        for i, mask in enumerate((1, 2, 3)):
            sent, far[1 + i], total = lax.optimization_barrier((sent, far[1 + i], total))
            outs.append(flip(sent, "dp", n, mask))
        out_x, out_y, out_d = outs
        total = add_product(far, functools.partial(places_far, shard), total)
        pieces, places = [from_x, from_y], functools.partial(places_near, shard, (1, 2))
    else:
        whole = cut(lambda shard: [0], shard)[0]
        pieces, places = [lax.all_gather(whole, "dp", axis=0, tiled=True)], lambda: [0]
    extra = [] if total is None else [total]

    query, state, chip, intra = call(
        functools.partial(project_attend, len(pieces), places),
        [
            array((CORES, rows, HEAD), bf16),
            array((CORES, HEAD, HEAD), f32),
            array((HEAD, HEAD), bf16),
            array((CORES, rows, HEAD), f32),
        ],
        [tok_own, tok_other, *pieces, *extra],
        [VMEM] * 4, [VMEM] * (2 + len(pieces) + len(extra)),
        flops=2 * CORES * rows * sum(piece.shape[0] for piece in pieces) * 3 * HEAD,
    )

    got, group = [], chip
    for step in range((blocks // CORES).bit_length() - 1):
        if got:
            group = (group.astype(f32) + got[-1].astype(f32)).astype(bf16)
            if grid:
                group, out_x, out_y = lax.optimization_barrier((group, out_x, out_y))
        got.append(flip(group, "seq", blocks, CORES << step))
    if grid:
        their_x = flip(out_x, "seq", blocks, 1)
        their_y = flip(out_y, "seq", blocks, 1)
    normed_own, normed_other = call(
        functools.partial(normalise, len(got)),
        [array((rows, HEAD), bf16)] * 2,
        [query, state, intra, norm_gain.reshape(heads, HEAD), *got],
        [VMEM] * 2, [VMEM] * (4 + len(got)),
    )
    normed_got = flip(normed_other, "seq", blocks, 1)

    if grid:
        out_d, normed_other = lax.optimization_barrier((out_d, normed_other))
        their_d = flip(out_d, "seq", blocks, 1)
        mine = [own_mine, out_x, out_y, out_d]
        theirs = [own_theirs, their_x, their_y, their_d]
        places = functools.partial(places_out, width)
    else:
        mine = [lax.all_gather(out_cut()[0], "dp", axis=1, tiled=True)]
        theirs = [flip(mine[0], "seq", blocks, 1)]
        places = lambda: [0]
    mixed = call(
        functools.partial(mix, len(mine), places),
        array((rows, n * width), bf16),
        [normed_own, normed_got, *mine, *theirs],
        HBM, [VMEM] * (2 + 2 * len(mine)),
        scratch=[pltpu.VMEM((rows, n * width), bf16), pltpu.SemaphoreType.DMA((16,))],
        flops=2 * rows * 2 * HEAD * n * width, moved=2 * rows * n * width,
    )
    return mixed[None]


def solution(mesh):
    n, blocks = mesh.shape["dp"], mesh.shape["seq"]
    return jax.shard_map(
        functools.partial(shards, n, blocks),
        mesh=mesh,
        in_specs=(P("dp", "seq", None), P("dp", None), P(), P(None, "dp")),
        out_specs=P("dp", "seq", None),
        check_vma=False,
    )
```

```python
import functools

import jax
import jax.numpy as jnp
from jax import lax
from jax.experimental import pallas as pl
from jax.experimental.pallas import tpu as pltpu
from jax.sharding import PartitionSpec as P

HEAD = 128
CORES = 2
VMEM_LIMIT = 24 * 1024 * 1024
CUT_LIMIT = 52 * 1024 * 1024
VMEM = pl.BlockSpec(memory_space=pltpu.VMEM)
HBM = pl.BlockSpec(memory_space=pltpu.HBM)


def flip(x, axis, size, mask):
    return lax.ppermute(x, axis, [(i, i ^ mask) for i in range(size)])


def dot(a, b, contract=((1,), (0,))):
    return lax.dot_general(a, b, (contract, ((), ())), preferred_element_type=jnp.float32)


def position():
    return lax.axis_index("dp"), lax.rem(lax.axis_index("seq"), CORES)


def quarter_of():
    return lax.rem(lax.axis_index("seq") // CORES, 4)


def cut_qkv(layout, w_qkv, *refs):
    outs, sem = refs[:-1], refs[-1]
    _, core = position()
    shard = w_qkv.shape[0]
    feat = w_qkv.shape[1] // 3
    copies = []
    for out, start in zip(outs, layout(shard)):
        rows = pl.ds(pl.multiple_of(start, 16), out.shape[0])
        for j in range(3):
            cols = pl.ds(pl.multiple_of(j * feat + core * HEAD, HEAD), HEAD)
            target = out.at[:, j * HEAD : (j + 1) * HEAD]
            copies.append(pltpu.make_async_copy(w_qkv.at[rows, cols], target, sem.at[len(copies)]))
            copies[-1].start()
    for copy in copies:
        copy.wait()


def cut_out(w_out, mine, theirs):
    _, core = position()
    for out, head in ((mine, core), (theirs, 1 - core)):
        out[...] = w_out[pl.ds(pl.multiple_of(head * HEAD, HEAD), HEAD), :]


def product(tok_a, tok_b, pieces, places):
    cols = [
        pl.ds(pl.multiple_of(place, 128), piece.shape[0]) for piece, place in zip(pieces, places)
    ]
    tok = jnp.concatenate(
        [jnp.concatenate([ref[:, c] for c in cols], axis=1) for ref in (tok_a, tok_b)], axis=0
    )
    weights = jnp.concatenate([piece[...] for piece in pieces], axis=0)
    return dot(tok, weights)


def places_near(shard, offsets):
    at = lax.axis_index("dp")
    return [(at ^ offset) * shard for offset in offsets]


def places_far(shard):
    start = places_near(shard, (3,))[0]
    mine = quarter_of()
    return [start + (mine ^ mask) * (shard // 4) for mask in (0, 2, 1, 3)]


def project(count, places, tok_a, tok_b, *refs):
    pieces, before, total = refs[:count], refs[count:-1], refs[-1]
    term = product(tok_a, tok_b, pieces, places())
    total[...] = before[0][...] + term if before else term


def project_attend(count, places, tok_a, tok_b, *refs):
    pieces, before = refs[:count], refs[count:-4]
    query_out, state_out, chip_out, intra_out = refs[-4:]
    proj = product(tok_a, tok_b, pieces, places())
    if before:
        proj = before[0][...] + proj
    rows = intra_out.shape[1]
    row = lax.broadcasted_iota(jnp.int32, (rows, rows), 0)
    col = lax.broadcasted_iota(jnp.int32, (rows, rows), 1)
    chip = None
    for b in range(CORES):
        part = proj[b * rows : (b + 1) * rows, :]
        act = part[:, : 2 * HEAD]
        act = (act / (1.0 + jnp.exp(-act))).astype(jnp.bfloat16)
        query, keys = act[:, :HEAD], act[:, HEAD:]
        values = part[:, 2 * HEAD :].astype(jnp.bfloat16)
        state = dot(keys, values, ((0,), (0,)))
        chip = state if chip is None else chip + state
        query_out[b] = query
        state_out[b] = state
        scores = dot(query, keys, ((1,), (1,)))
        scores = jnp.where(row >= col, scores, 0.0).astype(jnp.bfloat16)
        intra_out[b] = dot(scores, values)
    for i in range(chip_out.shape[0]):
        chip_out[i] = chip.astype(jnp.bfloat16)


def normalise(query, state, intra, gain, got, own_out, other_out):
    _, core = position()
    chip_at = lax.axis_index("seq") // CORES
    base = jnp.zeros((HEAD, HEAD), jnp.float32)
    for i in range(got.shape[0]):
        base = base + jnp.where(i < chip_at, got[i].astype(jnp.float32), 0.0)
    odd = core == 1
    own_prefix = jnp.where(odd, base + state[1], base)
    other_prefix = jnp.where(odd, base, base + state[0])
    scale = gain[pl.ds(core, 1), :]
    for b, (prefix, out) in enumerate(((own_prefix, own_out), (other_prefix, other_out))):
        attended = dot(query[b], prefix.astype(jnp.bfloat16)) + intra[b]
        meansq = jnp.mean(attended * attended, axis=-1, keepdims=True)
        out[...] = (attended * lax.rsqrt(meansq + 1e-06) * scale).astype(jnp.bfloat16)


def mix(count, places, own, other, *refs):
    mine, theirs, (out, stage, sem) = refs[:count], refs[count : 2 * count], refs[2 * count :]
    normed = jnp.concatenate([own[...], other[...]], axis=1)
    copies = []
    slot = 0
    for my_rows, their_rows, place in zip(mine, theirs, places()):
        width = my_rows.shape[1]
        step = min(width, 512)
        for at_col in range(0, width, step):
            part = slice(at_col, at_col + step)
            weights = jnp.concatenate([my_rows[:, part], their_rows[:, part]], axis=0)
            here = stage.at[:, slot : slot + step]
            here[...] = dot(normed, weights).astype(jnp.bfloat16)
            cols = pl.ds(pl.multiple_of(place + at_col, 128), step)
            copies.append(pltpu.make_async_copy(here, out.at[:, cols], sem.at[len(copies)]))
            copies[-1].start()
            slot += step
    for copy in copies:
        copy.wait()


def places_out(width):
    at = lax.axis_index("dp")
    return [(at ^ offset) * width for offset in range(4)]


def shards(n, blocks, tokens, w_qkv, norm_gain, w_out):
    tok_own = tokens[0]
    rows, depth = tok_own.shape
    shard = w_qkv.shape[0]
    heads = norm_gain.shape[0] // HEAD
    bf16, f32 = jnp.bfloat16, jnp.float32

    def call(kernel, outs, ins, out_specs, in_specs, scratch=(), flops=0, moved=0, limit=VMEM_LIMIT):
        return pl.pallas_call(
            kernel,
            out_shape=outs,
            in_specs=in_specs,
            out_specs=out_specs,
            scratch_shapes=scratch,
            compiler_params=pltpu.CompilerParams(vmem_limit_bytes=limit),
            cost_estimate=pl.CostEstimate(flops=flops, bytes_accessed=moved, transcendentals=0),
        )(*ins)

    def array(shape, kind):
        return jax.ShapeDtypeStruct(shape, kind)

    def add_product(pieces, places, total=None):
        extra = [] if total is None else [total]
        return call(
            functools.partial(project, len(pieces), places),
            array((CORES * rows, 3 * HEAD), f32),
            [tok_own, tok_other, *pieces, *extra],
            VMEM, [VMEM] * (2 + len(pieces) + len(extra)),
            flops=rows * HEAD * (1 if total is not None else 1000000),
        )

    tok_other = flip(tok_own, "seq", blocks, 1)
    width = w_out.shape[1]
    grid = n == 4 and blocks % (4 * CORES) == 0 and shard % 512 == 0 and width % 256 == 0

    def cut(layout, *sizes):
        return call(
            functools.partial(cut_qkv, layout),
            [array((size, 3 * HEAD), bf16) for size in sizes],
            [w_qkv], [VMEM] * len(sizes), [HBM],
            scratch=[pltpu.SemaphoreType.DMA((3 * len(sizes),))], limit=CUT_LIMIT,
        )

    out_cut = functools.partial(
        call, cut_out, [array((HEAD, width), bf16)] * 2, [w_out], [VMEM] * 2, [VMEM]
    )
    total = None
    if grid:
        quarter = shard // 4
        own, part = cut(lambda shard: [0, quarter_of() * quarter], shard, quarter)
        far = [flip(part, "dp", n, 3)]
        from_x = flip(own, "dp", n, 1)
        from_y = flip(own, "dp", n, 2)
        far.append(flip(far[0], "seq", blocks, CORES * 2))
        far.append(flip(far[0], "seq", blocks, CORES))
        here, own = lax.optimization_barrier((far[0], own))
        total = add_product([own], functools.partial(places_near, shard, (0,)))
        passed, total = lax.optimization_barrier((far[1], total))
        far.append(flip(passed, "seq", blocks, CORES))
        own_mine, own_theirs = out_cut()
        sent = own_mine
        outs = []
        for i, mask in enumerate((1, 2, 3)):
            sent, far[1 + i], total = lax.optimization_barrier((sent, far[1 + i], total))
            outs.append(flip(sent, "dp", n, mask))
        out_x, out_y, out_d = outs
        total = add_product(far[:3], lambda: places_far(shard)[:3], total)
        pieces = [from_x, from_y, far[3]]
        places = lambda: places_near(shard, (1, 2)) + places_far(shard)[3:]
    else:
        whole = cut(lambda shard: [0], shard)[0]
        pieces, places = [lax.all_gather(whole, "dp", axis=0, tiled=True)], lambda: [0]
    extra = [] if total is None else [total]

    query, state, chip, intra = call(
        functools.partial(project_attend, len(pieces), places),
        [
            array((CORES, rows, HEAD), bf16),
            array((CORES, HEAD, HEAD), f32),
            array((blocks // CORES, HEAD, HEAD), bf16),
            array((CORES, rows, HEAD), f32),
        ],
        [tok_own, tok_other, *pieces, *extra],
        [VMEM] * 4, [VMEM] * (2 + len(pieces) + len(extra)),
        flops=2 * CORES * rows * sum(piece.shape[0] for piece in pieces) * 3 * HEAD,
    )

    columns = [list(range(c, blocks, CORES)) for c in range(CORES)]
    got = lax.all_to_all(chip, "seq", 0, 0, axis_index_groups=columns, tiled=True)
    if grid:
        their_x = flip(out_x, "seq", blocks, 1)
        their_y = flip(out_y, "seq", blocks, 1)
    normed_own, normed_other = call(
        normalise,
        [array((rows, HEAD), bf16)] * 2,
        [query, state, intra, norm_gain.reshape(heads, HEAD), got],
        [VMEM] * 2, [VMEM] * 5,
    )
    normed_got = flip(normed_other, "seq", blocks, 1)

    if grid:
        out_d, normed_got = lax.optimization_barrier((out_d, normed_got))
        their_d = flip(out_d, "seq", blocks, 1)
        mine = [own_mine, out_x, out_y, out_d]
        theirs = [own_theirs, their_x, their_y, their_d]
        places = functools.partial(places_out, width)
    else:
        mine = [lax.all_gather(out_cut()[0], "dp", axis=1, tiled=True)]
        theirs = [flip(mine[0], "seq", blocks, 1)]
        places = lambda: [0]
    mixed = call(
        functools.partial(mix, len(mine), places),
        array((rows, n * width), bf16),
        [normed_own, normed_got, *mine, *theirs],
        HBM, [VMEM] * (2 + 2 * len(mine)),
        scratch=[pltpu.VMEM((rows, n * width), bf16), pltpu.SemaphoreType.DMA((16,))],
        flops=2 * rows * 2 * HEAD * n * width, moved=2 * rows * n * width,
    )
    return mixed[None]


def solution(mesh):
    n, blocks = mesh.shape["dp"], mesh.shape["seq"]
    return jax.shard_map(
        functools.partial(shards, n, blocks),
        mesh=mesh,
        in_specs=(P("dp", "seq", None), P("dp", None), P(), P(None, "dp")),
        out_specs=P("dp", "seq", None),
        check_vma=False,
    )
```

```python
import functools

import jax
import jax.numpy as jnp
from jax import lax
from jax.experimental import pallas as pl
from jax.experimental.pallas import tpu as pltpu
from jax.sharding import PartitionSpec as P

HEAD = 128
CORES = 2
VMEM_LIMIT = 24 * 1024 * 1024
CUT_LIMIT = 52 * 1024 * 1024
VMEM = pl.BlockSpec(memory_space=pltpu.VMEM)
HBM = pl.BlockSpec(memory_space=pltpu.HBM)


def flip(x, axis, size, mask):
    return lax.ppermute(x, axis, [(i, i ^ mask) for i in range(size)])


def dot(a, b, contract=((1,), (0,))):
    return lax.dot_general(a, b, (contract, ((), ())), preferred_element_type=jnp.float32)


def position():
    return lax.axis_index("dp"), lax.rem(lax.axis_index("seq"), CORES)


def quarter_of():
    return lax.rem(lax.axis_index("seq") // CORES, 4)


def cut_qkv(layout, w_qkv, *refs):
    outs, sem = refs[:-1], refs[-1]
    _, core = position()
    shard = w_qkv.shape[0]
    feat = w_qkv.shape[1] // 3
    copies = []
    for out, start in zip(outs, layout(shard)):
        rows = pl.ds(pl.multiple_of(start, 16), out.shape[0])
        for j in range(3):
            cols = pl.ds(pl.multiple_of(j * feat + core * HEAD, HEAD), HEAD)
            target = out.at[:, j * HEAD : (j + 1) * HEAD]
            copies.append(pltpu.make_async_copy(w_qkv.at[rows, cols], target, sem.at[len(copies)]))
            copies[-1].start()
    for copy in copies:
        copy.wait()


def cut_out(w_out, mine, theirs):
    _, core = position()
    for out, head in ((mine, core), (theirs, 1 - core)):
        out[...] = w_out[pl.ds(pl.multiple_of(head * HEAD, HEAD), HEAD), :]


def product(tok_a, tok_b, pieces, places):
    cols = [
        pl.ds(pl.multiple_of(place, 128), piece.shape[0]) for piece, place in zip(pieces, places)
    ]
    tok = jnp.concatenate(
        [jnp.concatenate([ref[:, c] for c in cols], axis=1) for ref in (tok_a, tok_b)], axis=0
    )
    weights = jnp.concatenate([piece[...] for piece in pieces], axis=0)
    return dot(tok, weights)


def places_near(shard, offsets):
    at = lax.axis_index("dp")
    return [(at ^ offset) * shard for offset in offsets]


def places_far(shard):
    start = places_near(shard, (3,))[0]
    mine = quarter_of()
    return [start + (mine ^ mask) * (shard // 4) for mask in (0, 2, 1, 3)]


def project(count, places, tok_a, tok_b, *refs):
    pieces, before, total = refs[:count], refs[count:-1], refs[-1]
    term = product(tok_a, tok_b, pieces, places())
    total[...] = before[0][...] + term if before else term


def project_states(count, places, tok_a, tok_b, *refs):
    pieces, before = refs[:count], refs[count:-4]
    act_out, value_out, state_out, chip_out = refs[-4:]
    proj = product(tok_a, tok_b, pieces, places())
    if before:
        proj = before[0][...] + proj
    rows = value_out.shape[1]
    chip = None
    for b in range(CORES):
        part = proj[b * rows : (b + 1) * rows, :]
        act = part[:, : 2 * HEAD]
        act = (act / (1.0 + jnp.exp(-act))).astype(jnp.bfloat16)
        values = part[:, 2 * HEAD :].astype(jnp.bfloat16)
        state = dot(act[:, HEAD:], values, ((0,), (0,)))
        chip = state if chip is None else chip + state
        act_out[b] = act
        value_out[b] = values
        state_out[b] = state
    chip_out[...] = chip.astype(jnp.bfloat16)


def attend(act, values, intra_out):
    rows = intra_out.shape[1]
    row = lax.broadcasted_iota(jnp.int32, (rows, rows), 0)
    col = lax.broadcasted_iota(jnp.int32, (rows, rows), 1)
    for b in range(CORES):
        scores = dot(act[b, :, :HEAD], act[b, :, HEAD:], ((1,), (1,)))
        scores = jnp.where(row >= col, scores, 0.0).astype(jnp.bfloat16)
        intra_out[b] = dot(scores, values[b])


def normalise(steps, act, state, intra, gain, *refs):
    got, (own_out, other_out) = refs[:steps], refs[steps:]
    _, core = position()
    chip_at = lax.axis_index("seq") // CORES
    base = jnp.zeros((HEAD, HEAD), jnp.float32)
    for step, ref in enumerate(got):
        base = base + jnp.where((chip_at >> step) % 2 == 1, ref[...].astype(jnp.float32), 0.0)
    odd = core == 1
    own_prefix = jnp.where(odd, base + state[1], base)
    other_prefix = jnp.where(odd, base, base + state[0])
    scale = gain[pl.ds(core, 1), :]
    for b, (prefix, out) in enumerate(((own_prefix, own_out), (other_prefix, other_out))):
        attended = dot(act[b, :, :HEAD], prefix.astype(jnp.bfloat16)) + intra[b]
        meansq = jnp.mean(attended * attended, axis=-1, keepdims=True)
        out[...] = (attended * lax.rsqrt(meansq + 1e-06) * scale).astype(jnp.bfloat16)


def mix(count, places, own, other, *refs):
    mine, theirs, (out, stage, sem) = refs[:count], refs[count : 2 * count], refs[2 * count :]
    normed = jnp.concatenate([own[...], other[...]], axis=1)
    copies = []
    slot = 0
    for my_rows, their_rows, place in zip(mine, theirs, places()):
        width = my_rows.shape[1]
        step = min(width, 512)
        for at_col in range(0, width, step):
            part = slice(at_col, at_col + step)
            weights = jnp.concatenate([my_rows[:, part], their_rows[:, part]], axis=0)
            here = stage.at[:, slot : slot + step]
            here[...] = dot(normed, weights).astype(jnp.bfloat16)
            cols = pl.ds(pl.multiple_of(place + at_col, 128), step)
            copies.append(pltpu.make_async_copy(here, out.at[:, cols], sem.at[len(copies)]))
            copies[-1].start()
            slot += step
    for copy in copies:
        copy.wait()


def places_out(width):
    at = lax.axis_index("dp")
    return [(at ^ offset) * width for offset in range(4)]


def shards(n, blocks, tokens, w_qkv, norm_gain, w_out):
    tok_own = tokens[0]
    rows, depth = tok_own.shape
    shard = w_qkv.shape[0]
    heads = norm_gain.shape[0] // HEAD
    bf16, f32 = jnp.bfloat16, jnp.float32

    def call(kernel, outs, ins, out_specs, in_specs, scratch=(), flops=0, moved=0, limit=VMEM_LIMIT):
        return pl.pallas_call(
            kernel,
            out_shape=outs,
            in_specs=in_specs,
            out_specs=out_specs,
            scratch_shapes=scratch,
            compiler_params=pltpu.CompilerParams(vmem_limit_bytes=limit),
            cost_estimate=pl.CostEstimate(flops=flops, bytes_accessed=moved, transcendentals=0),
        )(*ins)

    def array(shape, kind):
        return jax.ShapeDtypeStruct(shape, kind)

    def add_product(pieces, places, total=None):
        extra = [] if total is None else [total]
        return call(
            functools.partial(project, len(pieces), places),
            array((CORES * rows, 3 * HEAD), f32),
            [tok_own, tok_other, *pieces, *extra],
            VMEM, [VMEM] * (2 + len(pieces) + len(extra)),
            flops=rows * HEAD * (1 if total is not None else 1000000),
        )

    tok_other = flip(tok_own, "seq", blocks, 1)
    width = w_out.shape[1]
    grid = n == 4 and blocks % (4 * CORES) == 0 and shard % 512 == 0 and width % 256 == 0

    def cut(layout, *sizes):
        return call(
            functools.partial(cut_qkv, layout),
            [array((size, 3 * HEAD), bf16) for size in sizes],
            [w_qkv], [VMEM] * len(sizes), [HBM],
            scratch=[pltpu.SemaphoreType.DMA((3 * len(sizes),))], limit=CUT_LIMIT,
        )

    out_cut = functools.partial(
        call, cut_out, [array((HEAD, width), bf16)] * 2, [w_out], [VMEM] * 2, [VMEM]
    )
    total = None
    if grid:
        quarter = shard // 4
        own, part = cut(lambda shard: [0, quarter_of() * quarter], shard, quarter)
        far = [flip(part, "dp", n, 3)]
        from_x = flip(own, "dp", n, 1)
        from_y = flip(own, "dp", n, 2)
        far.append(flip(far[0], "seq", blocks, CORES * 2))
        far.append(flip(far[0], "seq", blocks, CORES))
        here, own = lax.optimization_barrier((far[0], own))
        total = add_product([own], functools.partial(places_near, shard, (0,)))
        passed, total = lax.optimization_barrier((far[1], total))
        far.append(flip(passed, "seq", blocks, CORES))
        own_mine, own_theirs = out_cut()
        sent = own_mine
        outs = []
        for i, mask in ((0, 1), (1, 2), (1, 3)):
            if mask == 1:
                sent, total = lax.optimization_barrier((sent, total))
            sent, far[1 + i] = lax.optimization_barrier((sent, far[1 + i]))
            outs.append(flip(sent, "dp", n, mask))
        out_x, out_y, out_d = outs
        total = add_product([from_x, from_y], functools.partial(places_near, shard, (1, 2)), total)
        pieces, places = far, functools.partial(places_far, shard)
    else:
        whole = cut(lambda shard: [0], shard)[0]
        pieces, places = [lax.all_gather(whole, "dp", axis=0, tiled=True)], lambda: [0]
    extra = [] if total is None else [total]

    act, values, state, chip = call(
        functools.partial(project_states, len(pieces), places),
        [
            array((CORES, rows, 2 * HEAD), bf16),
            array((CORES, rows, HEAD), bf16),
            array((CORES, HEAD, HEAD), f32),
            array((HEAD, HEAD), bf16),
        ],
        [tok_own, tok_other, *pieces, *extra],
        [VMEM] * 4, [VMEM] * (2 + len(pieces) + len(extra)),
        flops=2 * CORES * rows * sum(piece.shape[0] for piece in pieces) * 3 * HEAD,
    )
    intra = call(
        attend, array((CORES, rows, HEAD), f32), [act, values], VMEM, [VMEM] * 2,
        flops=4 * CORES * rows * rows * HEAD,
    )

    got, group = [], chip
    for step in range((blocks // CORES).bit_length() - 1):
        if got:
            group = (group.astype(f32) + got[-1].astype(f32)).astype(bf16)
            if grid:
                group, out_x, out_y = lax.optimization_barrier((group, out_x, out_y))
        got.append(flip(group, "seq", blocks, CORES << step))
    if grid:
        their_x = flip(out_x, "seq", blocks, 1)
        their_y = flip(out_y, "seq", blocks, 1)
    normed_own, normed_other = call(
        functools.partial(normalise, len(got)),
        [array((rows, HEAD), bf16)] * 2,
        [act, state, intra, norm_gain.reshape(heads, HEAD), *got],
        [VMEM] * 2, [VMEM] * (4 + len(got)),
    )
    normed_got = flip(normed_other, "seq", blocks, 1)

    if grid:
        out_d, normed_other = lax.optimization_barrier((out_d, normed_other))
        their_d = flip(out_d, "seq", blocks, 1)
        mine = [own_mine, out_x, out_y, out_d]
        theirs = [own_theirs, their_x, their_y, their_d]
        places = functools.partial(places_out, width)
    else:
        mine = [lax.all_gather(out_cut()[0], "dp", axis=1, tiled=True)]
        theirs = [flip(mine[0], "seq", blocks, 1)]
        places = lambda: [0]
    mixed = call(
        functools.partial(mix, len(mine), places),
        array((rows, n * width), bf16),
        [normed_own, normed_got, *mine, *theirs],
        HBM, [VMEM] * (2 + 2 * len(mine)),
        scratch=[pltpu.VMEM((rows, n * width), bf16), pltpu.SemaphoreType.DMA((16,))],
        flops=2 * rows * 2 * HEAD * n * width, moved=2 * rows * n * width,
    )
    return mixed[None]


def solution(mesh):
    n, blocks = mesh.shape["dp"], mesh.shape["seq"]
    return jax.shard_map(
        functools.partial(shards, n, blocks),
        mesh=mesh,
        in_specs=(P("dp", "seq", None), P("dp", None), P(), P(None, "dp")),
        out_specs=P("dp", "seq", None),
        check_vma=False,
    )
```

```python
import functools

import jax
import jax.numpy as jnp
from jax import lax
from jax.experimental import pallas as pl
from jax.experimental.pallas import tpu as pltpu
from jax.sharding import PartitionSpec as P

HEAD = 128
CORES = 2
VMEM_LIMIT = 24 * 1024 * 1024
CUT_LIMIT = 52 * 1024 * 1024
VMEM = pl.BlockSpec(memory_space=pltpu.VMEM)
HBM = pl.BlockSpec(memory_space=pltpu.HBM)


def flip(x, axis, size, mask):
    return lax.ppermute(x, axis, [(i, i ^ mask) for i in range(size)])


def dot(a, b, contract=((1,), (0,))):
    return lax.dot_general(a, b, (contract, ((), ())), preferred_element_type=jnp.float32)


def position():
    return lax.axis_index("dp"), lax.rem(lax.axis_index("seq"), CORES)


def quarter_of():
    return lax.rem(lax.axis_index("seq") // CORES, 4)


def cut_qkv(layout, w_qkv, *refs):
    outs, sem = refs[:-1], refs[-1]
    _, core = position()
    shard = w_qkv.shape[0]
    feat = w_qkv.shape[1] // 3
    copies = []
    for out, start in zip(outs, layout(shard)):
        rows = pl.ds(pl.multiple_of(start, 16), out.shape[0])
        for j in range(3):
            cols = pl.ds(pl.multiple_of(j * feat + core * HEAD, HEAD), HEAD)
            target = out.at[:, j * HEAD : (j + 1) * HEAD]
            copies.append(pltpu.make_async_copy(w_qkv.at[rows, cols], target, sem.at[len(copies)]))
            copies[-1].start()
    for copy in copies:
        copy.wait()


def cut_out(w_out, mine, theirs):
    _, core = position()
    for out, head in ((mine, core), (theirs, 1 - core)):
        out[...] = w_out[pl.ds(pl.multiple_of(head * HEAD, HEAD), HEAD), :]


def product(tok_a, tok_b, pieces, places):
    cols = [
        pl.ds(pl.multiple_of(place, 128), piece.shape[0]) for piece, place in zip(pieces, places)
    ]
    tok = jnp.concatenate(
        [jnp.concatenate([ref[:, c] for c in cols], axis=1) for ref in (tok_a, tok_b)], axis=0
    )
    weights = jnp.concatenate([piece[...] for piece in pieces], axis=0)
    return dot(tok, weights)


def places_near(shard, offsets):
    at = lax.axis_index("dp")
    return [(at ^ offset) * shard for offset in offsets]


def places_far(shard):
    start = places_near(shard, (3,))[0]
    mine = quarter_of()
    return [start + (mine ^ mask) * (shard // 4) for mask in (0, 2, 1, 3)]


def project(count, places, tok_a, tok_b, *refs):
    pieces, before, total = refs[:count], refs[count:-1], refs[-1]
    term = product(tok_a, tok_b, pieces, places())
    total[...] = before[0][...] + term if before else term


def project_states(count, places, tok_a, tok_b, *refs):
    pieces, before = refs[:count], refs[count:-4]
    act_out, value_out, state_out, chip_out = refs[-4:]
    proj = product(tok_a, tok_b, pieces, places())
    if before:
        proj = before[0][...] + proj
    rows = value_out.shape[1]
    chip = None
    for b in range(CORES):
        part = proj[b * rows : (b + 1) * rows, :]
        act = part[:, : 2 * HEAD]
        act = (act / (1.0 + jnp.exp(-act))).astype(jnp.bfloat16)
        values = part[:, 2 * HEAD :].astype(jnp.bfloat16)
        state = dot(act[:, HEAD:], values, ((0,), (0,)))
        chip = state if chip is None else chip + state
        act_out[b] = act
        value_out[b] = values
        state_out[b] = state
    chip_out[...] = chip.astype(jnp.bfloat16)


def attend(act, values, intra_out):
    rows = intra_out.shape[1]
    row = lax.broadcasted_iota(jnp.int32, (rows, rows), 0)
    col = lax.broadcasted_iota(jnp.int32, (rows, rows), 1)
    for b in range(CORES):
        scores = dot(act[b, :, :HEAD], act[b, :, HEAD:], ((1,), (1,)))
        scores = jnp.where(row >= col, scores, 0.0).astype(jnp.bfloat16)
        intra_out[b] = dot(scores, values[b])


def normalise(steps, act, state, intra, gain, *refs):
    got, (own_out, other_out) = refs[:steps], refs[steps:]
    _, core = position()
    chip_at = lax.axis_index("seq") // CORES
    base = jnp.zeros((HEAD, HEAD), jnp.float32)
    for step, ref in enumerate(got):
        base = base + jnp.where((chip_at >> step) % 2 == 1, ref[...].astype(jnp.float32), 0.0)
    odd = core == 1
    own_prefix = jnp.where(odd, base + state[1], base)
    other_prefix = jnp.where(odd, base, base + state[0])
    scale = gain[pl.ds(core, 1), :]
    for b, (prefix, out) in enumerate(((own_prefix, own_out), (other_prefix, other_out))):
        attended = dot(act[b, :, :HEAD], prefix.astype(jnp.bfloat16)) + intra[b]
        meansq = jnp.mean(attended * attended, axis=-1, keepdims=True)
        out[...] = (attended * lax.rsqrt(meansq + 1e-06) * scale).astype(jnp.bfloat16)


def mix(count, places, own, other, *refs):
    mine, theirs, (out, stage, sem) = refs[:count], refs[count : 2 * count], refs[-3:]
    normed = jnp.concatenate([own[...], other[...]], axis=1)
    copies = []
    slot = 0
    for my_rows, their_rows, place in zip(mine, theirs, places()):
        width = my_rows.shape[1]
        step = min(width, 512)
        for at_col in range(0, width, step):
            part = slice(at_col, at_col + step)
            weights = jnp.concatenate([my_rows[:, part], their_rows[:, part]], axis=0)
            here = stage.at[:, slot : slot + step]
            here[...] = dot(normed, weights).astype(jnp.bfloat16)
            cols = pl.ds(pl.multiple_of(place + at_col, 128), step)
            copies.append(pltpu.make_async_copy(here, out.at[:, cols], sem.at[len(copies)]))
            copies[-1].start()
            slot += step
    for copy in copies:
        copy.wait()


def places_out(width, offsets):
    at = lax.axis_index("dp")
    return [(at ^ offset) * width for offset in offsets]


def shards(n, blocks, tokens, w_qkv, norm_gain, w_out):
    tok_own = tokens[0]
    rows, depth = tok_own.shape
    shard = w_qkv.shape[0]
    heads = norm_gain.shape[0] // HEAD
    bf16, f32 = jnp.bfloat16, jnp.float32

    def call(kernel, outs, ins, out_specs, in_specs, scratch=(), flops=0, moved=0, limit=VMEM_LIMIT):
        return pl.pallas_call(
            kernel,
            out_shape=outs,
            in_specs=in_specs,
            out_specs=out_specs,
            scratch_shapes=scratch,
            compiler_params=pltpu.CompilerParams(vmem_limit_bytes=limit),
            cost_estimate=pl.CostEstimate(flops=flops, bytes_accessed=moved, transcendentals=0),
        )(*ins)

    def array(shape, kind):
        return jax.ShapeDtypeStruct(shape, kind)

    def add_product(pieces, places, total=None):
        extra = [] if total is None else [total]
        return call(
            functools.partial(project, len(pieces), places),
            array((CORES * rows, 3 * HEAD), f32),
            [tok_own, tok_other, *pieces, *extra],
            VMEM, [VMEM] * (2 + len(pieces) + len(extra)),
            flops=rows * HEAD * (1 if total is not None else 1000000),
        )

    tok_other = flip(tok_own, "seq", blocks, 1)
    width = w_out.shape[1]
    grid = n == 4 and blocks % (4 * CORES) == 0 and shard % 512 == 0 and width % 256 == 0

    def cut(layout, *sizes):
        return call(
            functools.partial(cut_qkv, layout),
            [array((size, 3 * HEAD), bf16) for size in sizes],
            [w_qkv], [VMEM] * len(sizes), [HBM],
            scratch=[pltpu.SemaphoreType.DMA((3 * len(sizes),))], limit=CUT_LIMIT,
        )

    out_cut = functools.partial(
        call, cut_out, [array((HEAD, width), bf16)] * 2, [w_out], [VMEM] * 2, [VMEM]
    )
    total = None
    if grid:
        quarter = shard // 4
        own, part = cut(lambda shard: [0, quarter_of() * quarter], shard, quarter)
        far = [flip(part, "dp", n, 3)]
        from_x = flip(own, "dp", n, 1)
        from_y = flip(own, "dp", n, 2)
        far.append(flip(far[0], "seq", blocks, CORES * 2))
        far.append(flip(far[0], "seq", blocks, CORES))
        here, own = lax.optimization_barrier((far[0], own))
        total = add_product([own], functools.partial(places_near, shard, (0,)))
        passed, total = lax.optimization_barrier((far[1], total))
        far.append(flip(passed, "seq", blocks, CORES))
        own_mine, own_theirs = out_cut()
        sent = own_mine
        outs = []
        for i, mask in ((0, 1), (1, 2), (1, 3)):
            if mask == 1:
                sent, total = lax.optimization_barrier((sent, total))
            sent, far[1 + i] = lax.optimization_barrier((sent, far[1 + i]))
            outs.append(flip(sent, "dp", n, mask))
        out_x, out_y, out_d = outs
        total = add_product([from_x, from_y], functools.partial(places_near, shard, (1, 2)), total)
        pieces, places = far, functools.partial(places_far, shard)
    else:
        whole = cut(lambda shard: [0], shard)[0]
        pieces, places = [lax.all_gather(whole, "dp", axis=0, tiled=True)], lambda: [0]
    extra = [] if total is None else [total]

    act, values, state, chip = call(
        functools.partial(project_states, len(pieces), places),
        [
            array((CORES, rows, 2 * HEAD), bf16),
            array((CORES, rows, HEAD), bf16),
            array((CORES, HEAD, HEAD), f32),
            array((HEAD, HEAD), bf16),
        ],
        [tok_own, tok_other, *pieces, *extra],
        [VMEM] * 4, [VMEM] * (2 + len(pieces) + len(extra)),
        flops=2 * CORES * rows * sum(piece.shape[0] for piece in pieces) * 3 * HEAD,
    )
    intra = call(
        attend, array((CORES, rows, HEAD), f32), [act, values], VMEM, [VMEM] * 2,
        flops=4 * CORES * rows * rows * HEAD,
    )

    got, group = [], chip
    for step in range((blocks // CORES).bit_length() - 1):
        if got:
            group = (group.astype(f32) + got[-1].astype(f32)).astype(bf16)
            if grid:
                group, out_x, out_y = lax.optimization_barrier((group, out_x, out_y))
        got.append(flip(group, "seq", blocks, CORES << step))
    if grid:
        their_x = flip(out_x, "seq", blocks, 1)
        their_y = flip(out_y, "seq", blocks, 1)
    normed_own, normed_other = call(
        functools.partial(normalise, len(got)),
        [array((rows, HEAD), bf16)] * 2,
        [act, state, intra, norm_gain.reshape(heads, HEAD), *got],
        [VMEM] * 2, [VMEM] * (4 + len(got)),
    )
    normed_got = flip(normed_other, "seq", blocks, 1)

    if grid:
        out_d, normed_got = lax.optimization_barrier((out_d, normed_got))
        their_d = flip(out_d, "seq", blocks, 1)

    def write(mine, theirs, places, before=()):
        columns = sum(piece.shape[1] for piece in mine)
        ins = [normed_own, normed_got, *mine, *theirs]
        return pl.pallas_call(
            functools.partial(mix, len(mine), places),
            out_shape=array((rows, n * width), bf16),
            in_specs=[VMEM] * len(ins) + [HBM] * len(before),
            out_specs=HBM,
            scratch_shapes=[pltpu.VMEM((rows, columns), bf16), pltpu.SemaphoreType.DMA((16,))],
            input_output_aliases={len(ins): 0} if before else {},
            compiler_params=pltpu.CompilerParams(vmem_limit_bytes=VMEM_LIMIT),
            cost_estimate=pl.CostEstimate(
                flops=2 * rows * 2 * HEAD * columns,
                bytes_accessed=2 * rows * columns,
                transcendentals=0,
            ),
        )(*ins, *before)

    if grid:
        mixed = write(
            [own_mine, out_x, out_y], [own_theirs, their_x, their_y],
            functools.partial(places_out, width, (0, 1, 2)),
        )
        mixed = write([out_d], [their_d], functools.partial(places_out, width, (3,)), [mixed])
    else:
        mine = lax.all_gather(out_cut()[0], "dp", axis=1, tiled=True)
        mixed = write([mine], [flip(mine, "seq", blocks, 1)], lambda: [0])
    return mixed[None]


def solution(mesh):
    n, blocks = mesh.shape["dp"], mesh.shape["seq"]
    return jax.shard_map(
        functools.partial(shards, n, blocks),
        mesh=mesh,
        in_specs=(P("dp", "seq", None), P("dp", None), P(), P(None, "dp")),
        out_specs=P("dp", "seq", None),
        check_vma=False,
    )
```

```python
import functools

import jax
import jax.numpy as jnp
from jax import lax
from jax.experimental import pallas as pl
from jax.experimental.pallas import tpu as pltpu
from jax.sharding import PartitionSpec as P

HEAD = 128
CORES = 2
VMEM_LIMIT = 24 * 1024 * 1024
CUT_LIMIT = 52 * 1024 * 1024
VMEM = pl.BlockSpec(memory_space=pltpu.VMEM)
HBM = pl.BlockSpec(memory_space=pltpu.HBM)


def flip(x, axis, size, mask):
    return lax.ppermute(x, axis, [(i, i ^ mask) for i in range(size)])


def dot(a, b, contract=((1,), (0,))):
    return lax.dot_general(a, b, (contract, ((), ())), preferred_element_type=jnp.float32)


def position():
    return lax.axis_index("dp"), lax.rem(lax.axis_index("seq"), CORES)


def quarter_of():
    return lax.rem(lax.axis_index("seq") // CORES, 4)


def cut_qkv(layout, w_qkv, *refs):
    outs, sem = refs[:-1], refs[-1]
    _, core = position()
    shard = w_qkv.shape[0]
    feat = w_qkv.shape[1] // 3
    copies = []
    for out, start in zip(outs, layout(shard)):
        rows = pl.ds(pl.multiple_of(start, 16), out.shape[0])
        for j in range(3):
            cols = pl.ds(pl.multiple_of(j * feat + core * HEAD, HEAD), HEAD)
            target = out.at[:, j * HEAD : (j + 1) * HEAD]
            copies.append(pltpu.make_async_copy(w_qkv.at[rows, cols], target, sem.at[len(copies)]))
            copies[-1].start()
    for copy in copies:
        copy.wait()


def cut_out(w_out, mine, theirs):
    _, core = position()
    for out, head in ((mine, core), (theirs, 1 - core)):
        out[...] = w_out[pl.ds(pl.multiple_of(head * HEAD, HEAD), HEAD), :]


def product(tok_a, tok_b, pieces, places):
    cols = [
        pl.ds(pl.multiple_of(place, 128), piece.shape[0]) for piece, place in zip(pieces, places)
    ]
    tok = jnp.concatenate(
        [jnp.concatenate([ref[:, c] for c in cols], axis=1) for ref in (tok_a, tok_b)], axis=0
    )
    weights = jnp.concatenate([piece[...] for piece in pieces], axis=0)
    return dot(tok, weights)


def places_near(shard, offsets):
    at = lax.axis_index("dp")
    return [(at ^ offset) * shard for offset in offsets]


def places_far(shard):
    start = places_near(shard, (3,))[0]
    mine = quarter_of()
    return [start + (mine ^ mask) * (shard // 4) for mask in (0, 2, 1, 3)]


def project(count, places, tok_a, tok_b, *refs):
    pieces, before, total = refs[:count], refs[count:-1], refs[-1]
    term = product(tok_a, tok_b, pieces, places())
    total[...] = before[0][...] + term if before else term


def project_states(count, places, tok_a, tok_b, *refs):
    pieces, before = refs[:count], refs[count:-4]
    act_out, value_out, state_out, chip_out = refs[-4:]
    proj = product(tok_a, tok_b, pieces, places())
    if before:
        proj = before[0][...] + proj
    rows = value_out.shape[1]
    chip = None
    for b in range(CORES):
        part = proj[b * rows : (b + 1) * rows, :]
        act = part[:, : 2 * HEAD]
        act = (act / (1.0 + jnp.exp(-act))).astype(jnp.bfloat16)
        values = part[:, 2 * HEAD :].astype(jnp.bfloat16)
        state = dot(act[:, HEAD:], values, ((0,), (0,)))
        chip = state if chip is None else chip + state
        act_out[b] = act
        value_out[b] = values
        state_out[b] = state
    chip_out[...] = chip.astype(jnp.bfloat16)


def attend(act, values, intra_out):
    rows = intra_out.shape[1]
    row = lax.broadcasted_iota(jnp.int32, (rows, rows), 0)
    col = lax.broadcasted_iota(jnp.int32, (rows, rows), 1)
    for b in range(CORES):
        scores = dot(act[b, :, :HEAD], act[b, :, HEAD:], ((1,), (1,)))
        scores = jnp.where(row >= col, scores, 0.0).astype(jnp.bfloat16)
        intra_out[b] = dot(scores, values[b])


def normalise(steps, act, state, intra, gain, *refs):
    got, (own_out, other_out) = refs[:steps], refs[steps:]
    _, core = position()
    chip_at = lax.axis_index("seq") // CORES
    base = jnp.zeros((HEAD, HEAD), jnp.float32)
    for step, ref in enumerate(got):
        base = base + jnp.where((chip_at >> step) % 2 == 1, ref[...].astype(jnp.float32), 0.0)
    odd = core == 1
    own_prefix = jnp.where(odd, base + state[1], base)
    other_prefix = jnp.where(odd, base, base + state[0])
    scale = gain[pl.ds(core, 1), :]
    for b, (prefix, out) in enumerate(((own_prefix, own_out), (other_prefix, other_out))):
        attended = dot(act[b, :, :HEAD], prefix.astype(jnp.bfloat16)) + intra[b]
        meansq = jnp.mean(attended * attended, axis=-1, keepdims=True)
        out[...] = (attended * lax.rsqrt(meansq + 1e-06) * scale).astype(jnp.bfloat16)


def mix(count, places, own, other, *refs):
    mine, theirs, (out, stage, sem) = refs[:count], refs[count : 2 * count], refs[2 * count :]
    normed = jnp.concatenate([own[...], other[...]], axis=1)
    copies = []
    slot = 0
    for my_rows, their_rows, place in zip(mine, theirs, places()):
        width = my_rows.shape[1]
        step = min(width, 512)
        for at_col in range(0, width, step):
            part = slice(at_col, at_col + step)
            weights = jnp.concatenate([my_rows[:, part], their_rows[:, part]], axis=0)
            here = stage.at[:, slot : slot + step]
            here[...] = dot(normed, weights).astype(jnp.bfloat16)
            cols = pl.ds(pl.multiple_of(place + at_col, 128), step)
            copies.append(pltpu.make_async_copy(here, out.at[:, cols], sem.at[len(copies)]))
            copies[-1].start()
            slot += step
    for copy in copies:
        copy.wait()


def places_out(width):
    at = lax.axis_index("dp")
    return [(at ^ offset) * width for offset in range(4)]


def shards(n, blocks, tokens, w_qkv, norm_gain, w_out):
    tok_own = tokens[0]
    rows, depth = tok_own.shape
    shard = w_qkv.shape[0]
    heads = norm_gain.shape[0] // HEAD
    bf16, f32 = jnp.bfloat16, jnp.float32

    def call(kernel, outs, ins, out_specs, in_specs, scratch=(), flops=0, moved=0, limit=VMEM_LIMIT):
        return pl.pallas_call(
            kernel,
            out_shape=outs,
            in_specs=in_specs,
            out_specs=out_specs,
            scratch_shapes=scratch,
            compiler_params=pltpu.CompilerParams(vmem_limit_bytes=limit),
            cost_estimate=pl.CostEstimate(flops=flops, bytes_accessed=moved, transcendentals=0),
        )(*ins)

    def array(shape, kind):
        return jax.ShapeDtypeStruct(shape, kind)

    def add_product(pieces, places, total=None):
        extra = [] if total is None else [total]
        return call(
            functools.partial(project, len(pieces), places),
            array((CORES * rows, 3 * HEAD), f32),
            [tok_own, tok_other, *pieces, *extra],
            VMEM, [VMEM] * (2 + len(pieces) + len(extra)),
            flops=rows * HEAD * (1 if total is not None else 1000000),
        )

    tok_other = flip(tok_own, "seq", blocks, 1)
    width = w_out.shape[1]
    grid = n == 4 and blocks % (4 * CORES) == 0 and shard % 512 == 0 and width % 256 == 0

    def cut(layout, *sizes):
        return call(
            functools.partial(cut_qkv, layout),
            [array((size, 3 * HEAD), bf16) for size in sizes],
            [w_qkv], [VMEM] * len(sizes), [HBM],
            scratch=[pltpu.SemaphoreType.DMA((3 * len(sizes),))], limit=CUT_LIMIT,
        )

    out_cut = functools.partial(
        call, cut_out, [array((HEAD, width), bf16)] * 2, [w_out], [VMEM] * 2, [VMEM]
    )
    total = None
    if grid:
        quarter = shard // 4
        own, part = cut(lambda shard: [0, quarter_of() * quarter], shard, quarter)
        far = [flip(part, "dp", n, 3)]
        from_x = flip(own, "dp", n, 1)
        from_y = flip(own, "dp", n, 2)
        far.append(flip(far[0], "seq", blocks, CORES * 2))
        far.append(flip(far[0], "seq", blocks, CORES))
        here, own = lax.optimization_barrier((far[0], own))
        total = add_product([own], functools.partial(places_near, shard, (0,)))
        passed, total = lax.optimization_barrier((far[1], total))
        far.append(flip(passed, "seq", blocks, CORES))
        own_mine, own_theirs = out_cut()
        sent = own_mine
        sent, total, far[1] = lax.optimization_barrier((sent, total, far[1]))
        out_d = flip(sent, "dp", n, 3)
        total = add_product(far[:3], lambda: places_far(shard)[:3], total)
        sent, total = lax.optimization_barrier((sent, total))
        out_x = flip(sent, "dp", n, 1)
        out_y = flip(sent, "dp", n, 2)
        total = add_product([from_x, from_y], functools.partial(places_near, shard, (1, 2)), total)
        pieces, places = far[3:], lambda: places_far(shard)[3:]
    else:
        whole = cut(lambda shard: [0], shard)[0]
        pieces, places = [lax.all_gather(whole, "dp", axis=0, tiled=True)], lambda: [0]
    extra = [] if total is None else [total]

    act, values, state, chip = call(
        functools.partial(project_states, len(pieces), places),
        [
            array((CORES, rows, 2 * HEAD), bf16),
            array((CORES, rows, HEAD), bf16),
            array((CORES, HEAD, HEAD), f32),
            array((HEAD, HEAD), bf16),
        ],
        [tok_own, tok_other, *pieces, *extra],
        [VMEM] * 4, [VMEM] * (2 + len(pieces) + len(extra)),
        flops=2 * CORES * rows * sum(piece.shape[0] for piece in pieces) * 3 * HEAD,
    )
    intra = call(
        attend, array((CORES, rows, HEAD), f32), [act, values], VMEM, [VMEM] * 2,
        flops=4 * CORES * rows * rows * HEAD,
    )

    got, group = [], chip
    for step in range((blocks // CORES).bit_length() - 1):
        if got:
            group = (group.astype(f32) + got[-1].astype(f32)).astype(bf16)
            if grid:
                group, out_d = lax.optimization_barrier((group, out_d))
        got.append(flip(group, "seq", blocks, CORES << step))
    if grid:
        their_d = flip(out_d, "seq", blocks, 1)
    normed_own, normed_other = call(
        functools.partial(normalise, len(got)),
        [array((rows, HEAD), bf16)] * 2,
        [act, state, intra, norm_gain.reshape(heads, HEAD), *got],
        [VMEM] * 2, [VMEM] * (4 + len(got)),
    )
    normed_got = flip(normed_other, "seq", blocks, 1)

    if grid:
        out_x, out_y, normed_other = lax.optimization_barrier((out_x, out_y, normed_other))
        their_x = flip(out_x, "seq", blocks, 1)
        their_y = flip(out_y, "seq", blocks, 1)
        mine = [own_mine, out_x, out_y, out_d]
        theirs = [own_theirs, their_x, their_y, their_d]
        places = functools.partial(places_out, width)
    else:
        mine = [lax.all_gather(out_cut()[0], "dp", axis=1, tiled=True)]
        theirs = [flip(mine[0], "seq", blocks, 1)]
        places = lambda: [0]
    mixed = call(
        functools.partial(mix, len(mine), places),
        array((rows, n * width), bf16),
        [normed_own, normed_got, *mine, *theirs],
        HBM, [VMEM] * (2 + 2 * len(mine)),
        scratch=[pltpu.VMEM((rows, n * width), bf16), pltpu.SemaphoreType.DMA((16,))],
        flops=2 * rows * 2 * HEAD * n * width, moved=2 * rows * n * width,
    )
    return mixed[None]


def solution(mesh):
    n, blocks = mesh.shape["dp"], mesh.shape["seq"]
    return jax.shard_map(
        functools.partial(shards, n, blocks),
        mesh=mesh,
        in_specs=(P("dp", "seq", None), P("dp", None), P(), P(None, "dp")),
        out_specs=P("dp", "seq", None),
        check_vma=False,
    )
```

```python
import functools

import jax
import jax.numpy as jnp
from jax import lax
from jax.experimental import pallas as pl
from jax.experimental.pallas import tpu as pltpu
from jax.sharding import PartitionSpec as P

HEAD = 128
CORES = 2
VMEM_LIMIT = 24 * 1024 * 1024
FIRST_LIMIT = 54 * 1024 * 1024
CUT_LIMIT = 52 * 1024 * 1024
VMEM = pl.BlockSpec(memory_space=pltpu.VMEM)
HBM = pl.BlockSpec(memory_space=pltpu.HBM)


def flip(x, axis, size, mask):
    return lax.ppermute(x, axis, [(i, i ^ mask) for i in range(size)])


def dot(a, b, contract=((1,), (0,))):
    return lax.dot_general(a, b, (contract, ((), ())), preferred_element_type=jnp.float32)


def position():
    return lax.axis_index("dp"), lax.rem(lax.axis_index("seq"), CORES)


def quarter_of():
    return lax.rem(lax.axis_index("seq") // CORES, 4)


def copy_all(pairs, sem):
    copies = [pltpu.make_async_copy(src, dst, sem.at[i]) for i, (src, dst) in enumerate(pairs)]
    for copy in copies:
        copy.start()
    for copy in copies:
        copy.wait()


def head_columns(w_qkv, which, core, start, count):
    feat = w_qkv.shape[1] // 3
    cols = pl.ds(pl.multiple_of(which * feat + core * HEAD, HEAD), HEAD)
    return w_qkv.at[pl.ds(pl.multiple_of(start, 16), count), cols]


def cut_first(w_qkv, w_out, part, own_kv, sem):
    _, core = position()
    shard = w_qkv.shape[0]
    quarter = shard // 4
    start = quarter_of() * quarter
    pairs = []
    for i, which in enumerate((1, 2, 0)):
        place = slice(i * quarter, (i + 1) * quarter)
        pairs.append((head_columns(w_qkv, which, core, start, quarter), part.at[place, :]))
    rows = pl.ds(pl.multiple_of(core * HEAD, HEAD), HEAD)
    width = w_out.shape[1] // 4
    for i in range(width // HEAD):
        cols = pl.ds(pl.multiple_of(quarter_of() * width + i * HEAD, HEAD), HEAD)
        place = slice(3 * quarter + i * HEAD, 3 * quarter + (i + 1) * HEAD)
        pairs.append((w_out.at[rows, cols], part.at[place, :]))
    for j in range(2):
        target = own_kv.at[:, j * HEAD : (j + 1) * HEAD]
        pairs.append((head_columns(w_qkv, 1 + j, core, 0, shard), target))
    copy_all(pairs, sem)


def cut_keys(w_qkv, own_kv, sem):
    _, core = position()
    copy_all(
        [
            (head_columns(w_qkv, 1 + j, core, 0, w_qkv.shape[0]), own_kv.at[:, j * HEAD : (j + 1) * HEAD])
            for j in range(2)
        ],
        sem,
    )


def cut_second(w_qkv, w_out, own_q, mine, theirs, sem):
    _, core = position()
    pairs = [(head_columns(w_qkv, 0, core, 0, w_qkv.shape[0]), own_q)]
    for out, head in ((mine, core), (theirs, 1 - core)):
        pairs.append((w_out.at[pl.ds(pl.multiple_of(head * HEAD, HEAD), HEAD), :], out))
    copy_all(pairs, sem)


def product(tok_a, tok_b, pieces, places):
    cols = [
        pl.ds(pl.multiple_of(place, 128), piece.shape[0]) for piece, place in zip(pieces, places)
    ]
    tok = jnp.concatenate(
        [jnp.concatenate([ref[:, c] for c in cols], axis=1) for ref in (tok_a, tok_b)], axis=0
    )
    weights = jnp.concatenate([piece[...] for piece in pieces], axis=0)
    return dot(tok, weights)


def keys_beside_values(piece):
    half = piece.shape[0] // 2
    return jnp.concatenate([piece[:half, :], piece[half:, :]], axis=1)


def places_near(shard, offsets):
    at = lax.axis_index("dp")
    return [(at ^ offset) * shard for offset in offsets]


def places_far(shard):
    start = places_near(shard, (3,))[0]
    mine = quarter_of()
    return [start + (mine ^ mask) * (shard // 4) for mask in (0, 2, 1, 3)]


def project(count, places, tok_a, tok_b, *refs):
    pieces, before, total = refs[:count], refs[count:-1], refs[-1]
    pieces = [keys_beside_values(piece) if piece.shape[1] == HEAD else piece for piece in pieces]
    term = product(tok_a, tok_b, pieces, places())
    total[...] = before[0][...] + term if before else term


def project_states(count, places, tok_a, tok_b, *refs):
    pieces, before = refs[:count], refs[count:-4]
    key_out, value_out, state_out, chip_out = refs[-4:]
    pieces = [keys_beside_values(piece) if piece.shape[1] == HEAD else piece for piece in pieces]
    proj = product(tok_a, tok_b, pieces, places())
    if before:
        proj = before[0][...] + proj
    rows = value_out.shape[1]
    chip = None
    for b in range(CORES):
        part = proj[b * rows : (b + 1) * rows, :]
        keys = part[:, :HEAD]
        keys = (keys / (1.0 + jnp.exp(-keys))).astype(jnp.bfloat16)
        values = part[:, HEAD:].astype(jnp.bfloat16)
        state = dot(keys, values, ((0,), (0,)))
        chip = state if chip is None else chip + state
        key_out[b] = keys
        value_out[b] = values
        state_out[b] = state
    chip_out[...] = chip.astype(jnp.bfloat16)


def project_queries(count, mixed, places, tok_a, tok_b, keys, values, *refs):
    pieces, outs = refs[:count], refs[count:]
    quarter = None
    if mixed:
        query_out, intra_out, columns_out = outs
        width = columns_out.shape[1] // 4
        quarter = pieces[-1].shape[0] - width
        for i, piece in enumerate(pieces[-mixed:]):
            start = (quarter_of() ^ (0, 2, 1, 3)[i]) * width
            for j in range(width // HEAD):
                cols = pl.ds(pl.multiple_of(start + j * HEAD, HEAD), HEAD)
                columns_out[:, cols] = piece[quarter + j * HEAD : quarter + (j + 1) * HEAD, :]
    else:
        query_out, intra_out = outs
    weights = [piece if i < count - mixed else piece.at[:quarter, :] for i, piece in enumerate(pieces)]
    proj = product(tok_a, tok_b, weights, places())
    query = (proj / (1.0 + jnp.exp(-proj))).astype(jnp.bfloat16)
    rows = intra_out.shape[1]
    row = lax.broadcasted_iota(jnp.int32, (rows, rows), 0)
    col = lax.broadcasted_iota(jnp.int32, (rows, rows), 1)
    for b in range(CORES):
        part = query[b * rows : (b + 1) * rows, :]
        query_out[b] = part
        scores = dot(part, keys[b], ((1,), (1,)))
        scores = jnp.where(row >= col, scores, 0.0).astype(jnp.bfloat16)
        intra_out[b] = dot(scores, values[b])


def normalise(steps, query, state, intra, gain, *refs):
    got, (own_out, other_out) = refs[:steps], refs[steps:]
    _, core = position()
    chip_at = lax.axis_index("seq") // CORES
    base = jnp.zeros((HEAD, HEAD), jnp.float32)
    for step, ref in enumerate(got):
        base = base + jnp.where((chip_at >> step) % 2 == 1, ref[...].astype(jnp.float32), 0.0)
    odd = core == 1
    own_prefix = jnp.where(odd, base + state[1], base)
    other_prefix = jnp.where(odd, base, base + state[0])
    scale = gain[pl.ds(core, 1), :]
    for b, (prefix, out) in enumerate(((own_prefix, own_out), (other_prefix, other_out))):
        attended = dot(query[b], prefix.astype(jnp.bfloat16)) + intra[b]
        meansq = jnp.mean(attended * attended, axis=-1, keepdims=True)
        out[...] = (attended * lax.rsqrt(meansq + 1e-06) * scale).astype(jnp.bfloat16)


def mix(count, places, own, other, *refs):
    mine, theirs, (out, stage, sem) = refs[:count], refs[count : 2 * count], refs[2 * count :]
    normed = jnp.concatenate([own[...], other[...]], axis=1)
    copies = []
    slot = 0
    for my_rows, their_rows, place in zip(mine, theirs, places()):
        width = my_rows.shape[1]
        step = min(width, 512)
        for at_col in range(0, width, step):
            part = slice(at_col, at_col + step)
            weights = jnp.concatenate([my_rows[:, part], their_rows[:, part]], axis=0)
            here = stage.at[:, slot : slot + step]
            here[...] = dot(normed, weights).astype(jnp.bfloat16)
            cols = pl.ds(pl.multiple_of(place + at_col, 128), step)
            copies.append(pltpu.make_async_copy(here, out.at[:, cols], sem.at[len(copies)]))
            copies[-1].start()
            slot += step
    for copy in copies:
        copy.wait()


def places_out(width):
    at = lax.axis_index("dp")
    return [(at ^ offset) * width for offset in range(4)]


def shards(n, blocks, tokens, w_qkv, norm_gain, w_out):
    tok_own = tokens[0]
    rows, depth = tok_own.shape
    shard = w_qkv.shape[0]
    heads = norm_gain.shape[0] // HEAD
    bf16, f32 = jnp.bfloat16, jnp.float32

    def call(kernel, outs, ins, out_specs, in_specs, scratch=(), flops=0, moved=0, limit=VMEM_LIMIT):
        return pl.pallas_call(
            kernel,
            out_shape=outs,
            in_specs=in_specs,
            out_specs=out_specs,
            scratch_shapes=scratch,
            compiler_params=pltpu.CompilerParams(vmem_limit_bytes=limit),
            cost_estimate=pl.CostEstimate(flops=flops, bytes_accessed=moved, transcendentals=0),
        )(*ins)

    def array(shape, kind):
        return jax.ShapeDtypeStruct(shape, kind)

    def add_product(pieces, places, total=None, cost=1):
        extra = [] if total is None else [total]
        return call(
            functools.partial(project, len(pieces), places),
            array((CORES * rows, 2 * HEAD), f32),
            [tok_own, tok_other, *pieces, *extra],
            VMEM, [VMEM] * (2 + len(pieces) + len(extra)),
            flops=rows * HEAD * cost,
        )

    def along_z(x, mask):
        return flip(x, "seq", blocks, CORES * mask)

    def near(*offsets):
        return functools.partial(places_near, shard, offsets)

    tok_other = flip(tok_own, "seq", blocks, 1)
    width = w_out.shape[1]
    quarter, narrow = shard // 4, width // 4
    grid = n == 4 and blocks % (4 * CORES) == 0 and shard % 512 == 0 and width % 512 == 0
    cut_params = dict(scratch=[pltpu.SemaphoreType.DMA((16,))], limit=CUT_LIMIT)

    def second_cut():
        return call(
            cut_second,
            [array((shard, HEAD), bf16)] + [array((HEAD, width), bf16)] * 2,
            [w_qkv, w_out], [VMEM] * 3, [HBM] * 2, **cut_params,
        )

    if grid:
        part, own_kv = call(
            cut_first,
            [array((3 * quarter + narrow, HEAD), bf16), array((shard, 2 * HEAD), bf16)],
            [w_qkv, w_out], [VMEM] * 2, [HBM] * 2,
            scratch=[pltpu.SemaphoreType.DMA((16,))], limit=FIRST_LIMIT,
        )
        part = flip(part, "dp", n, 3)
        far_kv, far_qo = [part[: 2 * quarter]], [part[2 * quarter :]]
        x_kv = flip(own_kv, "dp", n, 1)
        y_kv = flip(own_kv, "dp", n, 2)
        far_kv += [along_z(far_kv[0], 2), along_z(far_kv[0], 1)]
        far_qo += [along_z(far_qo[0], 2), along_z(far_qo[0], 1)]
        own_q, own_mine, own_theirs = second_cut()
        here, own = lax.optimization_barrier((far_kv[0], own_kv))
        total = add_product([own], near(0), cost=1000000)
        passed, total = lax.optimization_barrier((far_kv[1], total))
        far_kv.append(along_z(passed, 1))
        far_qo.append(along_z(far_qo[1], 1))
        send_q, total = lax.optimization_barrier((own_q, total))
        x_q = flip(send_q, "dp", n, 1)
        y_q = flip(send_q, "dp", n, 2)
        total = add_product(
            [x_kv, y_kv, *far_kv[:3]], lambda: places_near(shard, (1, 2)) + places_far(shard)[:3], total
        )
        pieces, places = far_kv[3:], lambda: places_far(shard)[3:]
        query_pieces, query_mixed = [own_q, x_q, y_q, *far_qo], 4
        query_places = lambda: places_near(shard, (0, 1, 2)) + places_far(shard)
    else:
        own_kv = call(
            cut_keys, [array((shard, 2 * HEAD), bf16)], [w_qkv], [VMEM], [HBM], **cut_params
        )[0]
        own_q, own_mine, own_theirs = second_cut()
        pieces, places = [lax.all_gather(own_kv, "dp", axis=0, tiled=True)], lambda: [0]
        query_pieces, query_mixed = [lax.all_gather(own_q, "dp", axis=0, tiled=True)], 0
        query_places = lambda: [0]
        total = None
    extra = [] if total is None else [total]

    keys, values, state, chip = call(
        functools.partial(project_states, len(pieces), places),
        [
            array((CORES, rows, HEAD), bf16),
            array((CORES, rows, HEAD), bf16),
            array((CORES, HEAD, HEAD), f32),
            array((HEAD, HEAD), bf16),
        ],
        [tok_own, tok_other, *pieces, *extra],
        [VMEM] * 4, [VMEM] * (2 + len(pieces) + len(extra)),
        flops=rows * HEAD,
    )

    got, group = [], chip
    for step in range((blocks // CORES).bit_length() - 1):
        if got:
            group = (group.astype(f32) + got[-1].astype(f32)).astype(bf16)
            if grid:
                group, x_q, y_q = lax.optimization_barrier((group, x_q, y_q))
        got.append(along_z(group, 1 << step))
    if grid:
        query_pieces[1:3] = [x_q, y_q]
        sent, chip = lax.optimization_barrier((own_mine, chip))
        out_x = flip(sent, "dp", n, 1)
        out_y = flip(sent, "dp", n, 2)

    outs = [array((CORES, rows, HEAD), bf16), array((CORES, rows, HEAD), f32)]
    if query_mixed:
        outs.append(array((HEAD, width), bf16))
    query, intra, *columns = call(
        functools.partial(project_queries, len(query_pieces), query_mixed, query_places),
        outs, [tok_own, tok_other, keys, values, *query_pieces],
        [VMEM] * len(outs), [VMEM] * (4 + len(query_pieces)),
        flops=rows * HEAD,
    )
    normed_own, normed_other = call(
        functools.partial(normalise, len(got)),
        [array((rows, HEAD), bf16)] * 2,
        [query, state, intra, norm_gain.reshape(heads, HEAD), *got],
        [VMEM] * 2, [VMEM] * (4 + len(got)),
    )
    normed_got = flip(normed_other, "seq", blocks, 1)

    if grid:
        out_x, out_y, normed_other = lax.optimization_barrier((out_x, out_y, normed_other))
        mine = [own_mine, out_x, out_y, *columns]
        theirs = [own_theirs] + [flip(piece, "seq", blocks, 1) for piece in mine[1:]]
        places = functools.partial(places_out, width)
    else:
        mine = [lax.all_gather(own_mine, "dp", axis=1, tiled=True)]
        theirs = [flip(mine[0], "seq", blocks, 1)]
        places = lambda: [0]
    mixed = call(
        functools.partial(mix, len(mine), places),
        array((rows, n * width), bf16),
        [normed_own, normed_got, *mine, *theirs],
        HBM, [VMEM] * (2 + 2 * len(mine)),
        scratch=[pltpu.VMEM((rows, n * width), bf16), pltpu.SemaphoreType.DMA((16,))],
        flops=2 * rows * 2 * HEAD * n * width, moved=2 * rows * n * width,
    )
    return mixed[None]


def solution(mesh):
    n, blocks = mesh.shape["dp"], mesh.shape["seq"]
    return jax.shard_map(
        functools.partial(shards, n, blocks),
        mesh=mesh,
        in_specs=(P("dp", "seq", None), P("dp", None), P(), P(None, "dp")),
        out_specs=P("dp", "seq", None),
        check_vma=False,
    )
```

```python
import functools

import jax
import jax.numpy as jnp
from jax import lax
from jax.experimental import pallas as pl
from jax.experimental.pallas import tpu as pltpu
from jax.sharding import PartitionSpec as P

HEAD = 128
CORES = 2
VMEM_LIMIT = 24 * 1024 * 1024
CUT_LIMIT = 52 * 1024 * 1024
VMEM = pl.BlockSpec(memory_space=pltpu.VMEM)
HBM = pl.BlockSpec(memory_space=pltpu.HBM)


def flip(x, axis, size, mask):
    return lax.ppermute(x, axis, [(i, i ^ mask) for i in range(size)])


def dot(a, b, contract=((1,), (0,))):
    return lax.dot_general(a, b, (contract, ((), ())), preferred_element_type=jnp.float32)


def position():
    return lax.axis_index("dp"), lax.rem(lax.axis_index("seq"), CORES)


def quarter_of():
    return lax.rem(lax.axis_index("seq") // CORES, 4)


def cut_qkv(w_qkv, own, *refs):
    parts, sem = refs[:-1], refs[-1]
    _, core = position()
    feat = w_qkv.shape[1] // 3
    copies = []
    for j in range(3):
        cols = pl.ds(pl.multiple_of(j * feat + core * HEAD, HEAD), HEAD)
        target = own.at[:, j * HEAD : (j + 1) * HEAD]
        copies.append(pltpu.make_async_copy(w_qkv.at[:, cols], target, sem.at[j]))
        copies[-1].start()
    for copy in copies:
        copy.wait()
    for part in parts:
        quarter = part.shape[0]
        part[...] = own[pl.ds(pl.multiple_of(quarter_of() * quarter, quarter), quarter), :]


def cut_out(w_out, mine, theirs):
    _, core = position()
    for out, head in ((mine, core), (theirs, 1 - core)):
        out[...] = w_out[pl.ds(pl.multiple_of(head * HEAD, HEAD), HEAD), :]


def product(tok_a, tok_b, pieces, places):
    cols = [
        pl.ds(pl.multiple_of(place, 128), piece.shape[0]) for piece, place in zip(pieces, places)
    ]
    tok = jnp.concatenate(
        [jnp.concatenate([ref[:, c] for c in cols], axis=1) for ref in (tok_a, tok_b)], axis=0
    )
    weights = jnp.concatenate([piece[...] for piece in pieces], axis=0)
    return dot(tok, weights)


def places_near(shard, offsets):
    at = lax.axis_index("dp")
    return [(at ^ offset) * shard for offset in offsets]


def places_far(shard):
    start = places_near(shard, (3,))[0]
    mine = quarter_of()
    return [start + (mine ^ mask) * (shard // 4) for mask in (0, 2, 1, 3)]


def project(count, places, tok_a, tok_b, *refs):
    pieces, before, total = refs[:count], refs[count:-1], refs[-1]
    term = product(tok_a, tok_b, pieces, places())
    total[...] = before[0][...] + term if before else term


def project_states(count, places, tok_a, tok_b, *refs):
    pieces, before = refs[:count], refs[count:-4]
    act_out, value_out, state_out, chip_out = refs[-4:]
    proj = product(tok_a, tok_b, pieces, places())
    if before:
        proj = before[0][...] + proj
    rows = value_out.shape[1]
    chip = None
    for b in range(CORES):
        part = proj[b * rows : (b + 1) * rows, :]
        act = part[:, : 2 * HEAD]
        act = (act / (1.0 + jnp.exp(-act))).astype(jnp.bfloat16)
        values = part[:, 2 * HEAD :].astype(jnp.bfloat16)
        state = dot(act[:, HEAD:], values, ((0,), (0,)))
        chip = state if chip is None else chip + state
        act_out[b] = act
        value_out[b] = values
        state_out[b] = state
    chip_out[...] = chip.astype(jnp.bfloat16)


def attend(act, values, intra_out):
    rows = intra_out.shape[1]
    row = lax.broadcasted_iota(jnp.int32, (rows, rows), 0)
    col = lax.broadcasted_iota(jnp.int32, (rows, rows), 1)
    for b in range(CORES):
        scores = dot(act[b, :, :HEAD], act[b, :, HEAD:], ((1,), (1,)))
        scores = jnp.where(row >= col, scores, 0.0).astype(jnp.bfloat16)
        intra_out[b] = dot(scores, values[b])


def normalise(steps, act, state, intra, gain, *refs):
    got, (own_out, other_out) = refs[:steps], refs[steps:]
    _, core = position()
    chip_at = lax.axis_index("seq") // CORES
    base = jnp.zeros((HEAD, HEAD), jnp.float32)
    for step, ref in enumerate(got):
        base = base + jnp.where((chip_at >> step) % 2 == 1, ref[...].astype(jnp.float32), 0.0)
    odd = core == 1
    own_prefix = jnp.where(odd, base + state[1], base)
    other_prefix = jnp.where(odd, base, base + state[0])
    scale = gain[pl.ds(core, 1), :]
    for b, (prefix, out) in enumerate(((own_prefix, own_out), (other_prefix, other_out))):
        attended = dot(act[b, :, :HEAD], prefix.astype(jnp.bfloat16)) + intra[b]
        meansq = jnp.mean(attended * attended, axis=-1, keepdims=True)
        out[...] = (attended * lax.rsqrt(meansq + 1e-06) * scale).astype(jnp.bfloat16)


def mix(count, places, own, other, *refs):
    mine, theirs, (out, stage, sem) = refs[:count], refs[count : 2 * count], refs[2 * count :]
    normed = jnp.concatenate([own[...], other[...]], axis=1)
    copies = []
    slot = 0
    for my_rows, their_rows, place in zip(mine, theirs, places()):
        width = my_rows.shape[1]
        step = min(width, 512)
        for at_col in range(0, width, step):
            part = slice(at_col, at_col + step)
            weights = jnp.concatenate([my_rows[:, part], their_rows[:, part]], axis=0)
            here = stage.at[:, slot : slot + step]
            here[...] = dot(normed, weights).astype(jnp.bfloat16)
            cols = pl.ds(pl.multiple_of(place + at_col, 128), step)
            copies.append(pltpu.make_async_copy(here, out.at[:, cols], sem.at[len(copies)]))
            copies[-1].start()
            slot += step
    for copy in copies:
        copy.wait()


def places_out(width):
    at = lax.axis_index("dp")
    return [(at ^ offset) * width for offset in range(4)]


def shards(n, blocks, tokens, w_qkv, norm_gain, w_out):
    tok_own = tokens[0]
    rows, depth = tok_own.shape
    shard = w_qkv.shape[0]
    heads = norm_gain.shape[0] // HEAD
    bf16, f32 = jnp.bfloat16, jnp.float32

    def call(kernel, outs, ins, out_specs, in_specs, scratch=(), flops=0, moved=0, limit=VMEM_LIMIT):
        return pl.pallas_call(
            kernel,
            out_shape=outs,
            in_specs=in_specs,
            out_specs=out_specs,
            scratch_shapes=scratch,
            compiler_params=pltpu.CompilerParams(vmem_limit_bytes=limit),
            cost_estimate=pl.CostEstimate(flops=flops, bytes_accessed=moved, transcendentals=0),
        )(*ins)

    def array(shape, kind):
        return jax.ShapeDtypeStruct(shape, kind)

    def add_product(pieces, places, total=None):
        extra = [] if total is None else [total]
        return call(
            functools.partial(project, len(pieces), places),
            array((CORES * rows, 3 * HEAD), f32),
            [tok_own, tok_other, *pieces, *extra],
            VMEM, [VMEM] * (2 + len(pieces) + len(extra)),
            flops=rows * HEAD * (1 if total is not None else 1000000),
        )

    tok_other = flip(tok_own, "seq", blocks, 1)
    width = w_out.shape[1]
    grid = n == 4 and blocks % (4 * CORES) == 0 and shard % 512 == 0 and width % 256 == 0

    def cut(*sizes):
        return call(
            cut_qkv,
            [array((size, 3 * HEAD), bf16) for size in sizes],
            [w_qkv], [VMEM] * len(sizes), [HBM],
            scratch=[pltpu.SemaphoreType.DMA((3,))], limit=CUT_LIMIT,
        )

    out_cut = functools.partial(
        call, cut_out, [array((HEAD, width), bf16)] * 2, [w_out], [VMEM] * 2, [VMEM]
    )
    total = None
    if grid:
        quarter = shard // 4
        own, part = cut(shard, quarter)
        far = [flip(part, "dp", n, 3)]
        from_x = flip(own, "dp", n, 1)
        from_y = flip(own, "dp", n, 2)
        far.append(flip(far[0], "seq", blocks, CORES * 2))
        far.append(flip(far[0], "seq", blocks, CORES))
        here, own = lax.optimization_barrier((far[0], own))
        total = add_product([own], functools.partial(places_near, shard, (0,)))
        passed, total = lax.optimization_barrier((far[1], total))
        far.append(flip(passed, "seq", blocks, CORES))
        own_mine, own_theirs = out_cut()
        sent = own_mine
        sent, total, far[1] = lax.optimization_barrier((sent, total, far[1]))
        out_x = flip(sent, "dp", n, 1)
        total = add_product(far[:3], lambda: places_far(shard)[:3], total)
        sent, total = lax.optimization_barrier((sent, total))
        out_y = flip(sent, "dp", n, 2)
        out_d = flip(sent, "dp", n, 3)
        total = add_product([from_x, from_y], functools.partial(places_near, shard, (1, 2)), total)
        pieces, places = far[3:], lambda: places_far(shard)[3:]
    else:
        whole = cut(shard)[0]
        pieces, places = [lax.all_gather(whole, "dp", axis=0, tiled=True)], lambda: [0]
    extra = [] if total is None else [total]

    act, values, state, chip = call(
        functools.partial(project_states, len(pieces), places),
        [
            array((CORES, rows, 2 * HEAD), bf16),
            array((CORES, rows, HEAD), bf16),
            array((CORES, HEAD, HEAD), f32),
            array((HEAD, HEAD), bf16),
        ],
        [tok_own, tok_other, *pieces, *extra],
        [VMEM] * 4, [VMEM] * (2 + len(pieces) + len(extra)),
        flops=2 * CORES * rows * sum(piece.shape[0] for piece in pieces) * 3 * HEAD,
    )
    intra = call(
        attend, array((CORES, rows, HEAD), f32), [act, values], VMEM, [VMEM] * 2,
        flops=4 * CORES * rows * rows * HEAD,
    )

    got, group = [], chip
    for step in range((blocks // CORES).bit_length() - 1):
        if got:
            group = (group.astype(f32) + got[-1].astype(f32)).astype(bf16)
            if grid:
                group, out_x, out_y = lax.optimization_barrier((group, out_x, out_y))
        got.append(flip(group, "seq", blocks, CORES << step))
    if grid:
        their_x = flip(out_x, "seq", blocks, 1)
        their_y = flip(out_y, "seq", blocks, 1)
    normed_own, normed_other = call(
        functools.partial(normalise, len(got)),
        [array((rows, HEAD), bf16)] * 2,
        [act, state, intra, norm_gain.reshape(heads, HEAD), *got],
        [VMEM] * 2, [VMEM] * (4 + len(got)),
    )
    normed_got = flip(normed_other, "seq", blocks, 1)

    if grid:
        out_d, normed_other = lax.optimization_barrier((out_d, normed_other))
        their_d = flip(out_d, "seq", blocks, 1)
        mine = [own_mine, out_x, out_y, out_d]
        theirs = [own_theirs, their_x, their_y, their_d]
        places = functools.partial(places_out, width)
    else:
        mine = [lax.all_gather(out_cut()[0], "dp", axis=1, tiled=True)]
        theirs = [flip(mine[0], "seq", blocks, 1)]
        places = lambda: [0]
    mixed = call(
        functools.partial(mix, len(mine), places),
        array((rows, n * width), bf16),
        [normed_own, normed_got, *mine, *theirs],
        HBM, [VMEM] * (2 + 2 * len(mine)),
        scratch=[pltpu.VMEM((rows, n * width), bf16), pltpu.SemaphoreType.DMA((16,))],
        flops=2 * rows * 2 * HEAD * n * width, moved=2 * rows * n * width,
    )
    return mixed[None]


def solution(mesh):
    n, blocks = mesh.shape["dp"], mesh.shape["seq"]
    return jax.shard_map(
        functools.partial(shards, n, blocks),
        mesh=mesh,
        in_specs=(P("dp", "seq", None), P("dp", None), P(), P(None, "dp")),
        out_specs=P("dp", "seq", None),
        check_vma=False,
    )
```

```python
import functools

import jax
import jax.numpy as jnp
from jax import lax
from jax.experimental import pallas as pl
from jax.experimental.pallas import tpu as pltpu
from jax.sharding import PartitionSpec as P

HEAD = 128
CORES = 2
VMEM_LIMIT = 24 * 1024 * 1024
FIRST_LIMIT = 53 * 1024 * 1024
CUT_LIMIT = 52 * 1024 * 1024
VMEM = pl.BlockSpec(memory_space=pltpu.VMEM)
HBM = pl.BlockSpec(memory_space=pltpu.HBM)


def flip(x, axis, size, mask):
    return lax.ppermute(x, axis, [(i, i ^ mask) for i in range(size)])


def dot(a, b, contract=((1,), (0,))):
    return lax.dot_general(a, b, (contract, ((), ())), preferred_element_type=jnp.float32)


def position():
    return lax.axis_index("dp"), lax.rem(lax.axis_index("seq"), CORES)


def quarter_of():
    return lax.rem(lax.axis_index("seq") // CORES, 4)


def cut_qkv(first, w_qkv, out, sem):
    _, core = position()
    feat = w_qkv.shape[1] // 3
    rows = pl.ds(pl.multiple_of(first(), 16), out.shape[0])
    copies = []
    for j in range(3):
        cols = pl.ds(pl.multiple_of(j * feat + core * HEAD, HEAD), HEAD)
        target = out.at[:, j * HEAD : (j + 1) * HEAD]
        copies.append(pltpu.make_async_copy(w_qkv.at[rows, cols], target, sem.at[j]))
        copies[-1].start()
    for copy in copies:
        copy.wait()


def cut_out(w_out, mine, theirs):
    _, core = position()
    for out, head in ((mine, core), (theirs, 1 - core)):
        out[...] = w_out[pl.ds(pl.multiple_of(head * HEAD, HEAD), HEAD), :]


def product(tok_a, tok_b, pieces, places):
    cols = [
        pl.ds(pl.multiple_of(place, 128), piece.shape[0]) for piece, place in zip(pieces, places)
    ]
    tok = jnp.concatenate(
        [jnp.concatenate([ref[:, c] for c in cols], axis=1) for ref in (tok_a, tok_b)], axis=0
    )
    weights = jnp.concatenate([piece[...] for piece in pieces], axis=0)
    return dot(tok, weights)


def places_near(shard, offsets):
    at = lax.axis_index("dp")
    return [(at ^ offset) * shard for offset in offsets]


def places_far(shard):
    start = places_near(shard, (3,))[0]
    mine = quarter_of()
    return [start + (mine ^ mask) * (shard // 4) for mask in (0, 2, 1, 3)]


def project(count, places, tok_a, tok_b, *refs):
    pieces, before, total = refs[:count], refs[count:-1], refs[-1]
    term = product(tok_a, tok_b, pieces, places())
    total[...] = before[0][...] + term if before else term


def project_states(count, places, tok_a, tok_b, *refs):
    pieces, before = refs[:count], refs[count:-4]
    act_out, value_out, state_out, chip_out = refs[-4:]
    proj = product(tok_a, tok_b, pieces, places())
    if before:
        proj = before[0][...] + proj
    rows = value_out.shape[1]
    chip = None
    for b in range(CORES):
        part = proj[b * rows : (b + 1) * rows, :]
        act = part[:, : 2 * HEAD]
        act = (act / (1.0 + jnp.exp(-act))).astype(jnp.bfloat16)
        values = part[:, 2 * HEAD :].astype(jnp.bfloat16)
        state = dot(act[:, HEAD:], values, ((0,), (0,)))
        chip = state if chip is None else chip + state
        act_out[b] = act
        value_out[b] = values
        state_out[b] = state
    chip_out[...] = chip.astype(jnp.bfloat16)


def attend(act, values, intra_out):
    rows = intra_out.shape[1]
    row = lax.broadcasted_iota(jnp.int32, (rows, rows), 0)
    col = lax.broadcasted_iota(jnp.int32, (rows, rows), 1)
    for b in range(CORES):
        scores = dot(act[b, :, :HEAD], act[b, :, HEAD:], ((1,), (1,)))
        scores = jnp.where(row >= col, scores, 0.0).astype(jnp.bfloat16)
        intra_out[b] = dot(scores, values[b])


def normalise(steps, act, state, intra, gain, *refs):
    got, (own_out, other_out) = refs[:steps], refs[steps:]
    _, core = position()
    chip_at = lax.axis_index("seq") // CORES
    base = jnp.zeros((HEAD, HEAD), jnp.float32)
    for step, ref in enumerate(got):
        base = base + jnp.where((chip_at >> step) % 2 == 1, ref[...].astype(jnp.float32), 0.0)
    odd = core == 1
    own_prefix = jnp.where(odd, base + state[1], base)
    other_prefix = jnp.where(odd, base, base + state[0])
    scale = gain[pl.ds(core, 1), :]
    for b, (prefix, out) in enumerate(((own_prefix, own_out), (other_prefix, other_out))):
        attended = dot(act[b, :, :HEAD], prefix.astype(jnp.bfloat16)) + intra[b]
        meansq = jnp.mean(attended * attended, axis=-1, keepdims=True)
        out[...] = (attended * lax.rsqrt(meansq + 1e-06) * scale).astype(jnp.bfloat16)


def mix(count, places, own, other, *refs):
    mine, theirs, (out, stage, sem) = refs[:count], refs[count : 2 * count], refs[2 * count :]
    normed = jnp.concatenate([own[...], other[...]], axis=1)
    copies = []
    slot = 0
    for my_rows, their_rows, place in zip(mine, theirs, places()):
        width = my_rows.shape[1]
        step = min(width, 512)
        for at_col in range(0, width, step):
            part = slice(at_col, at_col + step)
            weights = jnp.concatenate([my_rows[:, part], their_rows[:, part]], axis=0)
            here = stage.at[:, slot : slot + step]
            here[...] = dot(normed, weights).astype(jnp.bfloat16)
            cols = pl.ds(pl.multiple_of(place + at_col, 128), step)
            copies.append(pltpu.make_async_copy(here, out.at[:, cols], sem.at[len(copies)]))
            copies[-1].start()
            slot += step
    for copy in copies:
        copy.wait()


def places_out(width):
    at = lax.axis_index("dp")
    return [(at ^ offset) * width for offset in range(4)]


def shards(n, blocks, tokens, w_qkv, norm_gain, w_out):
    tok_own = tokens[0]
    rows, depth = tok_own.shape
    shard = w_qkv.shape[0]
    heads = norm_gain.shape[0] // HEAD
    bf16, f32 = jnp.bfloat16, jnp.float32

    def call(kernel, outs, ins, out_specs, in_specs, scratch=(), flops=0, moved=0, limit=VMEM_LIMIT):
        return pl.pallas_call(
            kernel,
            out_shape=outs,
            in_specs=in_specs,
            out_specs=out_specs,
            scratch_shapes=scratch,
            compiler_params=pltpu.CompilerParams(vmem_limit_bytes=limit),
            cost_estimate=pl.CostEstimate(flops=flops, bytes_accessed=moved, transcendentals=0),
        )(*ins)

    def array(shape, kind):
        return jax.ShapeDtypeStruct(shape, kind)

    def add_product(pieces, places, total=None):
        extra = [] if total is None else [total]
        return call(
            functools.partial(project, len(pieces), places),
            array((CORES * rows, 3 * HEAD), f32),
            [tok_own, tok_other, *pieces, *extra],
            VMEM, [VMEM] * (2 + len(pieces) + len(extra)),
            flops=rows * HEAD * (1 if total is not None else 1000000),
        )

    tok_other = flip(tok_own, "seq", blocks, 1)
    width = w_out.shape[1]
    grid = n == 4 and blocks % (4 * CORES) == 0 and shard % 512 == 0 and width % 256 == 0

    def cut(first, size, limit):
        return call(
            functools.partial(cut_qkv, first), array((size, 3 * HEAD), bf16), [w_qkv], VMEM, [HBM],
            scratch=[pltpu.SemaphoreType.DMA((3,))], limit=limit,
        )

    out_cut = functools.partial(
        call, cut_out, [array((HEAD, width), bf16)] * 2, [w_out], [VMEM] * 2, [VMEM]
    )
    total = None
    if grid:
        quarter = shard // 4
        part = cut(lambda: quarter_of() * quarter, quarter, FIRST_LIMIT)
        far = [flip(part, "dp", n, 3)]
        own = cut(lambda: 0, shard, CUT_LIMIT)
        from_x = flip(own, "dp", n, 1)
        from_y = flip(own, "dp", n, 2)
        far.append(flip(far[0], "seq", blocks, CORES * 2))
        far.append(flip(far[0], "seq", blocks, CORES))
        here, own = lax.optimization_barrier((far[0], own))
        total = add_product([own], functools.partial(places_near, shard, (0,)))
        passed, total = lax.optimization_barrier((far[1], total))
        far.append(flip(passed, "seq", blocks, CORES))
        own_mine, own_theirs = out_cut()
        sent = own_mine
        sent, total, far[1] = lax.optimization_barrier((sent, total, far[1]))
        out_x = flip(sent, "dp", n, 1)
        total = add_product(far[:3], lambda: places_far(shard)[:3], total)
        sent, total = lax.optimization_barrier((sent, total))
        out_y = flip(sent, "dp", n, 2)
        out_d = flip(sent, "dp", n, 3)
        total = add_product([from_x, from_y], functools.partial(places_near, shard, (1, 2)), total)
        pieces, places = far[3:], lambda: places_far(shard)[3:]
    else:
        whole = cut(lambda: 0, shard, CUT_LIMIT)
        pieces, places = [lax.all_gather(whole, "dp", axis=0, tiled=True)], lambda: [0]
    extra = [] if total is None else [total]

    act, values, state, chip = call(
        functools.partial(project_states, len(pieces), places),
        [
            array((CORES, rows, 2 * HEAD), bf16),
            array((CORES, rows, HEAD), bf16),
            array((CORES, HEAD, HEAD), f32),
            array((HEAD, HEAD), bf16),
        ],
        [tok_own, tok_other, *pieces, *extra],
        [VMEM] * 4, [VMEM] * (2 + len(pieces) + len(extra)),
        flops=2 * CORES * rows * sum(piece.shape[0] for piece in pieces) * 3 * HEAD,
    )
    intra = call(
        attend, array((CORES, rows, HEAD), f32), [act, values], VMEM, [VMEM] * 2,
        flops=4 * CORES * rows * rows * HEAD,
    )

    got, group = [], chip
    for step in range((blocks // CORES).bit_length() - 1):
        if got:
            group = (group.astype(f32) + got[-1].astype(f32)).astype(bf16)
            if grid:
                group, out_x, out_y = lax.optimization_barrier((group, out_x, out_y))
        got.append(flip(group, "seq", blocks, CORES << step))
    if grid:
        their_x = flip(out_x, "seq", blocks, 1)
        their_y = flip(out_y, "seq", blocks, 1)
    normed_own, normed_other = call(
        functools.partial(normalise, len(got)),
        [array((rows, HEAD), bf16)] * 2,
        [act, state, intra, norm_gain.reshape(heads, HEAD), *got],
        [VMEM] * 2, [VMEM] * (4 + len(got)),
    )
    normed_got = flip(normed_other, "seq", blocks, 1)

    if grid:
        out_d, normed_other = lax.optimization_barrier((out_d, normed_other))
        their_d = flip(out_d, "seq", blocks, 1)
        mine = [own_mine, out_x, out_y, out_d]
        theirs = [own_theirs, their_x, their_y, their_d]
        places = functools.partial(places_out, width)
    else:
        mine = [lax.all_gather(out_cut()[0], "dp", axis=1, tiled=True)]
        theirs = [flip(mine[0], "seq", blocks, 1)]
        places = lambda: [0]
    mixed = call(
        functools.partial(mix, len(mine), places),
        array((rows, n * width), bf16),
        [normed_own, normed_got, *mine, *theirs],
        HBM, [VMEM] * (2 + 2 * len(mine)),
        scratch=[pltpu.VMEM((rows, n * width), bf16), pltpu.SemaphoreType.DMA((16,))],
        flops=2 * rows * 2 * HEAD * n * width, moved=2 * rows * n * width,
    )
    return mixed[None]


def solution(mesh):
    n, blocks = mesh.shape["dp"], mesh.shape["seq"]
    return jax.shard_map(
        functools.partial(shards, n, blocks),
        mesh=mesh,
        in_specs=(P("dp", "seq", None), P("dp", None), P(), P(None, "dp")),
        out_specs=P("dp", "seq", None),
        check_vma=False,
    )
```

```python
import functools

import jax
import jax.numpy as jnp
from jax import lax
from jax.experimental import pallas as pl
from jax.experimental.pallas import tpu as pltpu
from jax.sharding import PartitionSpec as P

HEAD = 128
CORES = 2
VMEM_LIMIT = 24 * 1024 * 1024
FIRST_LIMIT = 53 * 1024 * 1024
CUT_LIMIT = 52 * 1024 * 1024
VMEM = pl.BlockSpec(memory_space=pltpu.VMEM)
HBM = pl.BlockSpec(memory_space=pltpu.HBM)


def flip(x, axis, size, mask):
    return lax.ppermute(x, axis, [(i, i ^ mask) for i in range(size)])


def dot(a, b, contract=((1,), (0,))):
    return lax.dot_general(a, b, (contract, ((), ())), preferred_element_type=jnp.float32)


def position():
    return lax.axis_index("dp"), lax.rem(lax.axis_index("seq"), CORES)


def parity():
    return lax.rem(lax.axis_index("seq") // CORES, 2)


def quarter_of():
    return lax.rem(lax.axis_index("seq") // CORES, 4)


def cut_qkv(first, w_qkv, out, sem):
    _, core = position()
    feat = w_qkv.shape[1] // 3
    rows = pl.ds(pl.multiple_of(first(), 16), out.shape[0])
    copies = []
    for j in range(3):
        cols = pl.ds(pl.multiple_of(j * feat + core * HEAD, HEAD), HEAD)
        target = out.at[:, j * HEAD : (j + 1) * HEAD]
        copies.append(pltpu.make_async_copy(w_qkv.at[rows, cols], target, sem.at[j]))
        copies[-1].start()
    for copy in copies:
        copy.wait()


def cut_out(w_out, mine, theirs, part):
    _, core = position()
    rows = pl.ds(pl.multiple_of(core * HEAD, HEAD), HEAD)
    other = pl.ds(pl.multiple_of((1 - core) * HEAD, HEAD), HEAD)
    mine[...] = w_out[rows, :]
    theirs[...] = w_out[other, :]
    half = part.shape[1]
    part[...] = w_out[rows, pl.ds(pl.multiple_of(parity() * half, half), half)]


def product(tok_a, tok_b, pieces, places):
    cols = [
        pl.ds(pl.multiple_of(place, 128), piece.shape[0]) for piece, place in zip(pieces, places)
    ]
    tok = jnp.concatenate(
        [jnp.concatenate([ref[:, c] for c in cols], axis=1) for ref in (tok_a, tok_b)], axis=0
    )
    weights = jnp.concatenate([piece[...] for piece in pieces], axis=0)
    return dot(tok, weights)


def places_near(shard, offsets):
    at = lax.axis_index("dp")
    return [(at ^ offset) * shard for offset in offsets]


def places_far(shard):
    start = places_near(shard, (3,))[0]
    mine = quarter_of()
    return [start + (mine ^ mask) * (shard // 4) for mask in (0, 2, 1, 3)]


def project(count, places, tok_a, tok_b, *refs):
    pieces, before, total = refs[:count], refs[count:-1], refs[-1]
    term = product(tok_a, tok_b, pieces, places())
    total[...] = before[0][...] + term if before else term


def project_states(count, places, tok_a, tok_b, *refs):
    pieces, before = refs[:count], refs[count:-4]
    act_out, value_out, state_out, chip_out = refs[-4:]
    proj = product(tok_a, tok_b, pieces, places())
    if before:
        proj = before[0][...] + proj
    rows = value_out.shape[1]
    chip = None
    for b in range(CORES):
        part = proj[b * rows : (b + 1) * rows, :]
        act = part[:, : 2 * HEAD]
        act = (act / (1.0 + jnp.exp(-act))).astype(jnp.bfloat16)
        values = part[:, 2 * HEAD :].astype(jnp.bfloat16)
        state = dot(act[:, HEAD:], values, ((0,), (0,)))
        chip = state if chip is None else chip + state
        act_out[b] = act
        value_out[b] = values
        state_out[b] = state
    chip_out[...] = chip.astype(jnp.bfloat16)


def attend(act, values, *refs):
    if len(refs) > 1:
        own_half, other_half, intra_out, columns_out = refs
        half = own_half.shape[1]
        columns_out[:, pl.ds(pl.multiple_of(parity() * half, half), half)] = own_half[...]
        columns_out[:, pl.ds(pl.multiple_of((1 - parity()) * half, half), half)] = other_half[...]
    else:
        intra_out = refs[0]
    rows = intra_out.shape[1]
    row = lax.broadcasted_iota(jnp.int32, (rows, rows), 0)
    col = lax.broadcasted_iota(jnp.int32, (rows, rows), 1)
    for b in range(CORES):
        scores = dot(act[b, :, :HEAD], act[b, :, HEAD:], ((1,), (1,)))
        scores = jnp.where(row >= col, scores, 0.0).astype(jnp.bfloat16)
        intra_out[b] = dot(scores, values[b])


def normalise(steps, act, state, intra, gain, *refs):
    got, (own_out, other_out) = refs[:steps], refs[steps:]
    _, core = position()
    chip_at = lax.axis_index("seq") // CORES
    base = jnp.zeros((HEAD, HEAD), jnp.float32)
    for step, ref in enumerate(got):
        base = base + jnp.where((chip_at >> step) % 2 == 1, ref[...].astype(jnp.float32), 0.0)
    odd = core == 1
    own_prefix = jnp.where(odd, base + state[1], base)
    other_prefix = jnp.where(odd, base, base + state[0])
    scale = gain[pl.ds(core, 1), :]
    for b, (prefix, out) in enumerate(((own_prefix, own_out), (other_prefix, other_out))):
        attended = dot(act[b, :, :HEAD], prefix.astype(jnp.bfloat16)) + intra[b]
        meansq = jnp.mean(attended * attended, axis=-1, keepdims=True)
        out[...] = (attended * lax.rsqrt(meansq + 1e-06) * scale).astype(jnp.bfloat16)


def mix(count, places, own, other, *refs):
    mine, theirs, (out, stage, sem) = refs[:count], refs[count : 2 * count], refs[2 * count :]
    normed = jnp.concatenate([own[...], other[...]], axis=1)
    copies = []
    slot = 0
    for my_rows, their_rows, place in zip(mine, theirs, places()):
        width = my_rows.shape[1]
        step = min(width, 512)
        for at_col in range(0, width, step):
            part = slice(at_col, at_col + step)
            weights = jnp.concatenate([my_rows[:, part], their_rows[:, part]], axis=0)
            here = stage.at[:, slot : slot + step]
            here[...] = dot(normed, weights).astype(jnp.bfloat16)
            cols = pl.ds(pl.multiple_of(place + at_col, 128), step)
            copies.append(pltpu.make_async_copy(here, out.at[:, cols], sem.at[len(copies)]))
            copies[-1].start()
            slot += step
    for copy in copies:
        copy.wait()


def places_out(width):
    at = lax.axis_index("dp")
    return [(at ^ offset) * width for offset in range(4)]


def shards(n, blocks, tokens, w_qkv, norm_gain, w_out):
    tok_own = tokens[0]
    rows, depth = tok_own.shape
    shard = w_qkv.shape[0]
    heads = norm_gain.shape[0] // HEAD
    bf16, f32 = jnp.bfloat16, jnp.float32

    def call(kernel, outs, ins, out_specs, in_specs, scratch=(), flops=0, moved=0, limit=VMEM_LIMIT):
        return pl.pallas_call(
            kernel,
            out_shape=outs,
            in_specs=in_specs,
            out_specs=out_specs,
            scratch_shapes=scratch,
            compiler_params=pltpu.CompilerParams(vmem_limit_bytes=limit),
            cost_estimate=pl.CostEstimate(flops=flops, bytes_accessed=moved, transcendentals=0),
        )(*ins)

    def array(shape, kind):
        return jax.ShapeDtypeStruct(shape, kind)

    def add_product(pieces, places, total=None):
        extra = [] if total is None else [total]
        return call(
            functools.partial(project, len(pieces), places),
            array((CORES * rows, 3 * HEAD), f32),
            [tok_own, tok_other, *pieces, *extra],
            VMEM, [VMEM] * (2 + len(pieces) + len(extra)),
            flops=rows * HEAD * (1 if total is not None else 1000000),
        )

    tok_other = flip(tok_own, "seq", blocks, 1)
    width = w_out.shape[1]
    grid = n == 4 and blocks % (4 * CORES) == 0 and shard % 512 == 0 and width % 256 == 0

    def cut(first, size, limit):
        return call(
            functools.partial(cut_qkv, first), array((size, 3 * HEAD), bf16), [w_qkv], VMEM, [HBM],
            scratch=[pltpu.SemaphoreType.DMA((3,))], limit=limit,
        )

    out_cut = functools.partial(
        call, cut_out, [array((HEAD, width), bf16)] * 2 + [array((HEAD, width // 2), bf16)],
        [w_out], [VMEM] * 3, [VMEM]
    )
    total = None
    if grid:
        quarter = shard // 4
        part = cut(lambda: quarter_of() * quarter, quarter, FIRST_LIMIT)
        far = [flip(part, "dp", n, 3)]
        own = cut(lambda: 0, shard, CUT_LIMIT)
        from_x = flip(own, "dp", n, 1)
        from_y = flip(own, "dp", n, 2)
        far.append(flip(far[0], "seq", blocks, CORES * 2))
        far.append(flip(far[0], "seq", blocks, CORES))
        here, own = lax.optimization_barrier((far[0], own))
        total = add_product([own], functools.partial(places_near, shard, (0,)))
        passed, total = lax.optimization_barrier((far[1], total))
        far.append(flip(passed, "seq", blocks, CORES))
        own_mine, own_theirs, own_part = out_cut()
        send_part, total, far[1] = lax.optimization_barrier((own_part, total, far[1]))
        out_d = flip(send_part, "dp", n, 3)
        out_e = flip(out_d, "seq", blocks, CORES)
        sent, total, far[1] = lax.optimization_barrier((own_mine, total, far[1]))
        out_x = flip(sent, "dp", n, 1)
        out_y = flip(sent, "dp", n, 2)
        total = add_product(far[:3], lambda: places_far(shard)[:3], total)
        total = add_product([from_x, from_y], functools.partial(places_near, shard, (1, 2)), total)
        pieces, places = far[3:], lambda: places_far(shard)[3:]
    else:
        whole = cut(lambda: 0, shard, CUT_LIMIT)
        pieces, places = [lax.all_gather(whole, "dp", axis=0, tiled=True)], lambda: [0]
    extra = [] if total is None else [total]

    act, values, state, chip = call(
        functools.partial(project_states, len(pieces), places),
        [
            array((CORES, rows, 2 * HEAD), bf16),
            array((CORES, rows, HEAD), bf16),
            array((CORES, HEAD, HEAD), f32),
            array((HEAD, HEAD), bf16),
        ],
        [tok_own, tok_other, *pieces, *extra],
        [VMEM] * 4, [VMEM] * (2 + len(pieces) + len(extra)),
        flops=2 * CORES * rows * sum(piece.shape[0] for piece in pieces) * 3 * HEAD,
    )
    got, group = [], chip
    for step in range((blocks // CORES).bit_length() - 1):
        if got:
            group = (group.astype(f32) + got[-1].astype(f32)).astype(bf16)
            if grid:
                group, out_d = lax.optimization_barrier((group, out_d))
        got.append(flip(group, "seq", blocks, CORES << step))
    scored, halves, outs = act, [], [array((CORES, rows, HEAD), f32)]
    if grid:
        scored, out_x, out_y = lax.optimization_barrier((act, out_x, out_y))
        halves = [out_d, out_e]
        outs.append(array((HEAD, width), bf16))
    intra, *columns = call(
        attend, outs, [scored, values, *halves], [VMEM] * len(outs), [VMEM] * (2 + len(halves)),
        flops=rows * HEAD * 1000000,
    )
    if grid:
        out_x, out_y, columns[0], got[-1] = lax.optimization_barrier(
            (out_x, out_y, columns[0], got[-1])
        )
        mine = [own_mine, out_x, out_y, *columns]
        theirs = [own_theirs] + [flip(piece, "seq", blocks, 1) for piece in mine[1:]]
    normed_own, normed_other = call(
        functools.partial(normalise, len(got)),
        [array((rows, HEAD), bf16)] * 2,
        [act, state, intra, norm_gain.reshape(heads, HEAD), *got],
        [VMEM] * 2, [VMEM] * (4 + len(got)),
    )
    normed_got = flip(normed_other, "seq", blocks, 1)

    if grid:
        places = functools.partial(places_out, width)
    else:
        mine = [lax.all_gather(out_cut()[0], "dp", axis=1, tiled=True)]
        theirs = [flip(mine[0], "seq", blocks, 1)]
        places = lambda: [0]
    mixed = call(
        functools.partial(mix, len(mine), places),
        array((rows, n * width), bf16),
        [normed_own, normed_got, *mine, *theirs],
        HBM, [VMEM] * (2 + 2 * len(mine)),
        scratch=[pltpu.VMEM((rows, n * width), bf16), pltpu.SemaphoreType.DMA((16,))],
        flops=2 * rows * 2 * HEAD * n * width, moved=2 * rows * n * width,
    )
    return mixed[None]


def solution(mesh):
    n, blocks = mesh.shape["dp"], mesh.shape["seq"]
    return jax.shard_map(
        functools.partial(shards, n, blocks),
        mesh=mesh,
        in_specs=(P("dp", "seq", None), P("dp", None), P(), P(None, "dp")),
        out_specs=P("dp", "seq", None),
        check_vma=False,
    )
```

```python
import functools

import jax
import jax.numpy as jnp
from jax import lax
from jax.experimental import pallas as pl
from jax.experimental.pallas import tpu as pltpu
from jax.sharding import PartitionSpec as P

HEAD = 128
CORES = 2
VMEM_LIMIT = 24 * 1024 * 1024
FIRST_LIMIT = 53 * 1024 * 1024
CUT_LIMIT = 52 * 1024 * 1024
VMEM = pl.BlockSpec(memory_space=pltpu.VMEM)
HBM = pl.BlockSpec(memory_space=pltpu.HBM)


def flip(x, axis, size, mask):
    return lax.ppermute(x, axis, [(i, i ^ mask) for i in range(size)])


def dot(a, b, contract=((1,), (0,))):
    return lax.dot_general(a, b, (contract, ((), ())), preferred_element_type=jnp.float32)


def position():
    return lax.axis_index("dp"), lax.rem(lax.axis_index("seq"), CORES)


def parity():
    return lax.rem(lax.axis_index("seq") // CORES, 2)


def quarter_of():
    return lax.rem(lax.axis_index("seq") // CORES, 4)


def cut_qkv(first, w_qkv, out, sem):
    _, core = position()
    feat = w_qkv.shape[1] // 3
    rows = pl.ds(pl.multiple_of(first(), 16), out.shape[0])
    copies = []
    for j in range(3):
        cols = pl.ds(pl.multiple_of(j * feat + core * HEAD, HEAD), HEAD)
        target = out.at[:, j * HEAD : (j + 1) * HEAD]
        copies.append(pltpu.make_async_copy(w_qkv.at[rows, cols], target, sem.at[j]))
        copies[-1].start()
    for copy in copies:
        copy.wait()


def cut_out(w_out, mine, theirs, part):
    _, core = position()
    rows = pl.ds(pl.multiple_of(core * HEAD, HEAD), HEAD)
    other = pl.ds(pl.multiple_of((1 - core) * HEAD, HEAD), HEAD)
    mine[...] = w_out[rows, :]
    theirs[...] = w_out[other, :]
    half = part.shape[1]
    part[...] = w_out[rows, pl.ds(pl.multiple_of(parity() * half, half), half)]


def product(tok_a, tok_b, pieces, places):
    cols = [
        pl.ds(pl.multiple_of(place, 128), piece.shape[0]) for piece, place in zip(pieces, places)
    ]
    tok = jnp.concatenate(
        [jnp.concatenate([ref[:, c] for c in cols], axis=1) for ref in (tok_a, tok_b)], axis=0
    )
    weights = jnp.concatenate([piece[...] for piece in pieces], axis=0)
    return dot(tok, weights)


def places_near(shard, offsets):
    at = lax.axis_index("dp")
    return [(at ^ offset) * shard for offset in offsets]


def places_far(shard):
    start = places_near(shard, (3,))[0]
    mine = quarter_of()
    return [start + (mine ^ mask) * (shard // 4) for mask in (0, 2, 1, 3)]


def project(count, places, tok_a, tok_b, *refs):
    pieces, before, total = refs[:count], refs[count:-1], refs[-1]
    term = product(tok_a, tok_b, pieces, places())
    total[...] = before[0][...] + term if before else term


def project_states(count, places, tok_a, tok_b, *refs):
    pieces, before = refs[:count], refs[count:-4]
    act_out, value_out, state_out, chip_out = refs[-4:]
    proj = product(tok_a, tok_b, pieces, places())
    if before:
        proj = before[0][...] + proj
    rows = value_out.shape[1]
    chip = None
    for b in range(CORES):
        part = proj[b * rows : (b + 1) * rows, :]
        act = part[:, : 2 * HEAD]
        act = (act / (1.0 + jnp.exp(-act))).astype(jnp.bfloat16)
        values = part[:, 2 * HEAD :].astype(jnp.bfloat16)
        state = dot(act[:, HEAD:], values, ((0,), (0,)))
        chip = state if chip is None else chip + state
        act_out[b] = act
        value_out[b] = values
        state_out[b] = state
    chip_out[...] = chip.astype(jnp.bfloat16)


def attend(act, values, *refs):
    if len(refs) > 1:
        own_half, other_half, intra_out, columns_out = refs
        half = own_half.shape[1]
        columns_out[:, pl.ds(pl.multiple_of(parity() * half, half), half)] = own_half[...]
        columns_out[:, pl.ds(pl.multiple_of((1 - parity()) * half, half), half)] = other_half[...]
    else:
        intra_out = refs[0]
    rows = intra_out.shape[1]
    row = lax.broadcasted_iota(jnp.int32, (rows, rows), 0)
    col = lax.broadcasted_iota(jnp.int32, (rows, rows), 1)
    for b in range(CORES):
        scores = dot(act[b, :, :HEAD], act[b, :, HEAD:], ((1,), (1,)))
        scores = jnp.where(row >= col, scores, 0.0).astype(jnp.bfloat16)
        intra_out[b] = dot(scores, values[b])


def normalise(steps, act, state, intra, gain, *refs):
    got, (own_out, other_out) = refs[:steps], refs[steps:]
    _, core = position()
    chip_at = lax.axis_index("seq") // CORES
    base = jnp.zeros((HEAD, HEAD), jnp.float32)
    for step, ref in enumerate(got):
        base = base + jnp.where((chip_at >> step) % 2 == 1, ref[...].astype(jnp.float32), 0.0)
    odd = core == 1
    own_prefix = jnp.where(odd, base + state[1], base)
    other_prefix = jnp.where(odd, base, base + state[0])
    scale = gain[pl.ds(core, 1), :]
    for b, (prefix, out) in enumerate(((own_prefix, own_out), (other_prefix, other_out))):
        attended = dot(act[b, :, :HEAD], prefix.astype(jnp.bfloat16)) + intra[b]
        meansq = jnp.mean(attended * attended, axis=-1, keepdims=True)
        out[...] = (attended * lax.rsqrt(meansq + 1e-06) * scale).astype(jnp.bfloat16)


def mix(count, places, own, other, *refs):
    mine, theirs, (out, stage, sem) = refs[:count], refs[count : 2 * count], refs[2 * count :]
    normed = jnp.concatenate([own[...], other[...]], axis=1)
    copies = []
    slot = 0
    for my_rows, their_rows, place in zip(mine, theirs, places()):
        width = my_rows.shape[1]
        step = min(width, 512)
        for at_col in range(0, width, step):
            part = slice(at_col, at_col + step)
            weights = jnp.concatenate([my_rows[:, part], their_rows[:, part]], axis=0)
            here = stage.at[:, slot : slot + step]
            here[...] = dot(normed, weights).astype(jnp.bfloat16)
            cols = pl.ds(pl.multiple_of(place + at_col, 128), step)
            copies.append(pltpu.make_async_copy(here, out.at[:, cols], sem.at[len(copies)]))
            copies[-1].start()
            slot += step
    for copy in copies:
        copy.wait()


def places_out(width):
    at = lax.axis_index("dp")
    return [(at ^ offset) * width for offset in range(4)]


def shards(n, blocks, tokens, w_qkv, norm_gain, w_out):
    tok_own = tokens[0]
    rows, depth = tok_own.shape
    shard = w_qkv.shape[0]
    heads = norm_gain.shape[0] // HEAD
    bf16, f32 = jnp.bfloat16, jnp.float32

    def call(kernel, outs, ins, out_specs, in_specs, scratch=(), flops=0, moved=0, limit=VMEM_LIMIT):
        return pl.pallas_call(
            kernel,
            out_shape=outs,
            in_specs=in_specs,
            out_specs=out_specs,
            scratch_shapes=scratch,
            compiler_params=pltpu.CompilerParams(vmem_limit_bytes=limit),
            cost_estimate=pl.CostEstimate(flops=flops, bytes_accessed=moved, transcendentals=0),
        )(*ins)

    def array(shape, kind):
        return jax.ShapeDtypeStruct(shape, kind)

    def add_product(pieces, places, total=None):
        extra = [] if total is None else [total]
        return call(
            functools.partial(project, len(pieces), places),
            array((CORES * rows, 3 * HEAD), f32),
            [tok_own, tok_other, *pieces, *extra],
            VMEM, [VMEM] * (2 + len(pieces) + len(extra)),
            flops=rows * HEAD * (1 if total is not None else 1000000),
        )

    tok_other = flip(tok_own, "seq", blocks, 1)
    width = w_out.shape[1]
    grid = n == 4 and blocks % (4 * CORES) == 0 and shard % 512 == 0 and width % 256 == 0

    def cut(first, size, limit):
        return call(
            functools.partial(cut_qkv, first), array((size, 3 * HEAD), bf16), [w_qkv], VMEM, [HBM],
            scratch=[pltpu.SemaphoreType.DMA((3,))], limit=limit,
        )

    out_cut = functools.partial(
        call, cut_out, [array((HEAD, width), bf16)] * 2 + [array((HEAD, width // 2), bf16)],
        [w_out], [VMEM] * 3, [VMEM]
    )
    total = None
    if grid:
        quarter = shard // 4
        part = cut(lambda: quarter_of() * quarter, quarter, FIRST_LIMIT)
        far = [flip(part, "dp", n, 3)]
        own = cut(lambda: 0, shard, CUT_LIMIT)
        from_x = flip(own, "dp", n, 1)
        from_y = flip(own, "dp", n, 2)
        far.append(flip(far[0], "seq", blocks, CORES * 2))
        far.append(flip(far[0], "seq", blocks, CORES))
        here, own = lax.optimization_barrier((far[0], own))
        total = add_product([own], functools.partial(places_near, shard, (0,)))
        passed, total = lax.optimization_barrier((far[1], total))
        far.append(flip(passed, "seq", blocks, CORES))
        own_mine, own_theirs, own_part = out_cut()
        send_part, total, far[1] = lax.optimization_barrier((own_part, total, far[1]))
        out_d = flip(send_part, "dp", n, 3)
        out_e = flip(out_d, "seq", blocks, CORES)
        sent, total, far[1] = lax.optimization_barrier((own_mine, total, far[1]))
        out_x = flip(sent, "dp", n, 1)
        out_y = flip(sent, "dp", n, 2)
        total = add_product(far[:3], lambda: places_far(shard)[:3], total)
        total = add_product([from_x, from_y], functools.partial(places_near, shard, (1, 2)), total)
        pieces, places = far[3:], lambda: places_far(shard)[3:]
    else:
        whole = cut(lambda: 0, shard, CUT_LIMIT)
        pieces, places = [lax.all_gather(whole, "dp", axis=0, tiled=True)], lambda: [0]
    extra = [] if total is None else [total]

    act, values, state, chip = call(
        functools.partial(project_states, len(pieces), places),
        [
            array((CORES, rows, 2 * HEAD), bf16),
            array((CORES, rows, HEAD), bf16),
            array((CORES, HEAD, HEAD), f32),
            array((HEAD, HEAD), bf16),
        ],
        [tok_own, tok_other, *pieces, *extra],
        [VMEM] * 4, [VMEM] * (2 + len(pieces) + len(extra)),
        flops=2 * CORES * rows * sum(piece.shape[0] for piece in pieces) * 3 * HEAD,
    )
    got, group = [], chip
    for step in range((blocks // CORES).bit_length() - 1):
        if got:
            group = (group.astype(f32) + got[-1].astype(f32)).astype(bf16)
            if grid:
                group, out_d = lax.optimization_barrier((group, out_d))
        got.append(flip(group, "seq", blocks, CORES << step))
    scored, halves, outs = act, [], [array((CORES, rows, HEAD), f32)]
    if grid:
        scored, out_x, out_y = lax.optimization_barrier((act, out_x, out_y))
        halves = [out_d, out_e]
        outs.append(array((HEAD, width), bf16))
    intra, *columns = call(
        attend, outs, [scored, values, *halves], [VMEM] * len(outs), [VMEM] * (2 + len(halves)),
        flops=rows * HEAD * 1000000,
    )
    if grid:
        mine = [own_mine, out_x, out_y, *columns]
        theirs = [own_theirs] + [flip(piece, "seq", blocks, 1) for piece in mine[1:]]
    normed_own, normed_other = call(
        functools.partial(normalise, len(got)),
        [array((rows, HEAD), bf16)] * 2,
        [act, state, intra, norm_gain.reshape(heads, HEAD), *got],
        [VMEM] * 2, [VMEM] * (4 + len(got)), flops=rows * HEAD * 1000000,
    )
    normed_got = flip(normed_other, "seq", blocks, 1)

    if grid:
        places = functools.partial(places_out, width)
    else:
        mine = [lax.all_gather(out_cut()[0], "dp", axis=1, tiled=True)]
        theirs = [flip(mine[0], "seq", blocks, 1)]
        places = lambda: [0]
    mixed = call(
        functools.partial(mix, len(mine), places),
        array((rows, n * width), bf16),
        [normed_own, normed_got, *mine, *theirs],
        HBM, [VMEM] * (2 + 2 * len(mine)),
        scratch=[pltpu.VMEM((rows, n * width), bf16), pltpu.SemaphoreType.DMA((16,))],
        flops=2 * rows * 2 * HEAD * n * width, moved=2 * rows * n * width,
    )
    return mixed[None]


def solution(mesh):
    n, blocks = mesh.shape["dp"], mesh.shape["seq"]
    return jax.shard_map(
        functools.partial(shards, n, blocks),
        mesh=mesh,
        in_specs=(P("dp", "seq", None), P("dp", None), P(), P(None, "dp")),
        out_specs=P("dp", "seq", None),
        check_vma=False,
    )
```

```python
import functools

import jax
import jax.numpy as jnp
from jax import lax
from jax.experimental import pallas as pl
from jax.experimental.pallas import tpu as pltpu
from jax.sharding import PartitionSpec as P

HEAD = 128
CORES = 2
VMEM_LIMIT = 24 * 1024 * 1024
FIRST_LIMIT = 53 * 1024 * 1024
CUT_LIMIT = 52 * 1024 * 1024
VMEM = pl.BlockSpec(memory_space=pltpu.VMEM)
HBM = pl.BlockSpec(memory_space=pltpu.HBM)


def flip(x, axis, size, mask):
    return lax.ppermute(x, axis, [(i, i ^ mask) for i in range(size)])


def dot(a, b, contract=((1,), (0,))):
    return lax.dot_general(a, b, (contract, ((), ())), preferred_element_type=jnp.float32)


def position():
    return lax.axis_index("dp"), lax.rem(lax.axis_index("seq"), CORES)


def parity():
    return lax.rem(lax.axis_index("seq") // CORES, 2)


def quarter_of():
    return lax.rem(lax.axis_index("seq") // CORES, 4)


def cut_qkv(first, w_qkv, out, *refs):
    pieces, sem = refs[:-1], refs[-1]
    _, core = position()
    feat = w_qkv.shape[1] // 3
    rows = pl.ds(pl.multiple_of(first(), 16), out.shape[0])
    copies = []
    for j in range(3):
        cols = pl.ds(pl.multiple_of(j * feat + core * HEAD, HEAD), HEAD)
        target = out.at[:, j * HEAD : (j + 1) * HEAD]
        copies.append(pltpu.make_async_copy(w_qkv.at[rows, cols], target, sem.at[j]))
        copies[-1].start()
    for copy in copies:
        copy.wait()
    at = 0
    for piece in pieces:
        piece[...] = out[at : at + piece.shape[0], :]
        at += piece.shape[0]


def cut_out(w_out, mine, theirs, part):
    _, core = position()
    rows = pl.ds(pl.multiple_of(core * HEAD, HEAD), HEAD)
    other = pl.ds(pl.multiple_of((1 - core) * HEAD, HEAD), HEAD)
    mine[...] = w_out[rows, :]
    theirs[...] = w_out[other, :]
    half = part.shape[1]
    part[...] = w_out[rows, pl.ds(pl.multiple_of(parity() * half, half), half)]


def product(tok_a, tok_b, pieces, places):
    cols = [
        pl.ds(pl.multiple_of(place, 128), piece.shape[0]) for piece, place in zip(pieces, places)
    ]
    tok = jnp.concatenate(
        [jnp.concatenate([ref[:, c] for c in cols], axis=1) for ref in (tok_a, tok_b)], axis=0
    )
    weights = jnp.concatenate([piece[...] for piece in pieces], axis=0)
    return dot(tok, weights)


def places_near(shard, offsets):
    at = lax.axis_index("dp")
    return [(at ^ offset) * shard for offset in offsets]


def places_last(shard):
    near_x, near_y = places_near(shard, (1, 2))
    return [near_x + 3 * (shard // 4), near_y]


def places_far(shard):
    start = places_near(shard, (3,))[0]
    mine = quarter_of()
    return [start + (mine ^ mask) * (shard // 4) for mask in (0, 2, 1, 3)]


def project(count, places, tok_a, tok_b, *refs):
    pieces, before, total = refs[:count], refs[count:-1], refs[-1]
    term = product(tok_a, tok_b, pieces, places())
    total[...] = before[0][...] + term if before else term


def project_states(count, places, tok_a, tok_b, *refs):
    pieces, before = refs[:count], refs[count:-4]
    act_out, value_out, state_out, chip_out = refs[-4:]
    proj = product(tok_a, tok_b, pieces, places())
    if before:
        proj = before[0][...] + proj
    rows = value_out.shape[1]
    chip = None
    for b in range(CORES):
        part = proj[b * rows : (b + 1) * rows, :]
        act = part[:, : 2 * HEAD]
        act = (act / (1.0 + jnp.exp(-act))).astype(jnp.bfloat16)
        values = part[:, 2 * HEAD :].astype(jnp.bfloat16)
        state = dot(act[:, HEAD:], values, ((0,), (0,)))
        chip = state if chip is None else chip + state
        act_out[b] = act
        value_out[b] = values
        state_out[b] = state
    chip_out[...] = chip.astype(jnp.bfloat16)


def attend(act, values, *refs):
    if len(refs) > 1:
        own_half, other_half, intra_out, columns_out = refs
        half = own_half.shape[1]
        columns_out[:, pl.ds(pl.multiple_of(parity() * half, half), half)] = own_half[...]
        columns_out[:, pl.ds(pl.multiple_of((1 - parity()) * half, half), half)] = other_half[...]
    else:
        intra_out = refs[0]
    rows = intra_out.shape[1]
    row = lax.broadcasted_iota(jnp.int32, (rows, rows), 0)
    col = lax.broadcasted_iota(jnp.int32, (rows, rows), 1)
    for b in range(CORES):
        scores = dot(act[b, :, :HEAD], act[b, :, HEAD:], ((1,), (1,)))
        scores = jnp.where(row >= col, scores, 0.0).astype(jnp.bfloat16)
        intra_out[b] = dot(scores, values[b])


def normalise(steps, act, state, intra, gain, *refs):
    got, (own_out, other_out) = refs[:steps], refs[steps:]
    _, core = position()
    chip_at = lax.axis_index("seq") // CORES
    base = jnp.zeros((HEAD, HEAD), jnp.float32)
    for step, ref in enumerate(got):
        base = base + jnp.where((chip_at >> step) % 2 == 1, ref[...].astype(jnp.float32), 0.0)
    odd = core == 1
    own_prefix = jnp.where(odd, base + state[1], base)
    other_prefix = jnp.where(odd, base, base + state[0])
    scale = gain[pl.ds(core, 1), :]
    for b, (prefix, out) in enumerate(((own_prefix, own_out), (other_prefix, other_out))):
        attended = dot(act[b, :, :HEAD], prefix.astype(jnp.bfloat16)) + intra[b]
        meansq = jnp.mean(attended * attended, axis=-1, keepdims=True)
        out[...] = (attended * lax.rsqrt(meansq + 1e-06) * scale).astype(jnp.bfloat16)


def mix(count, places, own, other, *refs):
    mine, theirs, (out, stage, sem) = refs[:count], refs[count : 2 * count], refs[2 * count :]
    normed = jnp.concatenate([own[...], other[...]], axis=1)
    copies = []
    slot = 0
    for my_rows, their_rows, place in zip(mine, theirs, places()):
        width = my_rows.shape[1]
        step = min(width, 512)
        for at_col in range(0, width, step):
            part = slice(at_col, at_col + step)
            weights = jnp.concatenate([my_rows[:, part], their_rows[:, part]], axis=0)
            here = stage.at[:, slot : slot + step]
            here[...] = dot(normed, weights).astype(jnp.bfloat16)
            cols = pl.ds(pl.multiple_of(place + at_col, 128), step)
            copies.append(pltpu.make_async_copy(here, out.at[:, cols], sem.at[len(copies)]))
            copies[-1].start()
            slot += step
    for copy in copies:
        copy.wait()


def places_out(width):
    at = lax.axis_index("dp")
    return [(at ^ offset) * width for offset in range(4)]


def shards(n, blocks, tokens, w_qkv, norm_gain, w_out):
    tok_own = tokens[0]
    rows, depth = tok_own.shape
    shard = w_qkv.shape[0]
    heads = norm_gain.shape[0] // HEAD
    bf16, f32 = jnp.bfloat16, jnp.float32

    def call(kernel, outs, ins, out_specs, in_specs, scratch=(), flops=0, moved=0, limit=VMEM_LIMIT):
        return pl.pallas_call(
            kernel,
            out_shape=outs,
            in_specs=in_specs,
            out_specs=out_specs,
            scratch_shapes=scratch,
            compiler_params=pltpu.CompilerParams(vmem_limit_bytes=limit),
            cost_estimate=pl.CostEstimate(flops=flops, bytes_accessed=moved, transcendentals=0),
        )(*ins)

    def array(shape, kind):
        return jax.ShapeDtypeStruct(shape, kind)

    def add_product(pieces, places, total=None):
        extra = [] if total is None else [total]
        return call(
            functools.partial(project, len(pieces), places),
            array((CORES * rows, 3 * HEAD), f32),
            [tok_own, tok_other, *pieces, *extra],
            VMEM, [VMEM] * (2 + len(pieces) + len(extra)),
            flops=rows * HEAD * (1 if total is not None else 1000000),
        )

    tok_other = flip(tok_own, "seq", blocks, 1)
    width = w_out.shape[1]
    grid = n == 4 and blocks % (4 * CORES) == 0 and shard % 512 == 0 and width % 256 == 0

    def cut(first, limit, *sizes):
        return call(
            functools.partial(cut_qkv, first),
            [array((size, 3 * HEAD), bf16) for size in sizes], [w_qkv], [VMEM] * len(sizes), [HBM],
            scratch=[pltpu.SemaphoreType.DMA((3,))], limit=limit,
        )

    out_cut = functools.partial(
        call, cut_out, [array((HEAD, width), bf16)] * 2 + [array((HEAD, width // 2), bf16)],
        [w_out], [VMEM] * 3, [VMEM]
    )
    total = None
    if grid:
        quarter = shard // 4
        part = cut(lambda: quarter_of() * quarter, FIRST_LIMIT, quarter)[0]
        far = [flip(part, "dp", n, 3)]
        own, most, last = cut(lambda: 0, CUT_LIMIT, shard, 3 * quarter, quarter)
        x_most = flip(most, "dp", n, 1)
        send_last, here = lax.optimization_barrier((last, far[0]))
        x_last = flip(send_last, "dp", n, 1)
        from_y = flip(own, "dp", n, 2)
        far.append(flip(far[0], "seq", blocks, CORES * 2))
        here, own = lax.optimization_barrier((far[0], own))
        total = add_product([own], functools.partial(places_near, shard, (0,)))
        send_far, total = lax.optimization_barrier((far[0], total))
        far.append(flip(send_far, "seq", blocks, CORES))
        passed, total = lax.optimization_barrier((far[1], total))
        far.append(flip(passed, "seq", blocks, CORES))
        own_mine, own_theirs, own_part = out_cut()
        send_part, total, far[1] = lax.optimization_barrier((own_part, total, far[1]))
        out_d = flip(send_part, "dp", n, 3)
        out_e = flip(out_d, "seq", blocks, CORES)
        sent, total, far[1] = lax.optimization_barrier((own_mine, total, far[1]))
        out_x = flip(sent, "dp", n, 1)
        out_y = flip(sent, "dp", n, 2)
        total = add_product(
            [x_most, *far[:3]], lambda: places_near(shard, (1,)) + places_far(shard)[:3], total
        )
        total = add_product([x_last, from_y], functools.partial(places_last, shard), total)
        pieces, places = far[3:], lambda: places_far(shard)[3:]
    else:
        whole = cut(lambda: 0, CUT_LIMIT, shard)[0]
        pieces, places = [lax.all_gather(whole, "dp", axis=0, tiled=True)], lambda: [0]
    extra = [] if total is None else [total]

    act, values, state, chip = call(
        functools.partial(project_states, len(pieces), places),
        [
            array((CORES, rows, 2 * HEAD), bf16),
            array((CORES, rows, HEAD), bf16),
            array((CORES, HEAD, HEAD), f32),
            array((HEAD, HEAD), bf16),
        ],
        [tok_own, tok_other, *pieces, *extra],
        [VMEM] * 4, [VMEM] * (2 + len(pieces) + len(extra)),
        flops=2 * CORES * rows * sum(piece.shape[0] for piece in pieces) * 3 * HEAD,
    )
    got, group = [], chip
    for step in range((blocks // CORES).bit_length() - 1):
        if got:
            group = (group.astype(f32) + got[-1].astype(f32)).astype(bf16)
            if grid:
                group, out_d = lax.optimization_barrier((group, out_d))
        got.append(flip(group, "seq", blocks, CORES << step))
    scored, halves, outs = act, [], [array((CORES, rows, HEAD), f32)]
    if grid:
        scored, out_x, out_y = lax.optimization_barrier((act, out_x, out_y))
        halves = [out_d, out_e]
        outs.append(array((HEAD, width), bf16))
    intra, *columns = call(
        attend, outs, [scored, values, *halves], [VMEM] * len(outs), [VMEM] * (2 + len(halves)),
        flops=rows * HEAD * 1000000,
    )
    if grid:
        mine = [own_mine, out_x, out_y, *columns]
        theirs = [own_theirs] + [flip(piece, "seq", blocks, 1) for piece in mine[1:]]
    normed_own, normed_other = call(
        functools.partial(normalise, len(got)),
        [array((rows, HEAD), bf16)] * 2,
        [act, state, intra, norm_gain.reshape(heads, HEAD), *got],
        [VMEM] * 2, [VMEM] * (4 + len(got)), flops=rows * HEAD * 1000000,
    )
    normed_got = flip(normed_other, "seq", blocks, 1)

    if grid:
        places = functools.partial(places_out, width)
    else:
        mine = [lax.all_gather(out_cut()[0], "dp", axis=1, tiled=True)]
        theirs = [flip(mine[0], "seq", blocks, 1)]
        places = lambda: [0]
    mixed = call(
        functools.partial(mix, len(mine), places),
        array((rows, n * width), bf16),
        [normed_own, normed_got, *mine, *theirs],
        HBM, [VMEM] * (2 + 2 * len(mine)),
        scratch=[pltpu.VMEM((rows, n * width), bf16), pltpu.SemaphoreType.DMA((16,))],
        flops=2 * rows * 2 * HEAD * n * width, moved=2 * rows * n * width,
    )
    return mixed[None]


def solution(mesh):
    n, blocks = mesh.shape["dp"], mesh.shape["seq"]
    return jax.shard_map(
        functools.partial(shards, n, blocks),
        mesh=mesh,
        in_specs=(P("dp", "seq", None), P("dp", None), P(), P(None, "dp")),
        out_specs=P("dp", "seq", None),
        check_vma=False,
    )
```

```python
import functools

import jax
import jax.numpy as jnp
from jax import lax
from jax.experimental import pallas as pl
from jax.experimental.pallas import tpu as pltpu
from jax.sharding import PartitionSpec as P

HEAD = 128
CORES = 2
VMEM_LIMIT = 24 * 1024 * 1024
FIRST_LIMIT = 53 * 1024 * 1024
CUT_LIMIT = 52 * 1024 * 1024
VMEM = pl.BlockSpec(memory_space=pltpu.VMEM)
HBM = pl.BlockSpec(memory_space=pltpu.HBM)


def flip(x, axis, size, mask):
    return lax.ppermute(x, axis, [(i, i ^ mask) for i in range(size)])


def dot(a, b, contract=((1,), (0,))):
    return lax.dot_general(a, b, (contract, ((), ())), preferred_element_type=jnp.float32)


def position():
    return lax.axis_index("dp"), lax.rem(lax.axis_index("seq"), CORES)


def parity():
    return lax.rem(lax.axis_index("seq") // CORES, 2)


def quarter_of():
    return lax.rem(lax.axis_index("seq") // CORES, 4)


def cut_qkv(first, w_qkv, out, *refs):
    pieces, sem = refs[:-1], refs[-1]
    _, core = position()
    feat = w_qkv.shape[1] // 3
    rows = pl.ds(pl.multiple_of(first(), 16), out.shape[0])
    copies = []
    for j in range(3):
        cols = pl.ds(pl.multiple_of(j * feat + core * HEAD, HEAD), HEAD)
        target = out.at[:, j * HEAD : (j + 1) * HEAD]
        copies.append(pltpu.make_async_copy(w_qkv.at[rows, cols], target, sem.at[j]))
        copies[-1].start()
    for copy in copies:
        copy.wait()
    at = 0
    for piece in pieces:
        piece[...] = out[at : at + piece.shape[0], :]
        at += piece.shape[0]


def cut_out(w_out, mine, theirs, part):
    _, core = position()
    rows = pl.ds(pl.multiple_of(core * HEAD, HEAD), HEAD)
    other = pl.ds(pl.multiple_of((1 - core) * HEAD, HEAD), HEAD)
    mine[...] = w_out[rows, :]
    theirs[...] = w_out[other, :]
    half = part.shape[1]
    part[...] = w_out[rows, pl.ds(pl.multiple_of(parity() * half, half), half)]


def product(tok_a, tok_b, pieces, places):
    cols = [
        pl.ds(pl.multiple_of(place, 128), piece.shape[0]) for piece, place in zip(pieces, places)
    ]
    tok = jnp.concatenate(
        [jnp.concatenate([ref[:, c] for c in cols], axis=1) for ref in (tok_a, tok_b)], axis=0
    )
    weights = jnp.concatenate([piece[...] for piece in pieces], axis=0)
    return dot(tok, weights)


def places_near(shard, offsets):
    at = lax.axis_index("dp")
    return [(at ^ offset) * shard for offset in offsets]


def places_last(shard):
    near_y, near_x = places_near(shard, (2, 1))
    return [near_y + 3 * (shard // 4), near_x]


def places_far(shard):
    start = places_near(shard, (3,))[0]
    mine = quarter_of()
    return [start + (mine ^ mask) * (shard // 4) for mask in (0, 2, 1, 3)]


def project(count, places, tok_a, tok_b, *refs):
    pieces, before, total = refs[:count], refs[count:-1], refs[-1]
    term = product(tok_a, tok_b, pieces, places())
    total[...] = before[0][...] + term if before else term


def project_states(count, places, tok_a, tok_b, *refs):
    pieces, before = refs[:count], refs[count:-4]
    act_out, value_out, state_out, chip_out = refs[-4:]
    proj = product(tok_a, tok_b, pieces, places())
    if before:
        proj = before[0][...] + proj
    rows = value_out.shape[1]
    chip = None
    for b in range(CORES):
        part = proj[b * rows : (b + 1) * rows, :]
        act = part[:, : 2 * HEAD]
        act = (act / (1.0 + jnp.exp(-act))).astype(jnp.bfloat16)
        values = part[:, 2 * HEAD :].astype(jnp.bfloat16)
        state = dot(act[:, HEAD:], values, ((0,), (0,)))
        chip = state if chip is None else chip + state
        act_out[b] = act
        value_out[b] = values
        state_out[b] = state
    chip_out[...] = chip.astype(jnp.bfloat16)


def attend(act, values, *refs):
    if len(refs) > 1:
        own_half, other_half, intra_out, columns_out = refs
        half = own_half.shape[1]
        columns_out[:, pl.ds(pl.multiple_of(parity() * half, half), half)] = own_half[...]
        columns_out[:, pl.ds(pl.multiple_of((1 - parity()) * half, half), half)] = other_half[...]
    else:
        intra_out = refs[0]
    rows = intra_out.shape[1]
    row = lax.broadcasted_iota(jnp.int32, (rows, rows), 0)
    col = lax.broadcasted_iota(jnp.int32, (rows, rows), 1)
    for b in range(CORES):
        scores = dot(act[b, :, :HEAD], act[b, :, HEAD:], ((1,), (1,)))
        scores = jnp.where(row >= col, scores, 0.0).astype(jnp.bfloat16)
        intra_out[b] = dot(scores, values[b])


def normalise(steps, act, state, intra, gain, *refs):
    got, (own_out, other_out) = refs[:steps], refs[steps:]
    _, core = position()
    chip_at = lax.axis_index("seq") // CORES
    base = jnp.zeros((HEAD, HEAD), jnp.float32)
    for step, ref in enumerate(got):
        base = base + jnp.where((chip_at >> step) % 2 == 1, ref[...].astype(jnp.float32), 0.0)
    odd = core == 1
    own_prefix = jnp.where(odd, base + state[1], base)
    other_prefix = jnp.where(odd, base, base + state[0])
    scale = gain[pl.ds(core, 1), :]
    for b, (prefix, out) in enumerate(((own_prefix, own_out), (other_prefix, other_out))):
        attended = dot(act[b, :, :HEAD], prefix.astype(jnp.bfloat16)) + intra[b]
        meansq = jnp.mean(attended * attended, axis=-1, keepdims=True)
        out[...] = (attended * lax.rsqrt(meansq + 1e-06) * scale).astype(jnp.bfloat16)


def mix(count, places, own, other, *refs):
    mine, theirs, (out, stage, sem) = refs[:count], refs[count : 2 * count], refs[2 * count :]
    normed = jnp.concatenate([own[...], other[...]], axis=1)
    copies = []
    slot = 0
    for my_rows, their_rows, place in zip(mine, theirs, places()):
        width = my_rows.shape[1]
        step = min(width, 512)
        for at_col in range(0, width, step):
            part = slice(at_col, at_col + step)
            weights = jnp.concatenate([my_rows[:, part], their_rows[:, part]], axis=0)
            here = stage.at[:, slot : slot + step]
            here[...] = dot(normed, weights).astype(jnp.bfloat16)
            cols = pl.ds(pl.multiple_of(place + at_col, 128), step)
            copies.append(pltpu.make_async_copy(here, out.at[:, cols], sem.at[len(copies)]))
            copies[-1].start()
            slot += step
    for copy in copies:
        copy.wait()


def places_out(width):
    at = lax.axis_index("dp")
    return [(at ^ offset) * width for offset in range(4)]


def shards(n, blocks, tokens, w_qkv, norm_gain, w_out):
    tok_own = tokens[0]
    rows, depth = tok_own.shape
    shard = w_qkv.shape[0]
    heads = norm_gain.shape[0] // HEAD
    bf16, f32 = jnp.bfloat16, jnp.float32

    def call(kernel, outs, ins, out_specs, in_specs, scratch=(), flops=0, moved=0, limit=VMEM_LIMIT):
        return pl.pallas_call(
            kernel,
            out_shape=outs,
            in_specs=in_specs,
            out_specs=out_specs,
            scratch_shapes=scratch,
            compiler_params=pltpu.CompilerParams(vmem_limit_bytes=limit),
            cost_estimate=pl.CostEstimate(flops=flops, bytes_accessed=moved, transcendentals=0),
        )(*ins)

    def array(shape, kind):
        return jax.ShapeDtypeStruct(shape, kind)

    def add_product(pieces, places, total=None):
        extra = [] if total is None else [total]
        return call(
            functools.partial(project, len(pieces), places),
            array((CORES * rows, 3 * HEAD), f32),
            [tok_own, tok_other, *pieces, *extra],
            VMEM, [VMEM] * (2 + len(pieces) + len(extra)),
            flops=rows * HEAD * (1 if total is not None else 1000000),
        )

    tok_other = flip(tok_own, "seq", blocks, 1)
    width = w_out.shape[1]
    grid = n == 4 and blocks % (4 * CORES) == 0 and shard % 512 == 0 and width % 256 == 0

    def cut(first, limit, *sizes):
        return call(
            functools.partial(cut_qkv, first),
            [array((size, 3 * HEAD), bf16) for size in sizes], [w_qkv], [VMEM] * len(sizes), [HBM],
            scratch=[pltpu.SemaphoreType.DMA((3,))], limit=limit,
        )

    out_cut = functools.partial(
        call, cut_out, [array((HEAD, width), bf16)] * 2 + [array((HEAD, width // 2), bf16)],
        [w_out], [VMEM] * 3, [VMEM]
    )
    total = None
    if grid:
        quarter = shard // 4
        part = cut(lambda: quarter_of() * quarter, FIRST_LIMIT, quarter)[0]
        far = [flip(part, "dp", n, 3)]
        own, most, last = cut(lambda: 0, CUT_LIMIT, shard, 3 * quarter, quarter)
        y_most = flip(most, "dp", n, 2)
        send_last, here = lax.optimization_barrier((last, far[0]))
        y_last = flip(send_last, "dp", n, 2)
        from_x = flip(own, "dp", n, 1)
        far.append(flip(far[0], "seq", blocks, CORES * 2))
        here, own = lax.optimization_barrier((far[0], own))
        total = add_product([own], functools.partial(places_near, shard, (0,)))
        send_far, total = lax.optimization_barrier((far[0], total))
        far.append(flip(send_far, "seq", blocks, CORES))
        passed, total = lax.optimization_barrier((far[1], total))
        far.append(flip(passed, "seq", blocks, CORES))
        own_mine, own_theirs, own_part = out_cut()
        send_part, total, far[1] = lax.optimization_barrier((own_part, total, far[1]))
        out_d = flip(send_part, "dp", n, 3)
        out_e = flip(out_d, "seq", blocks, CORES)
        sent, total, far[1] = lax.optimization_barrier((own_mine, total, far[1]))
        out_x = flip(sent, "dp", n, 1)
        out_y = flip(sent, "dp", n, 2)
        total = add_product(
            [y_most, *far[:3]], lambda: places_near(shard, (2,)) + places_far(shard)[:3], total
        )
        total = add_product([y_last, from_x], functools.partial(places_last, shard), total)
        pieces, places = far[3:], lambda: places_far(shard)[3:]
    else:
        whole = cut(lambda: 0, CUT_LIMIT, shard)[0]
        pieces, places = [lax.all_gather(whole, "dp", axis=0, tiled=True)], lambda: [0]
    extra = [] if total is None else [total]

    act, values, state, chip = call(
        functools.partial(project_states, len(pieces), places),
        [
            array((CORES, rows, 2 * HEAD), bf16),
            array((CORES, rows, HEAD), bf16),
            array((CORES, HEAD, HEAD), f32),
            array((HEAD, HEAD), bf16),
        ],
        [tok_own, tok_other, *pieces, *extra],
        [VMEM] * 4, [VMEM] * (2 + len(pieces) + len(extra)),
        flops=2 * CORES * rows * sum(piece.shape[0] for piece in pieces) * 3 * HEAD,
    )
    got, group = [], chip
    for step in range((blocks // CORES).bit_length() - 1):
        if got:
            group = (group.astype(f32) + got[-1].astype(f32)).astype(bf16)
            if grid:
                group, out_d = lax.optimization_barrier((group, out_d))
        got.append(flip(group, "seq", blocks, CORES << step))
    scored, halves, outs = act, [], [array((CORES, rows, HEAD), f32)]
    if grid:
        scored, out_x, out_y = lax.optimization_barrier((act, out_x, out_y))
        halves = [out_d, out_e]
        outs.append(array((HEAD, width), bf16))
    intra, *columns = call(
        attend, outs, [scored, values, *halves], [VMEM] * len(outs), [VMEM] * (2 + len(halves)),
        flops=rows * HEAD * 1000000,
    )
    if grid:
        mine = [own_mine, out_x, out_y, *columns]
        theirs = [own_theirs] + [flip(piece, "seq", blocks, 1) for piece in mine[1:]]
    normed_own, normed_other = call(
        functools.partial(normalise, len(got)),
        [array((rows, HEAD), bf16)] * 2,
        [act, state, intra, norm_gain.reshape(heads, HEAD), *got],
        [VMEM] * 2, [VMEM] * (4 + len(got)), flops=rows * HEAD * 1000000,
    )
    normed_got = flip(normed_other, "seq", blocks, 1)

    if grid:
        places = functools.partial(places_out, width)
    else:
        mine = [lax.all_gather(out_cut()[0], "dp", axis=1, tiled=True)]
        theirs = [flip(mine[0], "seq", blocks, 1)]
        places = lambda: [0]
    mixed = call(
        functools.partial(mix, len(mine), places),
        array((rows, n * width), bf16),
        [normed_own, normed_got, *mine, *theirs],
        HBM, [VMEM] * (2 + 2 * len(mine)),
        scratch=[pltpu.VMEM((rows, n * width), bf16), pltpu.SemaphoreType.DMA((16,))],
        flops=2 * rows * 2 * HEAD * n * width, moved=2 * rows * n * width,
    )
    return mixed[None]


def solution(mesh):
    n, blocks = mesh.shape["dp"], mesh.shape["seq"]
    return jax.shard_map(
        functools.partial(shards, n, blocks),
        mesh=mesh,
        in_specs=(P("dp", "seq", None), P("dp", None), P(), P(None, "dp")),
        out_specs=P("dp", "seq", None),
        check_vma=False,
    )
```

```python
import functools

import jax
import jax.numpy as jnp
from jax import lax
from jax.experimental import pallas as pl
from jax.experimental.pallas import tpu as pltpu
from jax.sharding import PartitionSpec as P

HEAD = 128
CORES = 2
VMEM_LIMIT = 24 * 1024 * 1024
FIRST_LIMIT = 53 * 1024 * 1024
CUT_LIMIT = 52 * 1024 * 1024
VMEM = pl.BlockSpec(memory_space=pltpu.VMEM)
HBM = pl.BlockSpec(memory_space=pltpu.HBM)


def flip(x, axis, size, mask):
    return lax.ppermute(x, axis, [(i, i ^ mask) for i in range(size)])


def dot(a, b, contract=((1,), (0,))):
    return lax.dot_general(a, b, (contract, ((), ())), preferred_element_type=jnp.float32)


def position():
    return lax.axis_index("dp"), lax.rem(lax.axis_index("seq"), CORES)


def parity():
    return lax.rem(lax.axis_index("seq") // CORES, 2)


def quarter_of():
    return lax.rem(lax.axis_index("seq") // CORES, 4)


def cut_qkv(first, w_qkv, out, *refs):
    pieces, sem = refs[:-1], refs[-1]
    _, core = position()
    feat = w_qkv.shape[1] // 3
    rows = pl.ds(pl.multiple_of(first(), 16), out.shape[0])
    copies = []
    for j in range(3):
        cols = pl.ds(pl.multiple_of(j * feat + core * HEAD, HEAD), HEAD)
        target = out.at[:, j * HEAD : (j + 1) * HEAD]
        copies.append(pltpu.make_async_copy(w_qkv.at[rows, cols], target, sem.at[j]))
        copies[-1].start()
    for copy in copies:
        copy.wait()
    at = 0
    for piece in pieces:
        piece[...] = out[at : at + piece.shape[0], :]
        at += piece.shape[0]


def cut_out(w_out, mine, theirs, part):
    _, core = position()
    rows = pl.ds(pl.multiple_of(core * HEAD, HEAD), HEAD)
    other = pl.ds(pl.multiple_of((1 - core) * HEAD, HEAD), HEAD)
    mine[...] = w_out[rows, :]
    theirs[...] = w_out[other, :]
    half = part.shape[1]
    part[...] = w_out[rows, pl.ds(pl.multiple_of(parity() * half, half), half)]


def product(tok_a, tok_b, pieces, places):
    cols = [
        pl.ds(pl.multiple_of(place, 128), piece.shape[0]) for piece, place in zip(pieces, places)
    ]
    tok = jnp.concatenate(
        [jnp.concatenate([ref[:, c] for c in cols], axis=1) for ref in (tok_a, tok_b)], axis=0
    )
    weights = jnp.concatenate([piece[...] for piece in pieces], axis=0)
    return dot(tok, weights)


def places_near(shard, offsets):
    at = lax.axis_index("dp")
    return [(at ^ offset) * shard for offset in offsets]


def places_last(shard):
    near_y, near_x = places_near(shard, (2, 1))
    return [near_y + 3 * (shard // 4), near_x]


def places_far(shard):
    start = places_near(shard, (3,))[0]
    mine = quarter_of()
    return [start + (mine ^ mask) * (shard // 4) for mask in (0, 2, 1, 3)]


def project(count, places, tok_a, tok_b, *refs):
    pieces, before, total = refs[:count], refs[count:-1], refs[-1]
    term = product(tok_a, tok_b, pieces, places())
    total[...] = before[0][...] + term if before else term


def project_states(count, places, tok_a, tok_b, *refs):
    pieces, before = refs[:count], refs[count:-4]
    act_out, value_out, state_out, chip_out = refs[-4:]
    proj = product(tok_a, tok_b, pieces, places())
    if before:
        proj = before[0][...] + proj
    rows = value_out.shape[1]
    chip = None
    for b in range(CORES):
        part = proj[b * rows : (b + 1) * rows, :]
        act = part[:, : 2 * HEAD]
        act = (act / (1.0 + jnp.exp(-act))).astype(jnp.bfloat16)
        values = part[:, 2 * HEAD :].astype(jnp.bfloat16)
        state = dot(act[:, HEAD:], values, ((0,), (0,)))
        chip = state if chip is None else chip + state
        act_out[b] = act
        value_out[b] = values
        state_out[b] = state
    chip_out[...] = chip.astype(jnp.bfloat16)


def attend(act, values, *refs):
    if len(refs) > 1:
        own_half, other_half, intra_out, columns_out = refs
        half = own_half.shape[1]
        columns_out[:, pl.ds(pl.multiple_of(parity() * half, half), half)] = own_half[...]
        columns_out[:, pl.ds(pl.multiple_of((1 - parity()) * half, half), half)] = other_half[...]
    else:
        intra_out = refs[0]
    rows = intra_out.shape[1]
    row = lax.broadcasted_iota(jnp.int32, (rows, rows), 0)
    col = lax.broadcasted_iota(jnp.int32, (rows, rows), 1)
    for b in range(CORES):
        scores = dot(act[b, :, :HEAD], act[b, :, HEAD:], ((1,), (1,)))
        scores = jnp.where(row >= col, scores, 0.0).astype(jnp.bfloat16)
        intra_out[b] = dot(scores, values[b])


def normalise(steps, act, state, intra, gain, *refs):
    got, (own_out, other_out) = refs[:steps], refs[steps:]
    _, core = position()
    chip_at = lax.axis_index("seq") // CORES
    base = jnp.zeros((HEAD, HEAD), jnp.float32)
    for step, ref in enumerate(got):
        base = base + jnp.where((chip_at >> step) % 2 == 1, ref[...].astype(jnp.float32), 0.0)
    odd = core == 1
    own_prefix = jnp.where(odd, base + state[1], base)
    other_prefix = jnp.where(odd, base, base + state[0])
    scale = gain[pl.ds(core, 1), :]
    for b, (prefix, out) in enumerate(((own_prefix, own_out), (other_prefix, other_out))):
        attended = dot(act[b, :, :HEAD], prefix.astype(jnp.bfloat16)) + intra[b]
        meansq = jnp.mean(attended * attended, axis=-1, keepdims=True)
        out[...] = (attended * lax.rsqrt(meansq + 1e-06) * scale).astype(jnp.bfloat16)


def mix(count, places, own, other, *refs):
    mine, theirs, (out, stage, sem) = refs[:count], refs[count : 2 * count], refs[2 * count :]
    normed = jnp.concatenate([own[...], other[...]], axis=1)
    copies = []
    slot = 0
    for my_rows, their_rows, place in zip(mine, theirs, places()):
        width = my_rows.shape[1]
        step = min(width, 512)
        for at_col in range(0, width, step):
            part = slice(at_col, at_col + step)
            weights = jnp.concatenate([my_rows[:, part], their_rows[:, part]], axis=0)
            here = stage.at[:, slot : slot + step]
            here[...] = dot(normed, weights).astype(jnp.bfloat16)
            cols = pl.ds(pl.multiple_of(place + at_col, 128), step)
            copies.append(pltpu.make_async_copy(here, out.at[:, cols], sem.at[len(copies)]))
            copies[-1].start()
            slot += step
    for copy in copies:
        copy.wait()


def places_out(width):
    at = lax.axis_index("dp")
    return [(at ^ offset) * width for offset in (0, 2, 1, 3)]


def shards(n, blocks, tokens, w_qkv, norm_gain, w_out):
    tok_own = tokens[0]
    rows, depth = tok_own.shape
    shard = w_qkv.shape[0]
    heads = norm_gain.shape[0] // HEAD
    bf16, f32 = jnp.bfloat16, jnp.float32

    def call(kernel, outs, ins, out_specs, in_specs, scratch=(), flops=0, moved=0, limit=VMEM_LIMIT):
        return pl.pallas_call(
            kernel,
            out_shape=outs,
            in_specs=in_specs,
            out_specs=out_specs,
            scratch_shapes=scratch,
            compiler_params=pltpu.CompilerParams(vmem_limit_bytes=limit),
            cost_estimate=pl.CostEstimate(flops=flops, bytes_accessed=moved, transcendentals=0),
        )(*ins)

    def array(shape, kind):
        return jax.ShapeDtypeStruct(shape, kind)

    def add_product(pieces, places, total=None):
        extra = [] if total is None else [total]
        return call(
            functools.partial(project, len(pieces), places),
            array((CORES * rows, 3 * HEAD), f32),
            [tok_own, tok_other, *pieces, *extra],
            VMEM, [VMEM] * (2 + len(pieces) + len(extra)),
            flops=rows * HEAD * (1 if total is not None else 1000000),
        )

    tok_other = flip(tok_own, "seq", blocks, 1)
    width = w_out.shape[1]
    grid = n == 4 and blocks % (4 * CORES) == 0 and shard % 512 == 0 and width % 256 == 0

    def cut(first, limit, *sizes):
        return call(
            functools.partial(cut_qkv, first),
            [array((size, 3 * HEAD), bf16) for size in sizes], [w_qkv], [VMEM] * len(sizes), [HBM],
            scratch=[pltpu.SemaphoreType.DMA((3,))], limit=limit,
        )

    out_cut = functools.partial(
        call, cut_out, [array((HEAD, width), bf16)] * 2 + [array((HEAD, width // 2), bf16)],
        [w_out], [VMEM] * 3, [VMEM]
    )
    total = None
    if grid:
        quarter = shard // 4
        part = cut(lambda: quarter_of() * quarter, FIRST_LIMIT, quarter)[0]
        far = [flip(part, "dp", n, 3)]
        own, most, last = cut(lambda: 0, CUT_LIMIT, shard, 3 * quarter, quarter)
        y_most = flip(most, "dp", n, 2)
        send_last, here = lax.optimization_barrier((last, far[0]))
        y_last = flip(send_last, "dp", n, 2)
        from_x = flip(own, "dp", n, 1)
        far.append(flip(far[0], "seq", blocks, CORES * 2))
        here, own = lax.optimization_barrier((far[0], own))
        total = add_product([own], functools.partial(places_near, shard, (0,)))
        send_far, total = lax.optimization_barrier((far[0], total))
        far.append(flip(send_far, "seq", blocks, CORES))
        passed, total = lax.optimization_barrier((far[1], total))
        far.append(flip(passed, "seq", blocks, CORES))
        own_mine, own_theirs, own_part = out_cut()
        send_part, total, far[1] = lax.optimization_barrier((own_part, total, far[1]))
        out_d = flip(send_part, "dp", n, 3)
        out_e = flip(out_d, "seq", blocks, CORES)
        sent, total, far[1] = lax.optimization_barrier((own_mine, total, far[1]))
        out_y = flip(sent, "dp", n, 2)
        out_x = flip(sent, "dp", n, 1)
        total = add_product(
            [y_most, *far[:3]], lambda: places_near(shard, (2,)) + places_far(shard)[:3], total
        )
        total = add_product([y_last, from_x], functools.partial(places_last, shard), total)
        pieces, places = far[3:], lambda: places_far(shard)[3:]
    else:
        whole = cut(lambda: 0, CUT_LIMIT, shard)[0]
        pieces, places = [lax.all_gather(whole, "dp", axis=0, tiled=True)], lambda: [0]
    extra = [] if total is None else [total]

    act, values, state, chip = call(
        functools.partial(project_states, len(pieces), places),
        [
            array((CORES, rows, 2 * HEAD), bf16),
            array((CORES, rows, HEAD), bf16),
            array((CORES, HEAD, HEAD), f32),
            array((HEAD, HEAD), bf16),
        ],
        [tok_own, tok_other, *pieces, *extra],
        [VMEM] * 4, [VMEM] * (2 + len(pieces) + len(extra)),
        flops=2 * CORES * rows * sum(piece.shape[0] for piece in pieces) * 3 * HEAD,
    )
    got, group = [], chip
    for step in range((blocks // CORES).bit_length() - 1):
        if got:
            group = (group.astype(f32) + got[-1].astype(f32)).astype(bf16)
            if grid:
                group, out_d = lax.optimization_barrier((group, out_d))
        got.append(flip(group, "seq", blocks, CORES << step))
    scored, halves, outs = act, [], [array((CORES, rows, HEAD), f32)]
    if grid:
        scored, out_y, out_x = lax.optimization_barrier((act, out_y, out_x))
        halves = [out_d, out_e]
        outs.append(array((HEAD, width), bf16))
    intra, *columns = call(
        attend, outs, [scored, values, *halves], [VMEM] * len(outs), [VMEM] * (2 + len(halves)),
        flops=rows * HEAD * 1000000,
    )
    if grid:
        mine = [own_mine, out_y, out_x, *columns]
        theirs = [own_theirs] + [flip(piece, "seq", blocks, 1) for piece in mine[1:]]
    normed_own, normed_other = call(
        functools.partial(normalise, len(got)),
        [array((rows, HEAD), bf16)] * 2,
        [act, state, intra, norm_gain.reshape(heads, HEAD), *got],
        [VMEM] * 2, [VMEM] * (4 + len(got)), flops=rows * HEAD * 1000000,
    )
    normed_got = flip(normed_other, "seq", blocks, 1)

    if grid:
        places = functools.partial(places_out, width)
    else:
        mine = [lax.all_gather(out_cut()[0], "dp", axis=1, tiled=True)]
        theirs = [flip(mine[0], "seq", blocks, 1)]
        places = lambda: [0]
    mixed = call(
        functools.partial(mix, len(mine), places),
        array((rows, n * width), bf16),
        [normed_own, normed_got, *mine, *theirs],
        HBM, [VMEM] * (2 + 2 * len(mine)),
        scratch=[pltpu.VMEM((rows, n * width), bf16), pltpu.SemaphoreType.DMA((16,))],
        flops=2 * rows * 2 * HEAD * n * width, moved=2 * rows * n * width,
    )
    return mixed[None]


def solution(mesh):
    n, blocks = mesh.shape["dp"], mesh.shape["seq"]
    return jax.shard_map(
        functools.partial(shards, n, blocks),
        mesh=mesh,
        in_specs=(P("dp", "seq", None), P("dp", None), P(), P(None, "dp")),
        out_specs=P("dp", "seq", None),
        check_vma=False,
    )
```

```python
import functools

import jax
import jax.numpy as jnp
from jax import lax
from jax.experimental import pallas as pl
from jax.experimental.pallas import tpu as pltpu
from jax.sharding import PartitionSpec as P

HEAD = 128
CORES = 2
VMEM_LIMIT = 24 * 1024 * 1024
FIRST_LIMIT = 53 * 1024 * 1024
CUT_LIMIT = 52 * 1024 * 1024
VMEM = pl.BlockSpec(memory_space=pltpu.VMEM)
HBM = pl.BlockSpec(memory_space=pltpu.HBM)


def flip(x, axis, size, mask):
    return lax.ppermute(x, axis, [(i, i ^ mask) for i in range(size)])


def dot(a, b, contract=((1,), (0,))):
    return lax.dot_general(a, b, (contract, ((), ())), preferred_element_type=jnp.float32)


def position():
    return lax.axis_index("dp"), lax.rem(lax.axis_index("seq"), CORES)


def parity():
    return lax.rem(lax.axis_index("seq") // CORES, 2)


def quarter_of():
    return lax.rem(lax.axis_index("seq") // CORES, 4)


def cut_qkv(first, w_qkv, out, *refs):
    pieces, sem = refs[:-1], refs[-1]
    _, core = position()
    feat = w_qkv.shape[1] // 3
    rows = pl.ds(pl.multiple_of(first(), 16), out.shape[0])
    copies = []
    for j in range(3):
        cols = pl.ds(pl.multiple_of(j * feat + core * HEAD, HEAD), HEAD)
        target = out.at[:, j * HEAD : (j + 1) * HEAD]
        copies.append(pltpu.make_async_copy(w_qkv.at[rows, cols], target, sem.at[j]))
        copies[-1].start()
    for copy in copies:
        copy.wait()
    at = 0
    for piece in pieces:
        piece[...] = out[at : at + piece.shape[0], :]
        at += piece.shape[0]


def cut_out(w_out, mine, theirs, part):
    _, core = position()
    rows = pl.ds(pl.multiple_of(core * HEAD, HEAD), HEAD)
    other = pl.ds(pl.multiple_of((1 - core) * HEAD, HEAD), HEAD)
    mine[...] = w_out[rows, :]
    theirs[...] = w_out[other, :]
    half = part.shape[1]
    part[...] = w_out[rows, pl.ds(pl.multiple_of(parity() * half, half), half)]


def product(tok_a, tok_b, pieces, places):
    cols = [
        pl.ds(pl.multiple_of(place, 128), piece.shape[0]) for piece, place in zip(pieces, places)
    ]
    tok = jnp.concatenate(
        [jnp.concatenate([ref[:, c] for c in cols], axis=1) for ref in (tok_a, tok_b)], axis=0
    )
    weights = jnp.concatenate([piece[...] for piece in pieces], axis=0)
    return dot(tok, weights)


def places_near(shard, offsets):
    at = lax.axis_index("dp")
    return [(at ^ offset) * shard for offset in offsets]


def places_last(shard):
    near_x, near_y = places_near(shard, (1, 2))
    return [near_x + 3 * (shard // 4), near_y]


def places_far(shard):
    start = places_near(shard, (3,))[0]
    mine = quarter_of()
    return [start + (mine ^ mask) * (shard // 4) for mask in (0, 2, 1, 3)]


def project_block(shard, tok, own, *refs):
    before, out = refs[:-1], refs[-1]
    rows = tok.shape[0]
    cols = pl.ds(pl.multiple_of(places_near(shard, (0,))[0], 128), shard)
    if before:
        out[:rows, :] = before[0][...]
    out[out.shape[0] - rows :, :] = dot(tok[:, cols], own[...])


def project(count, places, tok_a, tok_b, *refs):
    pieces, before, total = refs[:count], refs[count:-1], refs[-1]
    term = product(tok_a, tok_b, pieces, places())
    total[...] = before[0][...] + term if before else term


def project_states(count, places, tok_a, tok_b, *refs):
    pieces, before = refs[:count], refs[count:-4]
    act_out, value_out, state_out, chip_out = refs[-4:]
    proj = product(tok_a, tok_b, pieces, places())
    if before:
        proj = before[0][...] + proj
    rows = value_out.shape[1]
    chip = None
    for b in range(CORES):
        part = proj[b * rows : (b + 1) * rows, :]
        act = part[:, : 2 * HEAD]
        act = (act / (1.0 + jnp.exp(-act))).astype(jnp.bfloat16)
        values = part[:, 2 * HEAD :].astype(jnp.bfloat16)
        state = dot(act[:, HEAD:], values, ((0,), (0,)))
        chip = state if chip is None else chip + state
        act_out[b] = act
        value_out[b] = values
        state_out[b] = state
    chip_out[...] = chip.astype(jnp.bfloat16)


def attend(act, values, *refs):
    if len(refs) > 1:
        own_half, other_half, intra_out, columns_out = refs
        half = own_half.shape[1]
        columns_out[:, pl.ds(pl.multiple_of(parity() * half, half), half)] = own_half[...]
        columns_out[:, pl.ds(pl.multiple_of((1 - parity()) * half, half), half)] = other_half[...]
    else:
        intra_out = refs[0]
    rows = intra_out.shape[1]
    row = lax.broadcasted_iota(jnp.int32, (rows, rows), 0)
    col = lax.broadcasted_iota(jnp.int32, (rows, rows), 1)
    for b in range(CORES):
        scores = dot(act[b, :, :HEAD], act[b, :, HEAD:], ((1,), (1,)))
        scores = jnp.where(row >= col, scores, 0.0).astype(jnp.bfloat16)
        intra_out[b] = dot(scores, values[b])


def normalise(steps, act, state, intra, gain, *refs):
    got, (own_out, other_out) = refs[:steps], refs[steps:]
    _, core = position()
    chip_at = lax.axis_index("seq") // CORES
    base = jnp.zeros((HEAD, HEAD), jnp.float32)
    for step, ref in enumerate(got):
        base = base + jnp.where((chip_at >> step) % 2 == 1, ref[...].astype(jnp.float32), 0.0)
    odd = core == 1
    own_prefix = jnp.where(odd, base + state[1], base)
    other_prefix = jnp.where(odd, base, base + state[0])
    scale = gain[pl.ds(core, 1), :]
    for b, (prefix, out) in enumerate(((own_prefix, own_out), (other_prefix, other_out))):
        attended = dot(act[b, :, :HEAD], prefix.astype(jnp.bfloat16)) + intra[b]
        meansq = jnp.mean(attended * attended, axis=-1, keepdims=True)
        out[...] = (attended * lax.rsqrt(meansq + 1e-06) * scale).astype(jnp.bfloat16)


def mix(count, places, own, other, *refs):
    mine, theirs, (out, stage, sem) = refs[:count], refs[count : 2 * count], refs[2 * count :]
    normed = jnp.concatenate([own[...], other[...]], axis=1)
    copies = []
    slot = 0
    for my_rows, their_rows, place in zip(mine, theirs, places()):
        width = my_rows.shape[1]
        step = min(width, 512)
        for at_col in range(0, width, step):
            part = slice(at_col, at_col + step)
            weights = jnp.concatenate([my_rows[:, part], their_rows[:, part]], axis=0)
            here = stage.at[:, slot : slot + step]
            here[...] = dot(normed, weights).astype(jnp.bfloat16)
            cols = pl.ds(pl.multiple_of(place + at_col, 128), step)
            copies.append(pltpu.make_async_copy(here, out.at[:, cols], sem.at[len(copies)]))
            copies[-1].start()
            slot += step
    for copy in copies:
        copy.wait()


def places_out(width):
    at = lax.axis_index("dp")
    return [(at ^ offset) * width for offset in range(4)]


def shards(n, blocks, tokens, w_qkv, norm_gain, w_out):
    tok_own = tokens[0]
    rows, depth = tok_own.shape
    shard = w_qkv.shape[0]
    heads = norm_gain.shape[0] // HEAD
    bf16, f32 = jnp.bfloat16, jnp.float32

    def call(kernel, outs, ins, out_specs, in_specs, scratch=(), flops=0, moved=0, limit=VMEM_LIMIT):
        return pl.pallas_call(
            kernel,
            out_shape=outs,
            in_specs=in_specs,
            out_specs=out_specs,
            scratch_shapes=scratch,
            compiler_params=pltpu.CompilerParams(vmem_limit_bytes=limit),
            cost_estimate=pl.CostEstimate(flops=flops, bytes_accessed=moved, transcendentals=0),
        )(*ins)

    def array(shape, kind):
        return jax.ShapeDtypeStruct(shape, kind)

    def add_product(tok_other, pieces, places, total=None):
        extra = [] if total is None else [total]
        return call(
            functools.partial(project, len(pieces), places),
            array((CORES * rows, 3 * HEAD), f32),
            [tok_own, tok_other, *pieces, *extra],
            VMEM, [VMEM] * (2 + len(pieces) + len(extra)),
            flops=rows * HEAD * (1 if total is not None else 1000000),
        )

    width = w_out.shape[1]
    grid = n == 4 and blocks % (4 * CORES) == 0 and shard % 512 == 0 and width % 256 == 0

    def cut(first, limit, *sizes):
        return call(
            functools.partial(cut_qkv, first),
            [array((size, 3 * HEAD), bf16) for size in sizes], [w_qkv], [VMEM] * len(sizes), [HBM],
            scratch=[pltpu.SemaphoreType.DMA((3,))], limit=limit,
        )

    out_cut = functools.partial(
        call, cut_out, [array((HEAD, width), bf16)] * 2 + [array((HEAD, width // 2), bf16)],
        [w_out], [VMEM] * 3, [VMEM]
    )
    total = None
    if grid:
        quarter = shard // 4
        part = cut(lambda: quarter_of() * quarter, FIRST_LIMIT, quarter)[0]
        far = [flip(part, "dp", n, 3)]
        own, most, last = cut(lambda: 0, CUT_LIMIT, shard, 3 * quarter, quarter)
        send_tok, _ = lax.optimization_barrier((tok_own, far[0]))
        tok_other = flip(send_tok, "seq", blocks, 1)
        x_most = flip(most, "dp", n, 1)
        send_last, here = lax.optimization_barrier((last, far[0]))
        x_last = flip(send_last, "dp", n, 1)
        from_y = flip(own, "dp", n, 2)
        far.append(flip(far[0], "seq", blocks, CORES * 2))
        here, own = lax.optimization_barrier((far[0], own))
        first = call(
            functools.partial(project_block, shard), array((rows, 3 * HEAD), f32),
            [tok_own, own], VMEM, [VMEM] * 2, flops=rows * HEAD * 1000000,
        )
        total = call(
            functools.partial(project_block, shard), array((CORES * rows, 3 * HEAD), f32),
            [tok_other, own, first], VMEM, [VMEM] * 3, flops=rows * HEAD,
        )
        send_far, total = lax.optimization_barrier((far[0], total))
        far.append(flip(send_far, "seq", blocks, CORES))
        passed, total = lax.optimization_barrier((far[1], total))
        far.append(flip(passed, "seq", blocks, CORES))
        own_mine, own_theirs, own_part = out_cut()
        send_part, total, far[1] = lax.optimization_barrier((own_part, total, far[1]))
        out_d = flip(send_part, "dp", n, 3)
        out_e = flip(out_d, "seq", blocks, CORES)
        sent, total, far[1] = lax.optimization_barrier((own_mine, total, far[1]))
        out_x = flip(sent, "dp", n, 1)
        out_y = flip(sent, "dp", n, 2)
        total = add_product(
            tok_other, [x_most, *far[:3]], lambda: places_near(shard, (1,)) + places_far(shard)[:3], total
        )
        total = add_product(tok_other, [x_last, from_y], functools.partial(places_last, shard), total)
        pieces, places = far[3:], lambda: places_far(shard)[3:]
    else:
        tok_other = flip(tok_own, "seq", blocks, 1)
        whole = cut(lambda: 0, CUT_LIMIT, shard)[0]
        pieces, places = [lax.all_gather(whole, "dp", axis=0, tiled=True)], lambda: [0]
    extra = [] if total is None else [total]

    act, values, state, chip = call(
        functools.partial(project_states, len(pieces), places),
        [
            array((CORES, rows, 2 * HEAD), bf16),
            array((CORES, rows, HEAD), bf16),
            array((CORES, HEAD, HEAD), f32),
            array((HEAD, HEAD), bf16),
        ],
        [tok_own, tok_other, *pieces, *extra],
        [VMEM] * 4, [VMEM] * (2 + len(pieces) + len(extra)),
        flops=2 * CORES * rows * sum(piece.shape[0] for piece in pieces) * 3 * HEAD,
    )
    got, group = [], chip
    for step in range((blocks // CORES).bit_length() - 1):
        if got:
            group = (group.astype(f32) + got[-1].astype(f32)).astype(bf16)
            if grid:
                group, out_d = lax.optimization_barrier((group, out_d))
        got.append(flip(group, "seq", blocks, CORES << step))
    scored, halves, outs = act, [], [array((CORES, rows, HEAD), f32)]
    if grid:
        scored, out_x, out_y = lax.optimization_barrier((act, out_x, out_y))
        halves = [out_d, out_e]
        outs.append(array((HEAD, width), bf16))
    intra, *columns = call(
        attend, outs, [scored, values, *halves], [VMEM] * len(outs), [VMEM] * (2 + len(halves)),
        flops=rows * HEAD * 1000000,
    )
    if grid:
        mine = [own_mine, out_x, out_y, *columns]
        theirs = [own_theirs] + [flip(piece, "seq", blocks, 1) for piece in mine[1:]]
    normed_own, normed_other = call(
        functools.partial(normalise, len(got)),
        [array((rows, HEAD), bf16)] * 2,
        [act, state, intra, norm_gain.reshape(heads, HEAD), *got],
        [VMEM] * 2, [VMEM] * (4 + len(got)), flops=rows * HEAD * 1000000,
    )
    normed_got = flip(normed_other, "seq", blocks, 1)

    if grid:
        places = functools.partial(places_out, width)
    else:
        mine = [lax.all_gather(out_cut()[0], "dp", axis=1, tiled=True)]
        theirs = [flip(mine[0], "seq", blocks, 1)]
        places = lambda: [0]
    mixed = call(
        functools.partial(mix, len(mine), places),
        array((rows, n * width), bf16),
        [normed_own, normed_got, *mine, *theirs],
        HBM, [VMEM] * (2 + 2 * len(mine)),
        scratch=[pltpu.VMEM((rows, n * width), bf16), pltpu.SemaphoreType.DMA((16,))],
        flops=2 * rows * 2 * HEAD * n * width, moved=2 * rows * n * width,
    )
    return mixed[None]


def solution(mesh):
    n, blocks = mesh.shape["dp"], mesh.shape["seq"]
    return jax.shard_map(
        functools.partial(shards, n, blocks),
        mesh=mesh,
        in_specs=(P("dp", "seq", None), P("dp", None), P(), P(None, "dp")),
        out_specs=P("dp", "seq", None),
        check_vma=False,
    )
```

```python
import functools

import jax
import jax.numpy as jnp
from jax import lax
from jax.experimental import pallas as pl
from jax.experimental.pallas import tpu as pltpu
from jax.sharding import PartitionSpec as P

HEAD = 128
CORES = 2
VMEM_LIMIT = 24 * 1024 * 1024
FIRST_LIMIT = 53 * 1024 * 1024
CUT_LIMIT = 52 * 1024 * 1024
VMEM = pl.BlockSpec(memory_space=pltpu.VMEM)
HBM = pl.BlockSpec(memory_space=pltpu.HBM)


def flip(x, axis, size, mask):
    return lax.ppermute(x, axis, [(i, i ^ mask) for i in range(size)])


def dot(a, b, contract=((1,), (0,))):
    return lax.dot_general(a, b, (contract, ((), ())), preferred_element_type=jnp.float32)


def position():
    return lax.axis_index("dp"), lax.rem(lax.axis_index("seq"), CORES)


def parity():
    return lax.rem(lax.axis_index("seq") // CORES, 2)


def quarter_of():
    return lax.rem(lax.axis_index("seq") // CORES, 4)


def cut_qkv(first, w_qkv, out, *refs):
    pieces, sem = refs[:-1], refs[-1]
    _, core = position()
    feat = w_qkv.shape[1] // 3
    rows = pl.ds(pl.multiple_of(first(), 16), out.shape[0])
    copies = []
    for j in range(3):
        cols = pl.ds(pl.multiple_of(j * feat + core * HEAD, HEAD), HEAD)
        target = out.at[:, j * HEAD : (j + 1) * HEAD]
        copies.append(pltpu.make_async_copy(w_qkv.at[rows, cols], target, sem.at[j]))
        copies[-1].start()
    for copy in copies:
        copy.wait()
    at = 0
    for piece in pieces:
        piece[...] = out[at : at + piece.shape[0], :]
        at += piece.shape[0]


def cut_out(w_out, mine, theirs, part):
    _, core = position()
    rows = pl.ds(pl.multiple_of(core * HEAD, HEAD), HEAD)
    other = pl.ds(pl.multiple_of((1 - core) * HEAD, HEAD), HEAD)
    mine[...] = w_out[rows, :]
    theirs[...] = w_out[other, :]
    half = part.shape[1]
    part[...] = w_out[rows, pl.ds(pl.multiple_of(parity() * half, half), half)]


def product(tok_a, tok_b, pieces, places):
    cols = [
        pl.ds(pl.multiple_of(place, 128), piece.shape[0]) for piece, place in zip(pieces, places)
    ]
    weights = jnp.concatenate([piece[...] for piece in pieces], axis=0)
    blocks = [jnp.concatenate([ref[:, c] for c in cols], axis=1) for ref in (tok_a, tok_b)]
    return jnp.concatenate([dot(block, weights) for block in blocks], axis=0)


def places_near(shard, offsets):
    at = lax.axis_index("dp")
    return [(at ^ offset) * shard for offset in offsets]


def places_last(shard):
    near_x, near_y = places_near(shard, (1, 2))
    return [near_x + 3 * (shard // 4), near_y]


def places_far(shard):
    start = places_near(shard, (3,))[0]
    mine = quarter_of()
    return [start + (mine ^ mask) * (shard // 4) for mask in (0, 2, 1, 3)]


def project(count, places, tok_a, tok_b, *refs):
    pieces, before, total = refs[:count], refs[count:-1], refs[-1]
    term = product(tok_a, tok_b, pieces, places())
    total[...] = before[0][...] + term if before else term


def project_states(count, places, tok_a, tok_b, *refs):
    pieces, before = refs[:count], refs[count:-4]
    act_out, value_out, state_out, chip_out = refs[-4:]
    proj = product(tok_a, tok_b, pieces, places())
    if before:
        proj = before[0][...] + proj
    rows = value_out.shape[1]
    chip = None
    for b in range(CORES):
        part = proj[b * rows : (b + 1) * rows, :]
        act = part[:, : 2 * HEAD]
        act = (act / (1.0 + jnp.exp(-act))).astype(jnp.bfloat16)
        values = part[:, 2 * HEAD :].astype(jnp.bfloat16)
        state = dot(act[:, HEAD:], values, ((0,), (0,)))
        chip = state if chip is None else chip + state
        act_out[b] = act
        value_out[b] = values
        state_out[b] = state
    chip_out[...] = chip.astype(jnp.bfloat16)


def attend(act, values, *refs):
    if len(refs) > 1:
        own_half, other_half, intra_out, columns_out = refs
        half = own_half.shape[1]
        columns_out[:, pl.ds(pl.multiple_of(parity() * half, half), half)] = own_half[...]
        columns_out[:, pl.ds(pl.multiple_of((1 - parity()) * half, half), half)] = other_half[...]
    else:
        intra_out = refs[0]
    rows = intra_out.shape[1]
    row = lax.broadcasted_iota(jnp.int32, (rows, rows), 0)
    col = lax.broadcasted_iota(jnp.int32, (rows, rows), 1)
    for b in range(CORES):
        scores = dot(act[b, :, :HEAD], act[b, :, HEAD:], ((1,), (1,)))
        scores = jnp.where(row >= col, scores, 0.0).astype(jnp.bfloat16)
        intra_out[b] = dot(scores, values[b])


def normalise(steps, act, state, intra, gain, *refs):
    got, (own_out, other_out) = refs[:steps], refs[steps:]
    _, core = position()
    chip_at = lax.axis_index("seq") // CORES
    base = jnp.zeros((HEAD, HEAD), jnp.float32)
    for step, ref in enumerate(got):
        base = base + jnp.where((chip_at >> step) % 2 == 1, ref[...].astype(jnp.float32), 0.0)
    odd = core == 1
    own_prefix = jnp.where(odd, base + state[1], base)
    other_prefix = jnp.where(odd, base, base + state[0])
    scale = gain[pl.ds(core, 1), :]
    for b, (prefix, out) in enumerate(((own_prefix, own_out), (other_prefix, other_out))):
        attended = dot(act[b, :, :HEAD], prefix.astype(jnp.bfloat16)) + intra[b]
        meansq = jnp.mean(attended * attended, axis=-1, keepdims=True)
        out[...] = (attended * lax.rsqrt(meansq + 1e-06) * scale).astype(jnp.bfloat16)


def mix(count, places, own, other, *refs):
    mine, theirs, (out, stage, sem) = refs[:count], refs[count : 2 * count], refs[2 * count :]
    normed = jnp.concatenate([own[...], other[...]], axis=1)
    copies = []
    slot = 0
    for my_rows, their_rows, place in zip(mine, theirs, places()):
        width = my_rows.shape[1]
        step = min(width, 512)
        for at_col in range(0, width, step):
            part = slice(at_col, at_col + step)
            weights = jnp.concatenate([my_rows[:, part], their_rows[:, part]], axis=0)
            here = stage.at[:, slot : slot + step]
            here[...] = dot(normed, weights).astype(jnp.bfloat16)
            cols = pl.ds(pl.multiple_of(place + at_col, 128), step)
            copies.append(pltpu.make_async_copy(here, out.at[:, cols], sem.at[len(copies)]))
            copies[-1].start()
            slot += step
    for copy in copies:
        copy.wait()


def places_out(width):
    at = lax.axis_index("dp")
    return [(at ^ offset) * width for offset in range(4)]


def shards(n, blocks, tokens, w_qkv, norm_gain, w_out):
    tok_own = tokens[0]
    rows, depth = tok_own.shape
    shard = w_qkv.shape[0]
    heads = norm_gain.shape[0] // HEAD
    bf16, f32 = jnp.bfloat16, jnp.float32

    def call(kernel, outs, ins, out_specs, in_specs, scratch=(), flops=0, moved=0, limit=VMEM_LIMIT):
        return pl.pallas_call(
            kernel,
            out_shape=outs,
            in_specs=in_specs,
            out_specs=out_specs,
            scratch_shapes=scratch,
            compiler_params=pltpu.CompilerParams(vmem_limit_bytes=limit),
            cost_estimate=pl.CostEstimate(flops=flops, bytes_accessed=moved, transcendentals=0),
        )(*ins)

    def array(shape, kind):
        return jax.ShapeDtypeStruct(shape, kind)

    def add_product(pieces, places, total=None):
        extra = [] if total is None else [total]
        return call(
            functools.partial(project, len(pieces), places),
            array((CORES * rows, 3 * HEAD), f32),
            [tok_own, tok_other, *pieces, *extra],
            VMEM, [VMEM] * (2 + len(pieces) + len(extra)),
            flops=rows * HEAD * (1 if total is not None else 1000000),
        )

    tok_other = flip(tok_own, "seq", blocks, 1)
    width = w_out.shape[1]
    grid = n == 4 and blocks % (4 * CORES) == 0 and shard % 512 == 0 and width % 256 == 0

    def cut(first, limit, *sizes):
        return call(
            functools.partial(cut_qkv, first),
            [array((size, 3 * HEAD), bf16) for size in sizes], [w_qkv], [VMEM] * len(sizes), [HBM],
            scratch=[pltpu.SemaphoreType.DMA((3,))], limit=limit,
        )

    out_cut = functools.partial(
        call, cut_out, [array((HEAD, width), bf16)] * 2 + [array((HEAD, width // 2), bf16)],
        [w_out], [VMEM] * 3, [VMEM]
    )
    total = None
    if grid:
        quarter = shard // 4
        part = cut(lambda: quarter_of() * quarter, FIRST_LIMIT, quarter)[0]
        far = [flip(part, "dp", n, 3)]
        own, most, last = cut(lambda: 0, CUT_LIMIT, shard, 3 * quarter, quarter)
        x_most = flip(most, "dp", n, 1)
        send_last, here = lax.optimization_barrier((last, far[0]))
        x_last = flip(send_last, "dp", n, 1)
        from_y = flip(own, "dp", n, 2)
        far.append(flip(far[0], "seq", blocks, CORES * 2))
        here, own = lax.optimization_barrier((far[0], own))
        total = add_product([own], functools.partial(places_near, shard, (0,)))
        send_far, total = lax.optimization_barrier((far[0], total))
        far.append(flip(send_far, "seq", blocks, CORES))
        passed, total = lax.optimization_barrier((far[1], total))
        far.append(flip(passed, "seq", blocks, CORES))
        own_mine, own_theirs, own_part = out_cut()
        send_part, total, far[1] = lax.optimization_barrier((own_part, total, far[1]))
        out_d = flip(send_part, "dp", n, 3)
        out_e = flip(out_d, "seq", blocks, CORES)
        sent, total, far[1] = lax.optimization_barrier((own_mine, total, far[1]))
        out_x = flip(sent, "dp", n, 1)
        out_y = flip(sent, "dp", n, 2)
        total = add_product(
            [x_most, *far[:3]], lambda: places_near(shard, (1,)) + places_far(shard)[:3], total
        )
        total = add_product([x_last, from_y], functools.partial(places_last, shard), total)
        pieces, places = far[3:], lambda: places_far(shard)[3:]
    else:
        whole = cut(lambda: 0, CUT_LIMIT, shard)[0]
        pieces, places = [lax.all_gather(whole, "dp", axis=0, tiled=True)], lambda: [0]
    extra = [] if total is None else [total]

    act, values, state, chip = call(
        functools.partial(project_states, len(pieces), places),
        [
            array((CORES, rows, 2 * HEAD), bf16),
            array((CORES, rows, HEAD), bf16),
            array((CORES, HEAD, HEAD), f32),
            array((HEAD, HEAD), bf16),
        ],
        [tok_own, tok_other, *pieces, *extra],
        [VMEM] * 4, [VMEM] * (2 + len(pieces) + len(extra)),
        flops=2 * CORES * rows * sum(piece.shape[0] for piece in pieces) * 3 * HEAD,
    )
    got, group = [], chip
    for step in range((blocks // CORES).bit_length() - 1):
        if got:
            group = (group.astype(f32) + got[-1].astype(f32)).astype(bf16)
            if grid:
                group, out_d = lax.optimization_barrier((group, out_d))
        got.append(flip(group, "seq", blocks, CORES << step))
    scored, halves, outs = act, [], [array((CORES, rows, HEAD), f32)]
    if grid:
        scored, out_x, out_y = lax.optimization_barrier((act, out_x, out_y))
        halves = [out_d, out_e]
        outs.append(array((HEAD, width), bf16))
    intra, *columns = call(
        attend, outs, [scored, values, *halves], [VMEM] * len(outs), [VMEM] * (2 + len(halves)),
        flops=rows * HEAD * 1000000,
    )
    if grid:
        mine = [own_mine, out_x, out_y, *columns]
        theirs = [own_theirs] + [flip(piece, "seq", blocks, 1) for piece in mine[1:]]
    normed_own, normed_other = call(
        functools.partial(normalise, len(got)),
        [array((rows, HEAD), bf16)] * 2,
        [act, state, intra, norm_gain.reshape(heads, HEAD), *got],
        [VMEM] * 2, [VMEM] * (4 + len(got)), flops=rows * HEAD * 1000000,
    )
    normed_got = flip(normed_other, "seq", blocks, 1)

    if grid:
        places = functools.partial(places_out, width)
    else:
        mine = [lax.all_gather(out_cut()[0], "dp", axis=1, tiled=True)]
        theirs = [flip(mine[0], "seq", blocks, 1)]
        places = lambda: [0]
    mixed = call(
        functools.partial(mix, len(mine), places),
        array((rows, n * width), bf16),
        [normed_own, normed_got, *mine, *theirs],
        HBM, [VMEM] * (2 + 2 * len(mine)),
        scratch=[pltpu.VMEM((rows, n * width), bf16), pltpu.SemaphoreType.DMA((16,))],
        flops=2 * rows * 2 * HEAD * n * width, moved=2 * rows * n * width,
    )
    return mixed[None]


def solution(mesh):
    n, blocks = mesh.shape["dp"], mesh.shape["seq"]
    return jax.shard_map(
        functools.partial(shards, n, blocks),
        mesh=mesh,
        in_specs=(P("dp", "seq", None), P("dp", None), P(), P(None, "dp")),
        out_specs=P("dp", "seq", None),
        check_vma=False,
    )
```

```python
import functools

import jax
import jax.numpy as jnp
from jax import lax
from jax.experimental import pallas as pl
from jax.experimental.pallas import tpu as pltpu
from jax.sharding import PartitionSpec as P

HEAD = 128
CORES = 2
VMEM_LIMIT = 24 * 1024 * 1024
FIRST_LIMIT = 53 * 1024 * 1024
CUT_LIMIT = 52 * 1024 * 1024
VMEM = pl.BlockSpec(memory_space=pltpu.VMEM)
HBM = pl.BlockSpec(memory_space=pltpu.HBM)


def flip(x, axis, size, mask):
    return lax.ppermute(x, axis, [(i, i ^ mask) for i in range(size)])


def dot(a, b, contract=((1,), (0,))):
    return lax.dot_general(a, b, (contract, ((), ())), preferred_element_type=jnp.float32)


def position():
    return lax.axis_index("dp"), lax.rem(lax.axis_index("seq"), CORES)


def parity():
    return lax.rem(lax.axis_index("seq") // CORES, 2)


def quarter_of():
    return lax.rem(lax.axis_index("seq") // CORES, 4)


def cut_qkv(first, w_qkv, out, *refs):
    pieces, sem = refs[:-1], refs[-1]
    _, core = position()
    feat = w_qkv.shape[1] // 3
    rows = pl.ds(pl.multiple_of(first(), 16), out.shape[0])
    copies = []
    for j in range(3):
        cols = pl.ds(pl.multiple_of(j * feat + core * HEAD, HEAD), HEAD)
        target = out.at[:, j * HEAD : (j + 1) * HEAD]
        copies.append(pltpu.make_async_copy(w_qkv.at[rows, cols], target, sem.at[j]))
        copies[-1].start()
    for copy in copies:
        copy.wait()
    at = 0
    for piece in pieces:
        piece[...] = out[at : at + piece.shape[0], :]
        at += piece.shape[0]


def cut_out(w_out, mine, theirs, part):
    _, core = position()
    rows = pl.ds(pl.multiple_of(core * HEAD, HEAD), HEAD)
    other = pl.ds(pl.multiple_of((1 - core) * HEAD, HEAD), HEAD)
    mine[...] = w_out[rows, :]
    theirs[...] = w_out[other, :]
    half = part.shape[1]
    part[...] = w_out[rows, pl.ds(pl.multiple_of(parity() * half, half), half)]


def product(tok_a, tok_b, pieces, places):
    cols = [
        pl.ds(pl.multiple_of(place, 128), piece.shape[0]) for piece, place in zip(pieces, places)
    ]
    weights = jnp.concatenate([piece[...] for piece in pieces], axis=0)
    blocks = [jnp.concatenate([ref[:, c] for c in cols], axis=1) for ref in (tok_a, tok_b)]
    return jnp.concatenate([dot(block, weights) for block in blocks], axis=0)


def places_near(shard, offsets):
    at = lax.axis_index("dp")
    return [(at ^ offset) * shard for offset in offsets]


def places_last(shard):
    near_x, near_y = places_near(shard, (1, 2))
    return [near_x + 3 * (shard // 4), near_y]


def places_far(shard):
    start = places_near(shard, (3,))[0]
    mine = quarter_of()
    return [start + (mine ^ mask) * (shard // 4) for mask in (0, 2, 1, 3)]


def project(count, places, tok_a, tok_b, *refs):
    pieces, before, total = refs[:count], refs[count:-1], refs[-1]
    term = product(tok_a, tok_b, pieces, places())
    total[...] = before[0][...] + term if before else term


def project_states(count, places, tok_a, tok_b, *refs):
    pieces, before = refs[:count], refs[count:-4]
    act_out, value_out, state_out, chip_out = refs[-4:]
    proj = product(tok_a, tok_b, pieces, places())
    if before:
        proj = before[0][...] + proj
    rows = value_out.shape[1]
    chip = None
    for b in range(CORES):
        part = proj[b * rows : (b + 1) * rows, :]
        act = part[:, : 2 * HEAD]
        act = (act / (1.0 + jnp.exp(-act))).astype(jnp.bfloat16)
        values = part[:, 2 * HEAD :].astype(jnp.bfloat16)
        state = dot(act[:, HEAD:], values, ((0,), (0,)))
        chip = state if chip is None else chip + state
        act_out[b] = act
        value_out[b] = values
        state_out[b] = state
    chip_out[...] = chip.astype(jnp.bfloat16)


def attend(act, values, *refs):
    if len(refs) > 1:
        own_half, other_half, intra_out, columns_out = refs
        half = own_half.shape[1]
        columns_out[:, pl.ds(pl.multiple_of(parity() * half, half), half)] = own_half[...]
        columns_out[:, pl.ds(pl.multiple_of((1 - parity()) * half, half), half)] = other_half[...]
    else:
        intra_out = refs[0]
    rows = intra_out.shape[1]
    row = lax.broadcasted_iota(jnp.int32, (rows, rows), 0)
    col = lax.broadcasted_iota(jnp.int32, (rows, rows), 1)
    for b in range(CORES):
        scores = dot(act[b, :, :HEAD], act[b, :, HEAD:], ((1,), (1,)))
        scores = jnp.where(row >= col, scores, 0.0).astype(jnp.bfloat16)
        intra_out[b] = dot(scores, values[b])


def normalise(steps, act, state, intra, gain, *refs):
    got, (own_out, other_out) = refs[:steps], refs[steps:]
    _, core = position()
    chip_at = lax.axis_index("seq") // CORES
    base = jnp.zeros((HEAD, HEAD), jnp.float32)
    for step, ref in enumerate(got):
        base = base + jnp.where((chip_at >> step) % 2 == 1, ref[...].astype(jnp.float32), 0.0)
    odd = core == 1
    own_prefix = jnp.where(odd, base + state[1], base)
    other_prefix = jnp.where(odd, base, base + state[0])
    scale = gain[pl.ds(core, 1), :]
    for b, (prefix, out) in enumerate(((own_prefix, own_out), (other_prefix, other_out))):
        attended = dot(act[b, :, :HEAD], prefix.astype(jnp.bfloat16)) + intra[b]
        meansq = jnp.mean(attended * attended, axis=-1, keepdims=True)
        out[...] = (attended * lax.rsqrt(meansq + 1e-06) * scale).astype(jnp.bfloat16)


def mix(count, places, own, other, *refs):
    mine, theirs, (out, stage, sem) = refs[:count], refs[count : 2 * count], refs[2 * count :]
    normed = jnp.concatenate([own[...], other[...]], axis=1)
    copies = []
    slot = 0
    for i, (my_rows, their_rows, place) in enumerate(zip(mine, theirs, places())):
        width = my_rows.shape[1]
        step = min(width, 1024 if i < count - 1 else 512)
        for at_col in range(0, width, step):
            part = slice(at_col, at_col + step)
            weights = jnp.concatenate([my_rows[:, part], their_rows[:, part]], axis=0)
            here = stage.at[:, slot : slot + step]
            here[...] = dot(normed, weights).astype(jnp.bfloat16)
            cols = pl.ds(pl.multiple_of(place + at_col, 128), step)
            copies.append(pltpu.make_async_copy(here, out.at[:, cols], sem.at[len(copies)]))
            copies[-1].start()
            slot += step
    for copy in copies:
        copy.wait()


def places_out(width):
    at = lax.axis_index("dp")
    return [(at ^ offset) * width for offset in range(4)]


def shards(n, blocks, tokens, w_qkv, norm_gain, w_out):
    tok_own = tokens[0]
    rows, depth = tok_own.shape
    shard = w_qkv.shape[0]
    heads = norm_gain.shape[0] // HEAD
    bf16, f32 = jnp.bfloat16, jnp.float32

    def call(kernel, outs, ins, out_specs, in_specs, scratch=(), flops=0, moved=0, limit=VMEM_LIMIT):
        return pl.pallas_call(
            kernel,
            out_shape=outs,
            in_specs=in_specs,
            out_specs=out_specs,
            scratch_shapes=scratch,
            compiler_params=pltpu.CompilerParams(vmem_limit_bytes=limit),
            cost_estimate=pl.CostEstimate(flops=flops, bytes_accessed=moved, transcendentals=0),
        )(*ins)

    def array(shape, kind):
        return jax.ShapeDtypeStruct(shape, kind)

    def add_product(pieces, places, total=None):
        extra = [] if total is None else [total]
        return call(
            functools.partial(project, len(pieces), places),
            array((CORES * rows, 3 * HEAD), f32),
            [tok_own, tok_other, *pieces, *extra],
            VMEM, [VMEM] * (2 + len(pieces) + len(extra)),
            flops=rows * HEAD * (1 if total is not None else 1000000),
        )

    tok_other = flip(tok_own, "seq", blocks, 1)
    width = w_out.shape[1]
    grid = n == 4 and blocks % (4 * CORES) == 0 and shard % 512 == 0 and width % 256 == 0

    def cut(first, limit, *sizes):
        return call(
            functools.partial(cut_qkv, first),
            [array((size, 3 * HEAD), bf16) for size in sizes], [w_qkv], [VMEM] * len(sizes), [HBM],
            scratch=[pltpu.SemaphoreType.DMA((3,))], limit=limit,
        )

    out_cut = functools.partial(
        call, cut_out, [array((HEAD, width), bf16)] * 2 + [array((HEAD, width // 2), bf16)],
        [w_out], [VMEM] * 3, [VMEM]
    )
    total = None
    if grid:
        quarter = shard // 4
        part = cut(lambda: quarter_of() * quarter, FIRST_LIMIT, quarter)[0]
        far = [flip(part, "dp", n, 3)]
        own, most, last = cut(lambda: 0, CUT_LIMIT, shard, 3 * quarter, quarter)
        x_most = flip(most, "dp", n, 1)
        send_last, here = lax.optimization_barrier((last, far[0]))
        x_last = flip(send_last, "dp", n, 1)
        from_y = flip(own, "dp", n, 2)
        far.append(flip(far[0], "seq", blocks, CORES * 2))
        here, own = lax.optimization_barrier((far[0], own))
        total = add_product([own], functools.partial(places_near, shard, (0,)))
        send_far, total = lax.optimization_barrier((far[0], total))
        far.append(flip(send_far, "seq", blocks, CORES))
        passed, total = lax.optimization_barrier((far[1], total))
        far.append(flip(passed, "seq", blocks, CORES))
        own_mine, own_theirs, own_part = out_cut()
        send_part, total, far[1] = lax.optimization_barrier((own_part, total, far[1]))
        out_d = flip(send_part, "dp", n, 3)
        out_e = flip(out_d, "seq", blocks, CORES)
        sent, total, far[1] = lax.optimization_barrier((own_mine, total, far[1]))
        out_x = flip(sent, "dp", n, 1)
        out_y = flip(sent, "dp", n, 2)
        total = add_product(
            [x_most, *far[:3]], lambda: places_near(shard, (1,)) + places_far(shard)[:3], total
        )
        total = add_product([x_last, from_y], functools.partial(places_last, shard), total)
        pieces, places = far[3:], lambda: places_far(shard)[3:]
    else:
        whole = cut(lambda: 0, CUT_LIMIT, shard)[0]
        pieces, places = [lax.all_gather(whole, "dp", axis=0, tiled=True)], lambda: [0]
    extra = [] if total is None else [total]

    act, values, state, chip = call(
        functools.partial(project_states, len(pieces), places),
        [
            array((CORES, rows, 2 * HEAD), bf16),
            array((CORES, rows, HEAD), bf16),
            array((CORES, HEAD, HEAD), f32),
            array((HEAD, HEAD), bf16),
        ],
        [tok_own, tok_other, *pieces, *extra],
        [VMEM] * 4, [VMEM] * (2 + len(pieces) + len(extra)),
        flops=2 * CORES * rows * sum(piece.shape[0] for piece in pieces) * 3 * HEAD,
    )
    got, group = [], chip
    for step in range((blocks // CORES).bit_length() - 1):
        if got:
            group = (group.astype(f32) + got[-1].astype(f32)).astype(bf16)
            if grid:
                group, out_d = lax.optimization_barrier((group, out_d))
        got.append(flip(group, "seq", blocks, CORES << step))
    scored, halves, outs = act, [], [array((CORES, rows, HEAD), f32)]
    if grid:
        scored, out_x, out_y = lax.optimization_barrier((act, out_x, out_y))
        halves = [out_d, out_e]
        outs.append(array((HEAD, width), bf16))
    intra, *columns = call(
        attend, outs, [scored, values, *halves], [VMEM] * len(outs), [VMEM] * (2 + len(halves)),
        flops=rows * HEAD * 1000000,
    )
    if grid:
        mine = [own_mine, out_x, out_y, *columns]
        theirs = [own_theirs] + [flip(piece, "seq", blocks, 1) for piece in mine[1:]]
    normed_own, normed_other = call(
        functools.partial(normalise, len(got)),
        [array((rows, HEAD), bf16)] * 2,
        [act, state, intra, norm_gain.reshape(heads, HEAD), *got],
        [VMEM] * 2, [VMEM] * (4 + len(got)), flops=rows * HEAD * 1000000,
    )
    normed_got = flip(normed_other, "seq", blocks, 1)

    if grid:
        places = functools.partial(places_out, width)
    else:
        mine = [lax.all_gather(out_cut()[0], "dp", axis=1, tiled=True)]
        theirs = [flip(mine[0], "seq", blocks, 1)]
        places = lambda: [0]
    mixed = call(
        functools.partial(mix, len(mine), places),
        array((rows, n * width), bf16),
        [normed_own, normed_got, *mine, *theirs],
        HBM, [VMEM] * (2 + 2 * len(mine)),
        scratch=[pltpu.VMEM((rows, n * width), bf16), pltpu.SemaphoreType.DMA((16,))],
        flops=2 * rows * 2 * HEAD * n * width, moved=2 * rows * n * width,
    )
    return mixed[None]


def solution(mesh):
    n, blocks = mesh.shape["dp"], mesh.shape["seq"]
    return jax.shard_map(
        functools.partial(shards, n, blocks),
        mesh=mesh,
        in_specs=(P("dp", "seq", None), P("dp", None), P(), P(None, "dp")),
        out_specs=P("dp", "seq", None),
        check_vma=False,
    )
```

```python
import functools

import jax
import jax.numpy as jnp
from jax import lax
from jax.experimental import pallas as pl
from jax.experimental.pallas import tpu as pltpu
from jax.sharding import PartitionSpec as P

HEAD = 128
CORES = 2
VMEM_LIMIT = 24 * 1024 * 1024
FIRST_LIMIT = 53 * 1024 * 1024
CUT_LIMIT = 52 * 1024 * 1024
VMEM = pl.BlockSpec(memory_space=pltpu.VMEM)
HBM = pl.BlockSpec(memory_space=pltpu.HBM)


def flip(x, axis, size, mask):
    return lax.ppermute(x, axis, [(i, i ^ mask) for i in range(size)])


def dot(a, b, contract=((1,), (0,))):
    return lax.dot_general(a, b, (contract, ((), ())), preferred_element_type=jnp.float32)


def position():
    return lax.axis_index("dp"), lax.rem(lax.axis_index("seq"), CORES)


def parity():
    return lax.rem(lax.axis_index("seq") // CORES, 2)


def quarter_of():
    return lax.rem(lax.axis_index("seq") // CORES, 4)


def cut_qkv(first, w_qkv, out, *refs):
    pieces, sem = refs[:-1], refs[-1]
    _, core = position()
    feat = w_qkv.shape[1] // 3
    rows = pl.ds(pl.multiple_of(first(), 16), out.shape[0])
    copies = []
    for j in range(3):
        cols = pl.ds(pl.multiple_of(j * feat + core * HEAD, HEAD), HEAD)
        target = out.at[:, j * HEAD : (j + 1) * HEAD]
        copies.append(pltpu.make_async_copy(w_qkv.at[rows, cols], target, sem.at[j]))
        copies[-1].start()
    for copy in copies:
        copy.wait()
    at = 0
    for piece in pieces:
        piece[...] = out[at : at + piece.shape[0], :]
        at += piece.shape[0]


def cut_out(w_out, mine, theirs, part):
    _, core = position()
    rows = pl.ds(pl.multiple_of(core * HEAD, HEAD), HEAD)
    other = pl.ds(pl.multiple_of((1 - core) * HEAD, HEAD), HEAD)
    mine[...] = w_out[rows, :]
    theirs[...] = w_out[other, :]
    half = part.shape[1]
    part[...] = w_out[rows, pl.ds(pl.multiple_of(parity() * half, half), half)]


def product(tok_a, tok_b, pieces, places):
    cols = [
        pl.ds(pl.multiple_of(place, 128), piece.shape[0]) for piece, place in zip(pieces, places)
    ]
    weights = jnp.concatenate([piece[...] for piece in pieces], axis=0)
    blocks = [jnp.concatenate([ref[:, c] for c in cols], axis=1) for ref in (tok_a, tok_b)]
    return jnp.concatenate([dot(block, weights) for block in blocks], axis=0)


def places_near(shard, offsets):
    at = lax.axis_index("dp")
    return [(at ^ offset) * shard for offset in offsets]


def places_last(shard):
    near_x, near_y = places_near(shard, (1, 2))
    return [near_x + 3 * (shard // 4), near_y]


def places_far(shard):
    start = places_near(shard, (3,))[0]
    mine = quarter_of()
    return [start + (mine ^ mask) * (shard // 4) for mask in (0, 2, 1, 3)]


def project(count, places, tok_a, tok_b, *refs):
    pieces, before, total = refs[:count], refs[count:-1], refs[-1]
    term = product(tok_a, tok_b, pieces, places())
    total[...] = before[0][...] + term if before else term


def project_states(count, places, tok_a, tok_b, *refs):
    pieces, before = refs[:count], refs[count:-4]
    act_out, value_out, state_out, chip_out = refs[-4:]
    proj = product(tok_a, tok_b, pieces, places())
    if before:
        proj = before[0][...] + proj
    rows = value_out.shape[1]
    chip = None
    for b in range(CORES):
        part = proj[b * rows : (b + 1) * rows, :]
        act = part[:, : 2 * HEAD]
        act = (act / (1.0 + jnp.exp(-act))).astype(jnp.bfloat16)
        values = part[:, 2 * HEAD :].astype(jnp.bfloat16)
        state = dot(act[:, HEAD:], values, ((0,), (0,)))
        chip = state if chip is None else chip + state
        act_out[b] = act
        value_out[b] = values
        state_out[b] = state
    chip_out[...] = chip.astype(jnp.bfloat16)


def attend(act, values, *refs):
    if len(refs) > 1:
        own_half, other_half, intra_out, columns_out = refs
        half = own_half.shape[1]
        columns_out[:, pl.ds(pl.multiple_of(parity() * half, half), half)] = own_half[...]
        columns_out[:, pl.ds(pl.multiple_of((1 - parity()) * half, half), half)] = other_half[...]
    else:
        intra_out = refs[0]
    rows = intra_out.shape[1]
    row = lax.broadcasted_iota(jnp.int32, (rows, rows), 0)
    col = lax.broadcasted_iota(jnp.int32, (rows, rows), 1)
    for b in range(CORES):
        scores = dot(act[b, :, :HEAD], act[b, :, HEAD:], ((1,), (1,)))
        scores = jnp.where(row >= col, scores, 0.0).astype(jnp.bfloat16)
        intra_out[b] = dot(scores, values[b])


def normalise(steps, act, state, intra, gain, *refs):
    got, (own_out, other_out) = refs[:steps], refs[steps:]
    _, core = position()
    chip_at = lax.axis_index("seq") // CORES
    base = jnp.zeros((HEAD, HEAD), jnp.float32)
    for step, ref in enumerate(got):
        base = base + jnp.where((chip_at >> step) % 2 == 1, ref[...].astype(jnp.float32), 0.0)
    odd = core == 1
    own_prefix = jnp.where(odd, base + state[1], base)
    other_prefix = jnp.where(odd, base, base + state[0])
    scale = gain[pl.ds(core, 1), :]
    for b, (prefix, out) in enumerate(((own_prefix, own_out), (other_prefix, other_out))):
        attended = dot(act[b, :, :HEAD], prefix.astype(jnp.bfloat16)) + intra[b]
        meansq = jnp.mean(attended * attended, axis=-1, keepdims=True)
        out[...] = (attended * lax.rsqrt(meansq + 1e-06) * scale).astype(jnp.bfloat16)


def mix(count, places, own, other, *refs):
    mine, theirs, (out, stage, sem) = refs[:count], refs[count : 2 * count], refs[2 * count :]
    normed = jnp.concatenate([own[...], other[...]], axis=1)
    copies = []
    slot = 0
    for my_rows, their_rows, place in zip(mine, theirs, places()):
        width = my_rows.shape[1]
        step = min(width, 256)
        for at_col in range(0, width, step):
            part = slice(at_col, at_col + step)
            weights = jnp.concatenate([my_rows[:, part], their_rows[:, part]], axis=0)
            here = stage.at[:, slot : slot + step]
            here[...] = dot(normed, weights).astype(jnp.bfloat16)
            cols = pl.ds(pl.multiple_of(place + at_col, 128), step)
            copies.append(pltpu.make_async_copy(here, out.at[:, cols], sem.at[len(copies)]))
            copies[-1].start()
            slot += step
    for copy in copies:
        copy.wait()


def places_out(width):
    at = lax.axis_index("dp")
    return [(at ^ offset) * width for offset in range(4)]


def shards(n, blocks, tokens, w_qkv, norm_gain, w_out):
    tok_own = tokens[0]
    rows, depth = tok_own.shape
    shard = w_qkv.shape[0]
    heads = norm_gain.shape[0] // HEAD
    bf16, f32 = jnp.bfloat16, jnp.float32

    def call(kernel, outs, ins, out_specs, in_specs, scratch=(), flops=0, moved=0, limit=VMEM_LIMIT):
        return pl.pallas_call(
            kernel,
            out_shape=outs,
            in_specs=in_specs,
            out_specs=out_specs,
            scratch_shapes=scratch,
            compiler_params=pltpu.CompilerParams(vmem_limit_bytes=limit),
            cost_estimate=pl.CostEstimate(flops=flops, bytes_accessed=moved, transcendentals=0),
        )(*ins)

    def array(shape, kind):
        return jax.ShapeDtypeStruct(shape, kind)

    def add_product(pieces, places, total=None):
        extra = [] if total is None else [total]
        return call(
            functools.partial(project, len(pieces), places),
            array((CORES * rows, 3 * HEAD), f32),
            [tok_own, tok_other, *pieces, *extra],
            VMEM, [VMEM] * (2 + len(pieces) + len(extra)),
            flops=rows * HEAD * (1 if total is not None else 1000000),
        )

    tok_other = flip(tok_own, "seq", blocks, 1)
    width = w_out.shape[1]
    grid = n == 4 and blocks % (4 * CORES) == 0 and shard % 512 == 0 and width % 256 == 0

    def cut(first, limit, *sizes):
        return call(
            functools.partial(cut_qkv, first),
            [array((size, 3 * HEAD), bf16) for size in sizes], [w_qkv], [VMEM] * len(sizes), [HBM],
            scratch=[pltpu.SemaphoreType.DMA((3,))], limit=limit,
        )

    out_cut = functools.partial(
        call, cut_out, [array((HEAD, width), bf16)] * 2 + [array((HEAD, width // 2), bf16)],
        [w_out], [VMEM] * 3, [VMEM]
    )
    total = None
    if grid:
        quarter = shard // 4
        part = cut(lambda: quarter_of() * quarter, FIRST_LIMIT, quarter)[0]
        far = [flip(part, "dp", n, 3)]
        own, most, last = cut(lambda: 0, CUT_LIMIT, shard, 3 * quarter, quarter)
        x_most = flip(most, "dp", n, 1)
        send_last, here = lax.optimization_barrier((last, far[0]))
        x_last = flip(send_last, "dp", n, 1)
        from_y = flip(own, "dp", n, 2)
        far.append(flip(far[0], "seq", blocks, CORES * 2))
        here, own = lax.optimization_barrier((far[0], own))
        total = add_product([own], functools.partial(places_near, shard, (0,)))
        send_far, total = lax.optimization_barrier((far[0], total))
        far.append(flip(send_far, "seq", blocks, CORES))
        passed, total = lax.optimization_barrier((far[1], total))
        far.append(flip(passed, "seq", blocks, CORES))
        own_mine, own_theirs, own_part = out_cut()
        send_part, total, far[1] = lax.optimization_barrier((own_part, total, far[1]))
        out_d = flip(send_part, "dp", n, 3)
        out_e = flip(out_d, "seq", blocks, CORES)
        sent, total, far[1] = lax.optimization_barrier((own_mine, total, far[1]))
        out_x = flip(sent, "dp", n, 1)
        out_y = flip(sent, "dp", n, 2)
        total = add_product(
            [x_most, *far[:3]], lambda: places_near(shard, (1,)) + places_far(shard)[:3], total
        )
        total = add_product([x_last, from_y], functools.partial(places_last, shard), total)
        pieces, places = far[3:], lambda: places_far(shard)[3:]
    else:
        whole = cut(lambda: 0, CUT_LIMIT, shard)[0]
        pieces, places = [lax.all_gather(whole, "dp", axis=0, tiled=True)], lambda: [0]
    extra = [] if total is None else [total]

    act, values, state, chip = call(
        functools.partial(project_states, len(pieces), places),
        [
            array((CORES, rows, 2 * HEAD), bf16),
            array((CORES, rows, HEAD), bf16),
            array((CORES, HEAD, HEAD), f32),
            array((HEAD, HEAD), bf16),
        ],
        [tok_own, tok_other, *pieces, *extra],
        [VMEM] * 4, [VMEM] * (2 + len(pieces) + len(extra)),
        flops=2 * CORES * rows * sum(piece.shape[0] for piece in pieces) * 3 * HEAD,
    )
    got, group = [], chip
    for step in range((blocks // CORES).bit_length() - 1):
        if got:
            group = (group.astype(f32) + got[-1].astype(f32)).astype(bf16)
            if grid:
                group, out_d = lax.optimization_barrier((group, out_d))
        got.append(flip(group, "seq", blocks, CORES << step))
    scored, halves, outs = act, [], [array((CORES, rows, HEAD), f32)]
    if grid:
        scored, out_x, out_y = lax.optimization_barrier((act, out_x, out_y))
        halves = [out_d, out_e]
        outs.append(array((HEAD, width), bf16))
    intra, *columns = call(
        attend, outs, [scored, values, *halves], [VMEM] * len(outs), [VMEM] * (2 + len(halves)),
        flops=rows * HEAD * 1000000,
    )
    if grid:
        mine = [own_mine, out_x, out_y, *columns]
        theirs = [own_theirs] + [flip(piece, "seq", blocks, 1) for piece in mine[1:]]
    normed_own, normed_other = call(
        functools.partial(normalise, len(got)),
        [array((rows, HEAD), bf16)] * 2,
        [act, state, intra, norm_gain.reshape(heads, HEAD), *got],
        [VMEM] * 2, [VMEM] * (4 + len(got)), flops=rows * HEAD * 1000000,
    )
    normed_got = flip(normed_other, "seq", blocks, 1)

    if grid:
        places = functools.partial(places_out, width)
    else:
        mine = [lax.all_gather(out_cut()[0], "dp", axis=1, tiled=True)]
        theirs = [flip(mine[0], "seq", blocks, 1)]
        places = lambda: [0]
    mixed = call(
        functools.partial(mix, len(mine), places),
        array((rows, n * width), bf16),
        [normed_own, normed_got, *mine, *theirs],
        HBM, [VMEM] * (2 + 2 * len(mine)),
        scratch=[pltpu.VMEM((rows, n * width), bf16), pltpu.SemaphoreType.DMA((16,))],
        flops=2 * rows * 2 * HEAD * n * width, moved=2 * rows * n * width,
    )
    return mixed[None]


def solution(mesh):
    n, blocks = mesh.shape["dp"], mesh.shape["seq"]
    return jax.shard_map(
        functools.partial(shards, n, blocks),
        mesh=mesh,
        in_specs=(P("dp", "seq", None), P("dp", None), P(), P(None, "dp")),
        out_specs=P("dp", "seq", None),
        check_vma=False,
    )
```

```python
import functools

import jax
import jax.numpy as jnp
from jax import lax
from jax.experimental import pallas as pl
from jax.experimental.pallas import tpu as pltpu
from jax.sharding import PartitionSpec as P

HEAD = 128
CORES = 2
VMEM_LIMIT = 24 * 1024 * 1024
FIRST_LIMIT = 53 * 1024 * 1024
CUT_LIMIT = 52 * 1024 * 1024
VMEM = pl.BlockSpec(memory_space=pltpu.VMEM)
HBM = pl.BlockSpec(memory_space=pltpu.HBM)


def flip(x, axis, size, mask):
    return lax.ppermute(x, axis, [(i, i ^ mask) for i in range(size)])


def dot(a, b, contract=((1,), (0,))):
    return lax.dot_general(a, b, (contract, ((), ())), preferred_element_type=jnp.float32)


def position():
    return lax.axis_index("dp"), lax.rem(lax.axis_index("seq"), CORES)


def parity():
    return lax.rem(lax.axis_index("seq") // CORES, 2)


def quarter_of():
    return lax.rem(lax.axis_index("seq") // CORES, 4)


def cut_qkv(first, w_qkv, out, *refs):
    pieces, sem = refs[:-1], refs[-1]
    _, core = position()
    feat = w_qkv.shape[1] // 3
    rows = pl.ds(pl.multiple_of(first(), 16), out.shape[0])
    copies = []
    for j in range(3):
        cols = pl.ds(pl.multiple_of(j * feat + core * HEAD, HEAD), HEAD)
        target = out.at[:, j * HEAD : (j + 1) * HEAD]
        copies.append(pltpu.make_async_copy(w_qkv.at[rows, cols], target, sem.at[j]))
        copies[-1].start(priority=len(copies) % 2)
    for copy in copies:
        copy.wait()
    at = 0
    for piece in pieces:
        piece[...] = out[at : at + piece.shape[0], :]
        at += piece.shape[0]


def cut_out(w_out, mine, theirs, part):
    _, core = position()
    rows = pl.ds(pl.multiple_of(core * HEAD, HEAD), HEAD)
    other = pl.ds(pl.multiple_of((1 - core) * HEAD, HEAD), HEAD)
    mine[...] = w_out[rows, :]
    theirs[...] = w_out[other, :]
    half = part.shape[1]
    part[...] = w_out[rows, pl.ds(pl.multiple_of(parity() * half, half), half)]


def product(tok_a, tok_b, pieces, places):
    cols = [
        pl.ds(pl.multiple_of(place, 128), piece.shape[0]) for piece, place in zip(pieces, places)
    ]
    weights = jnp.concatenate([piece[...] for piece in pieces], axis=0)
    blocks = [jnp.concatenate([ref[:, c] for c in cols], axis=1) for ref in (tok_a, tok_b)]
    return jnp.concatenate([dot(block, weights) for block in blocks], axis=0)


def places_near(shard, offsets):
    at = lax.axis_index("dp")
    return [(at ^ offset) * shard for offset in offsets]


def places_last(shard):
    near_x, near_y = places_near(shard, (1, 2))
    return [near_x + 3 * (shard // 4), near_y]


def places_far(shard):
    start = places_near(shard, (3,))[0]
    mine = quarter_of()
    return [start + (mine ^ mask) * (shard // 4) for mask in (0, 2, 1, 3)]


def project(count, places, tok_a, tok_b, *refs):
    pieces, before, total = refs[:count], refs[count:-1], refs[-1]
    term = product(tok_a, tok_b, pieces, places())
    total[...] = before[0][...] + term if before else term


def project_states(count, places, tok_a, tok_b, *refs):
    pieces, before = refs[:count], refs[count:-4]
    act_out, value_out, state_out, chip_out = refs[-4:]
    proj = product(tok_a, tok_b, pieces, places())
    if before:
        proj = before[0][...] + proj
    rows = value_out.shape[1]
    chip = None
    for b in range(CORES):
        part = proj[b * rows : (b + 1) * rows, :]
        act = part[:, : 2 * HEAD]
        act = (act / (1.0 + jnp.exp(-act))).astype(jnp.bfloat16)
        values = part[:, 2 * HEAD :].astype(jnp.bfloat16)
        state = dot(act[:, HEAD:], values, ((0,), (0,)))
        chip = state if chip is None else chip + state
        act_out[b] = act
        value_out[b] = values
        state_out[b] = state
    chip_out[...] = chip.astype(jnp.bfloat16)


def attend(act, values, *refs):
    if len(refs) > 1:
        own_half, other_half, intra_out, columns_out = refs
        half = own_half.shape[1]
        columns_out[:, pl.ds(pl.multiple_of(parity() * half, half), half)] = own_half[...]
        columns_out[:, pl.ds(pl.multiple_of((1 - parity()) * half, half), half)] = other_half[...]
    else:
        intra_out = refs[0]
    rows = intra_out.shape[1]
    row = lax.broadcasted_iota(jnp.int32, (rows, rows), 0)
    col = lax.broadcasted_iota(jnp.int32, (rows, rows), 1)
    for b in range(CORES):
        scores = dot(act[b, :, :HEAD], act[b, :, HEAD:], ((1,), (1,)))
        scores = jnp.where(row >= col, scores, 0.0).astype(jnp.bfloat16)
        intra_out[b] = dot(scores, values[b])


def normalise(steps, act, state, intra, gain, *refs):
    got, (own_out, other_out) = refs[:steps], refs[steps:]
    _, core = position()
    chip_at = lax.axis_index("seq") // CORES
    base = jnp.zeros((HEAD, HEAD), jnp.float32)
    for step, ref in enumerate(got):
        base = base + jnp.where((chip_at >> step) % 2 == 1, ref[...].astype(jnp.float32), 0.0)
    odd = core == 1
    own_prefix = jnp.where(odd, base + state[1], base)
    other_prefix = jnp.where(odd, base, base + state[0])
    scale = gain[pl.ds(core, 1), :]
    for b, (prefix, out) in enumerate(((own_prefix, own_out), (other_prefix, other_out))):
        attended = dot(act[b, :, :HEAD], prefix.astype(jnp.bfloat16)) + intra[b]
        meansq = jnp.mean(attended * attended, axis=-1, keepdims=True)
        out[...] = (attended * lax.rsqrt(meansq + 1e-06) * scale).astype(jnp.bfloat16)


def mix(count, places, own, other, *refs):
    mine, theirs, (out, stage, sem) = refs[:count], refs[count : 2 * count], refs[2 * count :]
    normed = jnp.concatenate([own[...], other[...]], axis=1)
    copies = []
    slot = 0
    for my_rows, their_rows, place in zip(mine, theirs, places()):
        width = my_rows.shape[1]
        step = min(width, 512)
        for at_col in range(0, width, step):
            part = slice(at_col, at_col + step)
            weights = jnp.concatenate([my_rows[:, part], their_rows[:, part]], axis=0)
            here = stage.at[:, slot : slot + step]
            here[...] = dot(normed, weights).astype(jnp.bfloat16)
            cols = pl.ds(pl.multiple_of(place + at_col, 128), step)
            copies.append(pltpu.make_async_copy(here, out.at[:, cols], sem.at[len(copies)]))
            copies[-1].start(priority=len(copies) % 2)
            slot += step
    for copy in copies:
        copy.wait()


def places_out(width):
    at = lax.axis_index("dp")
    return [(at ^ offset) * width for offset in range(4)]


def shards(n, blocks, tokens, w_qkv, norm_gain, w_out):
    tok_own = tokens[0]
    rows, depth = tok_own.shape
    shard = w_qkv.shape[0]
    heads = norm_gain.shape[0] // HEAD
    bf16, f32 = jnp.bfloat16, jnp.float32

    def call(kernel, outs, ins, out_specs, in_specs, scratch=(), flops=0, moved=0, limit=VMEM_LIMIT):
        return pl.pallas_call(
            kernel,
            out_shape=outs,
            in_specs=in_specs,
            out_specs=out_specs,
            scratch_shapes=scratch,
            compiler_params=pltpu.CompilerParams(vmem_limit_bytes=limit),
            cost_estimate=pl.CostEstimate(flops=flops, bytes_accessed=moved, transcendentals=0),
        )(*ins)

    def array(shape, kind):
        return jax.ShapeDtypeStruct(shape, kind)

    def add_product(pieces, places, total=None):
        extra = [] if total is None else [total]
        return call(
            functools.partial(project, len(pieces), places),
            array((CORES * rows, 3 * HEAD), f32),
            [tok_own, tok_other, *pieces, *extra],
            VMEM, [VMEM] * (2 + len(pieces) + len(extra)),
            flops=rows * HEAD * (1 if total is not None else 1000000),
        )

    tok_other = flip(tok_own, "seq", blocks, 1)
    width = w_out.shape[1]
    grid = n == 4 and blocks % (4 * CORES) == 0 and shard % 512 == 0 and width % 256 == 0

    def cut(first, limit, *sizes):
        return call(
            functools.partial(cut_qkv, first),
            [array((size, 3 * HEAD), bf16) for size in sizes], [w_qkv], [VMEM] * len(sizes), [HBM],
            scratch=[pltpu.SemaphoreType.DMA((3,))], limit=limit,
        )

    out_cut = functools.partial(
        call, cut_out, [array((HEAD, width), bf16)] * 2 + [array((HEAD, width // 2), bf16)],
        [w_out], [VMEM] * 3, [VMEM]
    )
    total = None
    if grid:
        quarter = shard // 4
        part = cut(lambda: quarter_of() * quarter, FIRST_LIMIT, quarter)[0]
        far = [flip(part, "dp", n, 3)]
        own, most, last = cut(lambda: 0, CUT_LIMIT, shard, 3 * quarter, quarter)
        x_most = flip(most, "dp", n, 1)
        send_last, here = lax.optimization_barrier((last, far[0]))
        x_last = flip(send_last, "dp", n, 1)
        from_y = flip(own, "dp", n, 2)
        far.append(flip(far[0], "seq", blocks, CORES * 2))
        here, own = lax.optimization_barrier((far[0], own))
        total = add_product([own], functools.partial(places_near, shard, (0,)))
        send_far, total = lax.optimization_barrier((far[0], total))
        far.append(flip(send_far, "seq", blocks, CORES))
        passed, total = lax.optimization_barrier((far[1], total))
        far.append(flip(passed, "seq", blocks, CORES))
        own_mine, own_theirs, own_part = out_cut()
        send_part, total, far[1] = lax.optimization_barrier((own_part, total, far[1]))
        out_d = flip(send_part, "dp", n, 3)
        out_e = flip(out_d, "seq", blocks, CORES)
        sent, total, far[1] = lax.optimization_barrier((own_mine, total, far[1]))
        out_x = flip(sent, "dp", n, 1)
        out_y = flip(sent, "dp", n, 2)
        total = add_product(
            [x_most, *far[:3]], lambda: places_near(shard, (1,)) + places_far(shard)[:3], total
        )
        total = add_product([x_last, from_y], functools.partial(places_last, shard), total)
        pieces, places = far[3:], lambda: places_far(shard)[3:]
    else:
        whole = cut(lambda: 0, CUT_LIMIT, shard)[0]
        pieces, places = [lax.all_gather(whole, "dp", axis=0, tiled=True)], lambda: [0]
    extra = [] if total is None else [total]

    act, values, state, chip = call(
        functools.partial(project_states, len(pieces), places),
        [
            array((CORES, rows, 2 * HEAD), bf16),
            array((CORES, rows, HEAD), bf16),
            array((CORES, HEAD, HEAD), f32),
            array((HEAD, HEAD), bf16),
        ],
        [tok_own, tok_other, *pieces, *extra],
        [VMEM] * 4, [VMEM] * (2 + len(pieces) + len(extra)),
        flops=2 * CORES * rows * sum(piece.shape[0] for piece in pieces) * 3 * HEAD,
    )
    got, group = [], chip
    for step in range((blocks // CORES).bit_length() - 1):
        if got:
            group = (group.astype(f32) + got[-1].astype(f32)).astype(bf16)
            if grid:
                group, out_d = lax.optimization_barrier((group, out_d))
        got.append(flip(group, "seq", blocks, CORES << step))
    scored, halves, outs = act, [], [array((CORES, rows, HEAD), f32)]
    if grid:
        scored, out_x, out_y = lax.optimization_barrier((act, out_x, out_y))
        halves = [out_d, out_e]
        outs.append(array((HEAD, width), bf16))
    intra, *columns = call(
        attend, outs, [scored, values, *halves], [VMEM] * len(outs), [VMEM] * (2 + len(halves)),
        flops=rows * HEAD * 1000000,
    )
    if grid:
        mine = [own_mine, out_x, out_y, *columns]
        theirs = [own_theirs] + [flip(piece, "seq", blocks, 1) for piece in mine[1:]]
    normed_own, normed_other = call(
        functools.partial(normalise, len(got)),
        [array((rows, HEAD), bf16)] * 2,
        [act, state, intra, norm_gain.reshape(heads, HEAD), *got],
        [VMEM] * 2, [VMEM] * (4 + len(got)), flops=rows * HEAD * 1000000,
    )
    normed_got = flip(normed_other, "seq", blocks, 1)

    if grid:
        places = functools.partial(places_out, width)
    else:
        mine = [lax.all_gather(out_cut()[0], "dp", axis=1, tiled=True)]
        theirs = [flip(mine[0], "seq", blocks, 1)]
        places = lambda: [0]
    mixed = call(
        functools.partial(mix, len(mine), places),
        array((rows, n * width), bf16),
        [normed_own, normed_got, *mine, *theirs],
        HBM, [VMEM] * (2 + 2 * len(mine)),
        scratch=[pltpu.VMEM((rows, n * width), bf16), pltpu.SemaphoreType.DMA((16,))],
        flops=2 * rows * 2 * HEAD * n * width, moved=2 * rows * n * width,
    )
    return mixed[None]


def solution(mesh):
    n, blocks = mesh.shape["dp"], mesh.shape["seq"]
    return jax.shard_map(
        functools.partial(shards, n, blocks),
        mesh=mesh,
        in_specs=(P("dp", "seq", None), P("dp", None), P(), P(None, "dp")),
        out_specs=P("dp", "seq", None),
        check_vma=False,
    )
```

```python
import functools

import jax
import jax.numpy as jnp
from jax import lax
from jax.experimental import pallas as pl
from jax.experimental.pallas import tpu as pltpu
from jax.sharding import PartitionSpec as P

HEAD = 128
CORES = 2
VMEM_LIMIT = 24 * 1024 * 1024
FIRST_LIMIT = 53 * 1024 * 1024
CUT_LIMIT = 52 * 1024 * 1024
VMEM = pl.BlockSpec(memory_space=pltpu.VMEM)
HBM = pl.BlockSpec(memory_space=pltpu.HBM)


def flip(x, axis, size, mask):
    return lax.ppermute(x, axis, [(i, i ^ mask) for i in range(size)])


def dot(a, b, contract=((1,), (0,))):
    return lax.dot_general(a, b, (contract, ((), ())), preferred_element_type=jnp.float32)


def position():
    return lax.axis_index("dp"), lax.rem(lax.axis_index("seq"), CORES)


def parity():
    return lax.rem(lax.axis_index("seq") // CORES, 2)


def quarter_of():
    return lax.rem(lax.axis_index("seq") // CORES, 4)


def cut_qkv(first, w_qkv, out, *refs):
    pieces, sem = refs[:-1], refs[-1]
    _, core = position()
    feat = w_qkv.shape[1] // 3
    step = out.shape[0] // 2
    copies = []
    for i in range(6):
        j, at = i // 2, i % 2 * step
        rows = pl.ds(pl.multiple_of(first() + at, 16), step)
        cols = pl.ds(pl.multiple_of(j * feat + core * HEAD, HEAD), HEAD)
        target = out.at[at : at + step, j * HEAD : (j + 1) * HEAD]
        copies.append(pltpu.make_async_copy(w_qkv.at[rows, cols], target, sem.at[i]))
        copies[-1].start()
    for copy in copies:
        copy.wait()
    at = 0
    for piece in pieces:
        piece[...] = out[at : at + piece.shape[0], :]
        at += piece.shape[0]


def cut_out(w_out, mine, theirs, part):
    _, core = position()
    rows = pl.ds(pl.multiple_of(core * HEAD, HEAD), HEAD)
    other = pl.ds(pl.multiple_of((1 - core) * HEAD, HEAD), HEAD)
    mine[...] = w_out[rows, :]
    theirs[...] = w_out[other, :]
    half = part.shape[1]
    part[...] = w_out[rows, pl.ds(pl.multiple_of(parity() * half, half), half)]


def product(tok_a, tok_b, pieces, places):
    cols = [
        pl.ds(pl.multiple_of(place, 128), piece.shape[0]) for piece, place in zip(pieces, places)
    ]
    weights = jnp.concatenate([piece[...] for piece in pieces], axis=0)
    blocks = [jnp.concatenate([ref[:, c] for c in cols], axis=1) for ref in (tok_a, tok_b)]
    return jnp.concatenate([dot(block, weights) for block in blocks], axis=0)


def places_near(shard, offsets):
    at = lax.axis_index("dp")
    return [(at ^ offset) * shard for offset in offsets]


def places_last(shard):
    near_x, near_y = places_near(shard, (1, 2))
    return [near_x + 3 * (shard // 4), near_y]


def places_far(shard):
    start = places_near(shard, (3,))[0]
    mine = quarter_of()
    return [start + (mine ^ mask) * (shard // 4) for mask in (0, 2, 1, 3)]


def project(count, places, tok_a, tok_b, *refs):
    pieces, before, total = refs[:count], refs[count:-1], refs[-1]
    term = product(tok_a, tok_b, pieces, places())
    total[...] = before[0][...] + term if before else term


def project_states(count, places, tok_a, tok_b, *refs):
    pieces, before = refs[:count], refs[count:-4]
    act_out, value_out, state_out, chip_out = refs[-4:]
    proj = product(tok_a, tok_b, pieces, places())
    if before:
        proj = before[0][...] + proj
    rows = value_out.shape[1]
    chip = None
    for b in range(CORES):
        part = proj[b * rows : (b + 1) * rows, :]
        act = part[:, : 2 * HEAD]
        act = (act / (1.0 + jnp.exp(-act))).astype(jnp.bfloat16)
        values = part[:, 2 * HEAD :].astype(jnp.bfloat16)
        state = dot(act[:, HEAD:], values, ((0,), (0,)))
        chip = state if chip is None else chip + state
        act_out[b] = act
        value_out[b] = values
        state_out[b] = state
    chip_out[...] = chip.astype(jnp.bfloat16)


def attend(act, values, *refs):
    if len(refs) > 1:
        own_half, other_half, intra_out, columns_out = refs
        half = own_half.shape[1]
        columns_out[:, pl.ds(pl.multiple_of(parity() * half, half), half)] = own_half[...]
        columns_out[:, pl.ds(pl.multiple_of((1 - parity()) * half, half), half)] = other_half[...]
    else:
        intra_out = refs[0]
    rows = intra_out.shape[1]
    row = lax.broadcasted_iota(jnp.int32, (rows, rows), 0)
    col = lax.broadcasted_iota(jnp.int32, (rows, rows), 1)
    for b in range(CORES):
        scores = dot(act[b, :, :HEAD], act[b, :, HEAD:], ((1,), (1,)))
        scores = jnp.where(row >= col, scores, 0.0).astype(jnp.bfloat16)
        intra_out[b] = dot(scores, values[b])


def normalise(steps, act, state, intra, gain, *refs):
    got, (own_out, other_out) = refs[:steps], refs[steps:]
    _, core = position()
    chip_at = lax.axis_index("seq") // CORES
    base = jnp.zeros((HEAD, HEAD), jnp.float32)
    for step, ref in enumerate(got):
        base = base + jnp.where((chip_at >> step) % 2 == 1, ref[...].astype(jnp.float32), 0.0)
    odd = core == 1
    own_prefix = jnp.where(odd, base + state[1], base)
    other_prefix = jnp.where(odd, base, base + state[0])
    scale = gain[pl.ds(core, 1), :]
    for b, (prefix, out) in enumerate(((own_prefix, own_out), (other_prefix, other_out))):
        attended = dot(act[b, :, :HEAD], prefix.astype(jnp.bfloat16)) + intra[b]
        meansq = jnp.mean(attended * attended, axis=-1, keepdims=True)
        out[...] = (attended * lax.rsqrt(meansq + 1e-06) * scale).astype(jnp.bfloat16)


def mix(count, places, own, other, *refs):
    mine, theirs, (out, stage, sem) = refs[:count], refs[count : 2 * count], refs[2 * count :]
    normed = jnp.concatenate([own[...], other[...]], axis=1)
    copies = []
    slot = 0
    for my_rows, their_rows, place in zip(mine, theirs, places()):
        width = my_rows.shape[1]
        step = min(width, 512)
        for at_col in range(0, width, step):
            part = slice(at_col, at_col + step)
            weights = jnp.concatenate([my_rows[:, part], their_rows[:, part]], axis=0)
            here = stage.at[:, slot : slot + step]
            here[...] = dot(normed, weights).astype(jnp.bfloat16)
            cols = pl.ds(pl.multiple_of(place + at_col, 128), step)
            copies.append(pltpu.make_async_copy(here, out.at[:, cols], sem.at[len(copies)]))
            copies[-1].start()
            slot += step
    for copy in copies:
        copy.wait()


def places_out(width):
    at = lax.axis_index("dp")
    return [(at ^ offset) * width for offset in range(4)]


def shards(n, blocks, tokens, w_qkv, norm_gain, w_out):
    tok_own = tokens[0]
    rows, depth = tok_own.shape
    shard = w_qkv.shape[0]
    heads = norm_gain.shape[0] // HEAD
    bf16, f32 = jnp.bfloat16, jnp.float32

    def call(kernel, outs, ins, out_specs, in_specs, scratch=(), flops=0, moved=0, limit=VMEM_LIMIT):
        return pl.pallas_call(
            kernel,
            out_shape=outs,
            in_specs=in_specs,
            out_specs=out_specs,
            scratch_shapes=scratch,
            compiler_params=pltpu.CompilerParams(vmem_limit_bytes=limit),
            cost_estimate=pl.CostEstimate(flops=flops, bytes_accessed=moved, transcendentals=0),
        )(*ins)

    def array(shape, kind):
        return jax.ShapeDtypeStruct(shape, kind)

    def add_product(pieces, places, total=None):
        extra = [] if total is None else [total]
        return call(
            functools.partial(project, len(pieces), places),
            array((CORES * rows, 3 * HEAD), f32),
            [tok_own, tok_other, *pieces, *extra],
            VMEM, [VMEM] * (2 + len(pieces) + len(extra)),
            flops=rows * HEAD * (1 if total is not None else 1000000),
        )

    tok_other = flip(tok_own, "seq", blocks, 1)
    width = w_out.shape[1]
    grid = n == 4 and blocks % (4 * CORES) == 0 and shard % 512 == 0 and width % 256 == 0

    def cut(first, limit, *sizes):
        return call(
            functools.partial(cut_qkv, first),
            [array((size, 3 * HEAD), bf16) for size in sizes], [w_qkv], [VMEM] * len(sizes), [HBM],
            scratch=[pltpu.SemaphoreType.DMA((6,))], limit=limit,
        )

    out_cut = functools.partial(
        call, cut_out, [array((HEAD, width), bf16)] * 2 + [array((HEAD, width // 2), bf16)],
        [w_out], [VMEM] * 3, [VMEM]
    )
    total = None
    if grid:
        quarter = shard // 4
        part = cut(lambda: quarter_of() * quarter, FIRST_LIMIT, quarter)[0]
        far = [flip(part, "dp", n, 3)]
        own, most, last = cut(lambda: 0, CUT_LIMIT, shard, 3 * quarter, quarter)
        x_most = flip(most, "dp", n, 1)
        send_last, here = lax.optimization_barrier((last, far[0]))
        x_last = flip(send_last, "dp", n, 1)
        from_y = flip(own, "dp", n, 2)
        far.append(flip(far[0], "seq", blocks, CORES * 2))
        here, own = lax.optimization_barrier((far[0], own))
        total = add_product([own], functools.partial(places_near, shard, (0,)))
        send_far, total = lax.optimization_barrier((far[0], total))
        far.append(flip(send_far, "seq", blocks, CORES))
        passed, total = lax.optimization_barrier((far[1], total))
        far.append(flip(passed, "seq", blocks, CORES))
        own_mine, own_theirs, own_part = out_cut()
        send_part, total, far[1] = lax.optimization_barrier((own_part, total, far[1]))
        out_d = flip(send_part, "dp", n, 3)
        out_e = flip(out_d, "seq", blocks, CORES)
        sent, total, far[1] = lax.optimization_barrier((own_mine, total, far[1]))
        out_x = flip(sent, "dp", n, 1)
        out_y = flip(sent, "dp", n, 2)
        total = add_product(
            [x_most, *far[:3]], lambda: places_near(shard, (1,)) + places_far(shard)[:3], total
        )
        total = add_product([x_last, from_y], functools.partial(places_last, shard), total)
        pieces, places = far[3:], lambda: places_far(shard)[3:]
    else:
        whole = cut(lambda: 0, CUT_LIMIT, shard)[0]
        pieces, places = [lax.all_gather(whole, "dp", axis=0, tiled=True)], lambda: [0]
    extra = [] if total is None else [total]

    act, values, state, chip = call(
        functools.partial(project_states, len(pieces), places),
        [
            array((CORES, rows, 2 * HEAD), bf16),
            array((CORES, rows, HEAD), bf16),
            array((CORES, HEAD, HEAD), f32),
            array((HEAD, HEAD), bf16),
        ],
        [tok_own, tok_other, *pieces, *extra],
        [VMEM] * 4, [VMEM] * (2 + len(pieces) + len(extra)),
        flops=2 * CORES * rows * sum(piece.shape[0] for piece in pieces) * 3 * HEAD,
    )
    got, group = [], chip
    for step in range((blocks // CORES).bit_length() - 1):
        if got:
            group = (group.astype(f32) + got[-1].astype(f32)).astype(bf16)
            if grid:
                group, out_d = lax.optimization_barrier((group, out_d))
        got.append(flip(group, "seq", blocks, CORES << step))
    scored, halves, outs = act, [], [array((CORES, rows, HEAD), f32)]
    if grid:
        scored, out_x, out_y = lax.optimization_barrier((act, out_x, out_y))
        halves = [out_d, out_e]
        outs.append(array((HEAD, width), bf16))
    intra, *columns = call(
        attend, outs, [scored, values, *halves], [VMEM] * len(outs), [VMEM] * (2 + len(halves)),
        flops=rows * HEAD * 1000000,
    )
    if grid:
        mine = [own_mine, out_x, out_y, *columns]
        theirs = [own_theirs] + [flip(piece, "seq", blocks, 1) for piece in mine[1:]]
    normed_own, normed_other = call(
        functools.partial(normalise, len(got)),
        [array((rows, HEAD), bf16)] * 2,
        [act, state, intra, norm_gain.reshape(heads, HEAD), *got],
        [VMEM] * 2, [VMEM] * (4 + len(got)), flops=rows * HEAD * 1000000,
    )
    normed_got = flip(normed_other, "seq", blocks, 1)

    if grid:
        places = functools.partial(places_out, width)
    else:
        mine = [lax.all_gather(out_cut()[0], "dp", axis=1, tiled=True)]
        theirs = [flip(mine[0], "seq", blocks, 1)]
        places = lambda: [0]
    mixed = call(
        functools.partial(mix, len(mine), places),
        array((rows, n * width), bf16),
        [normed_own, normed_got, *mine, *theirs],
        HBM, [VMEM] * (2 + 2 * len(mine)),
        scratch=[pltpu.VMEM((rows, n * width), bf16), pltpu.SemaphoreType.DMA((16,))],
        flops=2 * rows * 2 * HEAD * n * width, moved=2 * rows * n * width,
    )
    return mixed[None]


def solution(mesh):
    n, blocks = mesh.shape["dp"], mesh.shape["seq"]
    return jax.shard_map(
        functools.partial(shards, n, blocks),
        mesh=mesh,
        in_specs=(P("dp", "seq", None), P("dp", None), P(), P(None, "dp")),
        out_specs=P("dp", "seq", None),
        check_vma=False,
    )
```
